128 devices in a mesh: group: 4 (over z), dev: 32 (over y, x, core).
Axes of the slice: x: 4, y: 4, z: 4, core: 2. Of those that a mesh axis runs over, the one named last changes fastest.
Arguments:
- coarse_dens: float32 [6144, 1024], P('dev'), may hold values from 0.1 to 3
- coarse_diff: bfloat16 [6144, 1024], P('dev'), may hold values from 0.19921875 to 1
- coarse_pot: bfloat16 [6144, 1024], P('dev'), may hold values from -1 to 1
- fine_dens: float32 [28672, 1024], P(('group', 'dev')), may hold values from 0.1 to 3
- fine_diff: bfloat16 [28672, 1024], P(('group', 'dev')), may hold values from 0.19921875 to 1
- fine_pot: bfloat16 [28672, 1024], P(('group', 'dev')), may hold values from -1 to 1
- parents: int32 [896], replicated, may hold values from 0 to 1535, as said below
Outputs:
- coarse_out: float32 [6144, 1024], P('dev')
- fine_out: float32 [28672, 1024], P(('group', 'dev'))
The draws below stay inside these ranges and needn't reach their ends.
Inputs may be any that keep to these rules, and one draw needn't show every extreme that they name: `parents`: all ids are distinct. The fine box at index (g * 32 + d) * 7 + k refines an octant of a coarse box held by dev index d - 1, d or d + 1 (cyclically; coarse box c is held by dev index c // 6), and for every d each of the three occurs.
All inputs are finite; a program needn't handle non-finite values.
Results may differ from the reference program's by a relative error of at most 0.0003.
Values sent between devices are 32-bit elements; how exact they have to be, the bound alone decides.
No kernel may reach another device: no remote copies, remote signals or barrier semaphores. Data moves between devices by JAX's collectives and lax.ppermute only.
A program may use at most 512 MiB of HBM per device.

```python
import math
import jax
import jax.numpy as jnp
from jax import lax

S = 32
CB = 6
FB = 7
CBOXES = 192
FBOXES = 896
N_GROUP = 4
N_DEV = 32


def draw_parents(key, part):
    key = jax.random.fold_in(key, 7)
    octant_total = 8 * CB
    per_dev = N_GROUP * FB
    spare = (octant_total - per_dev) // 2
    key_low, key_high, key_order, key_shuffle = jax.random.split(key, 4)
    from_prev = jax.random.randint(key_low, (N_DEV,), 1, spare + 1)
    from_next = jax.random.randint(key_high, (N_DEV,), 1, spare + 1)
    own_count = per_dev - from_prev - from_next
    orders = jax.vmap(lambda subkey: jax.random.permutation(subkey, octant_total))(jax.random.split(key_order, N_DEV))
    device = jnp.arange(N_DEV, dtype=jnp.int32)[:, None]
    slot_index = jnp.arange(per_dev, dtype=jnp.int32)[None, :]
    before = (device - 1) % N_DEV
    after = (device + 1) % N_DEV
    low_pos = from_next[(device - 2) % N_DEV] + own_count[before] + slot_index
    own_pos = from_next[before] + slot_index - from_prev[device]
    high_pos = slot_index - from_prev[device] - own_count[device]
    in_low = slot_index < from_prev[device]
    in_own = slot_index < from_prev[device] + own_count[device]
    source = jnp.where(in_low, before, jnp.where(in_own, device, after))
    position = jnp.clip(jnp.where(in_low, low_pos, jnp.where(in_own, own_pos, high_pos)), 0, octant_total - 1)
    chosen = source * octant_total + orders[source, position]
    shuffles = jax.vmap(lambda subkey: jax.random.permutation(subkey, per_dev))(jax.random.split(key_shuffle, N_DEV))
    chosen = jnp.take_along_axis(chosen, shuffles, axis=1)
    return chosen.reshape(N_DEV, N_GROUP, FB).transpose(1, 0, 2).reshape(-1).astype(jnp.int32)


def steps_of(own_key, dims, pieces, low, largest):
    loudness = 1.0
    for dim, parts in pieces:
        heights = jax.random.uniform(jax.random.fold_in(jax.random.fold_in(own_key, 6), dim), (parts,), jnp.float32, low / len(pieces), largest / len(pieces))
        loudness = loudness * jnp.repeat(jnp.exp(heights), dims[dim] // parts).reshape((-1,) + (1,) * (len(dims) - 1 - dim))
    return loudness


def setup_inputs(seed: int = 0) -> dict:
    seeds = jax.random.split(jax.random.key(seed), 8)
    coarse_dens = jnp.clip(jnp.exp(math.log(3.0) - 3.4011974 * jax.random.uniform(seeds[0], (CBOXES * S, S * S), jnp.float32) ** steps_of(seeds[0], (CBOXES * S, S * S), ((0, 32),), -0.2, 0.2)), 0.1, 3.0)
    coarse_diff = jnp.clip(jnp.exp(math.log(1.0) - 1.6133518 * jax.random.uniform(seeds[1], (CBOXES * S, S * S), jnp.float32) ** steps_of(seeds[1], (CBOXES * S, S * S), ((0, 32),), -0.2, 0.2)), 0.19921875, 1.0).astype(jnp.bfloat16)
    coarse_pot = jnp.clip(jax.random.uniform(seeds[2], (CBOXES * S, S * S), jnp.float32, -1.0, 1.0) * steps_of(seeds[2], (CBOXES * S, S * S), ((0, 32),), -0.4, 0.0), -1.0, 1.0).astype(jnp.bfloat16)
    fine_dens = jnp.clip(jnp.exp(math.log(3.0) - 3.4011974 * jax.random.uniform(seeds[3], (FBOXES * S, S * S), jnp.float32) ** steps_of(seeds[3], (FBOXES * S, S * S), ((0, 128),), -0.2, 0.2)), 0.1, 3.0)
    fine_diff = jnp.clip(jnp.exp(math.log(1.0) - 1.6133518 * jax.random.uniform(seeds[4], (FBOXES * S, S * S), jnp.float32) ** steps_of(seeds[4], (FBOXES * S, S * S), ((0, 128),), -0.2, 0.2)), 0.19921875, 1.0).astype(jnp.bfloat16)
    fine_pot = jnp.clip(jax.random.uniform(seeds[5], (FBOXES * S, S * S), jnp.float32, -1.0, 1.0) * steps_of(seeds[5], (FBOXES * S, S * S), ((0, 128),), -0.4, 0.0), -1.0, 1.0).astype(jnp.bfloat16)
    parents = draw_parents(jax.random.fold_in(seeds[7], 71), 0)
    return {"coarse_dens": coarse_dens, "coarse_diff": coarse_diff, "coarse_pot": coarse_pot, "fine_dens": fine_dens, "fine_diff": fine_diff, "fine_pot": fine_pot, "parents": parents}


step_ratio = 0.06


def shifted(values, ghosts):
    x_low, x_high, y_low, y_high, z_low, z_high = ghosts
    zcoord = lax.broadcasted_iota(jnp.int32, values.shape, 2) % S
    x_minus = jnp.concatenate([x_low[:, None, :], values[:, :-1]], axis=1)
    x_plus = jnp.concatenate([values[:, 1:], x_high[:, None, :]], axis=1)
    y_minus = jnp.concatenate([y_low, values[:, :, :-S]], axis=2)
    y_plus = jnp.concatenate([values[:, :, S:], y_high], axis=2)
    z_minus = jnp.where(zcoord == 0, jnp.repeat(z_low, S, axis=2), jnp.concatenate([values[:, :, :1], values[:, :, :-1]], axis=2))
    z_plus = jnp.where(zcoord == S - 1, jnp.repeat(z_high, S, axis=2), jnp.concatenate([values[:, :, 1:], values[:, :, -1:]], axis=2))
    return (x_minus, x_plus, y_minus, y_plus, z_minus, z_plus)


def edge_ghosts(values):
    return (values[:, 0], values[:, -1], values[:, :, :S], values[:, :, -S:], values[:, :, ::S], values[:, :, S - 1::S])


def advance(density, dens_ghosts, diffusion, near_diff, potential, near_pot, diff_rate, drift_rate):
    near_dens = shifted(density, dens_ghosts)
    change = jnp.zeros_like(density)
    for other_dens, other_diff, other_pot in zip(near_dens, near_diff, near_pot):
        change = change + diff_rate * 0.5 * (diffusion + other_diff) * (density - other_dens) + drift_rate * (potential - other_pot) * 0.5 * (density + other_dens)
    return density - change


def faces_table(extended, box_count):
    half_edge = S // 2
    interior = extended[1:-1].reshape(box_count, 2, half_edge, 2, half_edge, 2, half_edge)

    def rows_to_faces(picked):
        return picked.reshape(box_count, 2, 2, half_edge, 2, half_edge).transpose(0, 1, 2, 4, 3, 5)

    x_low = rows_to_faces(extended[0:2 * box_count * half_edge:half_edge])
    x_high = rows_to_faces(extended[half_edge + 1::half_edge][:2 * box_count])
    y_face_lo = interior[:, :, :, 0, half_edge - 1].transpose(0, 1, 3, 2, 4)
    blanks = jnp.zeros_like(y_face_lo)
    y_low = jnp.stack([blanks, y_face_lo], axis=2)
    y_face_hi = interior[:, :, :, 1, 0].transpose(0, 1, 3, 2, 4)
    y_high = jnp.stack([y_face_hi, blanks], axis=2)
    z_face_lo = interior[:, :, :, :, :, 0, half_edge - 1].transpose(0, 1, 3, 2, 4)
    z_low = jnp.stack([blanks, z_face_lo], axis=3)
    z_face_hi = interior[:, :, :, :, :, 1, 0].transpose(0, 1, 3, 2, 4)
    z_high = jnp.stack([z_face_hi, blanks], axis=3)
    face_stack = jnp.stack([x_low, x_high, y_low, y_high, z_low, z_high], axis=4)
    return face_stack.reshape(box_count * 8, 6, half_edge * half_edge)


def face_ghosts(face_rows):
    half_edge = S // 2
    box_count = face_rows.shape[0]
    enlarged = jnp.repeat(jnp.repeat(face_rows.reshape(box_count, 6, half_edge, half_edge), 2, axis=2), 2, axis=3)
    return (enlarged[:, 0].reshape(box_count, S * S), enlarged[:, 1].reshape(box_count, S * S), enlarged[:, 2], enlarged[:, 3], enlarged[:, 4], enlarged[:, 5])


def fine_steps(density, diffusion, potential, first_rows, second_rows):
    near_diff = shifted(diffusion, edge_ghosts(diffusion))
    near_pot = shifted(potential, edge_ghosts(potential))
    density = advance(density, face_ghosts(first_rows), diffusion, near_diff, potential, near_pot, 2.0 * step_ratio, step_ratio)
    return advance(density, face_ghosts(second_rows), diffusion, near_diff, potential, near_pot, 2.0 * step_ratio, step_ratio)


def coarsen(density):
    half_edge = S // 2
    box_count = density.shape[0]
    summed = density.reshape(box_count, half_edge, 2, half_edge, 2, half_edge, 2).sum(axis=(2, 4, 6))
    return (summed * 0.125).reshape(box_count, half_edge, half_edge * half_edge)


def split_octants(values, box_count):
    half_edge = S // 2
    parted = values.reshape(box_count, 2, half_edge, 2, half_edge, 2, half_edge).transpose(0, 1, 3, 5, 2, 4, 6)
    return parted.reshape(box_count * 8, half_edge, half_edge * half_edge)


def join_octants(octants, box_count):
    half_edge = S // 2
    parted = octants.reshape(box_count, 2, 2, 2, half_edge, half_edge, half_edge).transpose(0, 1, 4, 2, 5, 3, 6)
    return parted.reshape(box_count * S, S * S)


def coarse_step(extended):
    interior = extended[:, 1:-1]
    length_x = interior.shape[1]
    blanks = jnp.zeros((1, length_x, S), jnp.float32)
    dens_ghosts = (extended[0, :1], extended[0, -1:], blanks, blanks, blanks, blanks)
    diff_ghosts = (extended[1, :1], extended[1, -1:]) + edge_ghosts(interior[1:2])[2:]
    pot_ghosts = (extended[2, :1], extended[2, -1:]) + edge_ghosts(interior[2:3])[2:]
    near_diff = shifted(interior[1:2], diff_ghosts)
    near_pot = shifted(interior[2:3], pot_ghosts)
    return advance(interior[0:1], dens_ghosts, interior[1:2], near_diff, interior[2:3], near_pot, step_ratio, step_ratio)[0]


def reference(coarse_dens, coarse_diff, coarse_pot, fine_dens, fine_diff, fine_pot, parents):
    stacked = jnp.stack([coarse_dens, coarse_diff.astype(jnp.float32), coarse_pot.astype(jnp.float32)])
    extended = jnp.concatenate([stacked[:, -1:], stacked, stacked[:, :1]], axis=1)
    coarse_mid = coarse_step(extended)
    new_ext = jnp.concatenate([coarse_mid[-1:], coarse_mid, coarse_mid[:1]], axis=0)
    rims_old = faces_table(extended[0], CBOXES)
    rims_mid = 0.5 * (rims_old + faces_table(new_ext, CBOXES))
    first_rows = rims_old[parents]
    second_rows = rims_mid[parents]

    def one_box(box_items):
        density, diffusion, potential, first_one, second_one = box_items
        result = fine_steps(density[None], diffusion[None].astype(jnp.float32), potential[None].astype(jnp.float32), first_one[None], second_one[None])
        return result[0], coarsen(result)[0]

    fine_result, averages = lax.map(one_box, (fine_dens.reshape(FBOXES, S, S * S), fine_diff.reshape(FBOXES, S, S * S), fine_pot.reshape(FBOXES, S, S * S), first_rows, second_rows))
    octants = split_octants(coarse_mid, CBOXES).at[parents].set(averages)
    return join_octants(octants, CBOXES), fine_result.reshape(FBOXES * S, S * S)
```

```python
import functools

import jax
import jax.numpy as jnp
from jax import lax
from jax.experimental import pallas as pl
from jax.experimental.pallas import tpu as pltpu
from jax.sharding import PartitionSpec as P

S = 32
H = 16
LANES = 128
GROUPS = 8
OCTANTS = 8
PACK = 24
RATE = 0.06
VMEM_LIMIT = 48 * 1024 * 1024


def lane_ids():
    return lax.broadcasted_iota(jnp.int32, (8, LANES), 1)


def row_ids():
    return lax.broadcasted_iota(jnp.int32, (8, LANES), 0)


def gather_lanes(tile, index):
    return jnp.take_along_axis(tile, index, axis=1, mode="promise_in_bounds")


def lane_groups(ref, row):
    return [ref[row : row + 8, LANES * j : LANES * (j + 1)] for j in range(GROUPS)]


def sum_yz(tiles, lanes, edge):
    z = lanes & (S - 1)
    up = [pltpu.roll(t, S, 1) for t in tiles]
    down = [pltpu.roll(t, LANES - S, 1) for t in tiles]
    out = []
    for j, tile in enumerate(tiles):
        fill = tile if edge else jnp.zeros_like(tile)
        low = jnp.where(lanes >= S, up[j], up[j - 1] if j > 0 else fill)
        high = jnp.where(lanes < LANES - S, down[j], down[j + 1] if j + 1 < GROUPS else fill)
        left = jnp.where(z != 0, pltpu.roll(tile, 1, 1), fill)
        right = jnp.where(z != S - 1, pltpu.roll(tile, LANES - 1, 1), fill)
        out.append((low + high) + (left + right))
    return out


def octant_place(local_id):
    box = local_id >> 3
    return box * S + ((local_id >> 2) & 1) * H, (local_id >> 1) & 1, local_id & 1


def edges_kernel(u0, k0, v0, u1, k1, v1, first_ref, last_ref):
    first_ref[0:2, :] = u0[0:2, :]
    first_ref[2:4, :] = k0[...].astype(jnp.float32)[0:2, :]
    first_ref[4:6, :] = v0[...].astype(jnp.float32)[0:2, :]
    first_ref[6:8, :] = u0[0:2, :]
    last_ref[0:2, :] = u1[6:8, :]
    last_ref[2:4, :] = k1[...].astype(jnp.float32)[14:16, :]
    last_ref[4:6, :] = v1[...].astype(jnp.float32)[14:16, :]
    last_ref[6:8, :] = u1[6:8, :]


def pack_rims(old, mid, xs, pack_ref, slot, local_id, base):
    lanes, rows = lane_ids(), row_ids()
    start, oy, oz = octant_place(local_id)
    start = start + base
    half = pl.multiple_of(oy * (S * H), LANES)
    for n, (ref, shift, row) in enumerate(((old, -8, 7), (old, H, 0), (mid, -8, 7), (mid, H, 0))):
        tile = ref[pl.ds(pl.multiple_of(start + shift, 8), 8), pl.ds(half, S * H)]
        line = tile[row : row + 1, :]
        xs[n : n + 1, :] = line
        xs[n + 4 : n + 5, :] = line
    index_x = ((lanes >> 4) & 3) * S + oz * H + (lanes & (H - 1))
    picked = [gather_lanes(xs[:, LANES * s : LANES * (s + 1)], index_x) for s in range(4)]
    low = jnp.where(lanes < 64, picked[0], picked[1])
    high = jnp.where(lanes < 64, picked[2], picked[3])
    faces = jnp.where(rows < 4, low, high)
    mean = 0.5 * (faces + pltpu.roll(faces, 2, 0))
    pack_ref[slot, 0:8, :] = jnp.where((rows & 2) == 0, faces, mean)
    index_y = oy * (LANES - S) + oz * H + (lanes & (H - 1))
    index_z = (lanes & 3) * S + H - oz
    y_group = pl.multiple_of(S * H - LANES * oy, LANES)
    for t in range(2):
        at = pl.multiple_of(start + 8 * t, 8)
        values = []
        for ref in (old, mid):
            y_face = gather_lanes(ref[pl.ds(at, 8), pl.ds(y_group, LANES)], index_y)
            parts = [
                gather_lanes(ref[pl.ds(at, 8), pl.ds(pl.multiple_of(half + LANES * s, LANES), LANES)], index_z)
                for s in range(4)
            ]
            which = (lanes >> 2) & 3
            z_face = jnp.where(
                which < 2,
                jnp.where(which == 0, parts[0], parts[1]),
                jnp.where(which == 2, parts[2], parts[3]),
            )
            values.append(jnp.where(lanes < S, y_face, z_face))
        pack_ref[slot, 8 + 8 * t : 16 + 8 * t, :] = jnp.where(
            (lanes & H) == 0, values[0], 0.5 * (values[0] + values[1])
        )


def coarse_kernel(parents, u_ref, k_ref, v_ref, before, after, mid_out, to_prev, to_own, to_next, u, p, q, m, xs, *, boxes):
    rows = u_ref.shape[0]
    base = 16
    rate = 0.5 * RATE
    dev, devices = lax.axis_index("dev"), lax.axis_size("dev")
    group = lax.axis_index("group")
    octants = OCTANTS * (rows // S)

    for place, ref in ((base - 2, before), (base + rows, after)):
        u[place : place + 2, :] = ref[0:2, :]
        diff, pot = rate * ref[2:4, :], rate * ref[4:6, :]
        p[place : place + 2, :] = diff + pot
        q[place : place + 2, :] = diff - pot

    @pl.loop(0, rows // 16)
    def _(i):
        at = pl.multiple_of(i * 16, 16)
        to = pl.multiple_of(base + i * 16, 16)
        diff = rate * k_ref[pl.ds(at, 16), :].astype(jnp.float32)
        pot = rate * v_ref[pl.ds(at, 16), :].astype(jnp.float32)
        u[pl.ds(to, 16), :] = u_ref[pl.ds(at, 16), :]
        p[pl.ds(to, 16), :] = diff + pot
        q[pl.ds(to, 16), :] = diff - pot

    lanes = lane_ids()

    @pl.loop(0, rows // 8 + 2)
    def _(i):
        at = pl.multiple_of(base - 8 + i * 8, 8)
        views = [ref.at[pl.ds(pl.multiple_of(base - 16 + i * 8, 8), 24), :] for ref in (u, p, q)]
        uc, pc, qc = (lane_groups(view, 8) for view in views)
        ul, pll, ql = (lane_groups(view, 7) for view in views)
        uh, ph, qh = (lane_groups(view, 9) for view in views)
        sum_u = sum_yz(uc, lanes, False)
        sum_w = sum_yz([a * b for a, b in zip(pc, uc)], lanes, False)
        sum_q = sum_yz(qc, lanes, True)
        for j in range(GROUPS):
            keep = (1.0 - 6.0 * pc[j]) - (sum_q[j] + (ql[j] + qh[j]))
            near_u = sum_u[j] + (ul[j] + uh[j])
            near_w = sum_w[j] + (pll[j] * ul[j] + ph[j] * uh[j])
            m[pl.ds(at, 8), LANES * j : LANES * (j + 1)] = keep * uc[j] + (qc[j] * near_u + near_w)

    @pl.loop(0, rows // 8)
    def _(i):
        at = pl.multiple_of(i * 8, 8)
        mid_out[pl.ds(at, 8), :] = m[pl.ds(pl.multiple_of(base + i * 8, 8), 8), :]

    for ref, step in ((to_prev, devices - 1), (to_own, 0), (to_next, 1)):
        target = lax.rem(dev + step, devices)
        for k in range(boxes):
            local_id = parents[(group * devices + target) * boxes + k] - dev * octants
            local_id = jnp.minimum(jnp.maximum(local_id, 0), octants - 1)
            pack_rims(u, m, xs, ref, k, local_id, base)


def fine_kernel(parents, u_ref, k_ref, v_ref, from_prev, from_own, from_next, out_ref, avg_ref, u0, w0, u1, w1, p, q, c, rim, *, boxes, octants):
    dev, devices = lax.axis_index("dev"), lax.axis_size("dev")
    group = lax.axis_index("group")
    k = pl.program_id(0)
    parent = parents[(group * devices + dev) * boxes + k]
    prev_id = parent - lax.rem(dev + devices - 1, devices) * octants
    own_id = parent - dev * octants
    is_own = jnp.logical_and(own_id >= 0, own_id < octants)
    is_prev = jnp.logical_and(prev_id >= 0, prev_id < octants)
    oy, oz = (parent >> 1) & 1, parent & 1
    lanes, rows = lane_ids(), row_ids()
    z = lanes & (S - 1)
    base = 8

    @pl.when(k == 0)
    def _():
        for ref in (u0, w0, u1, w1):
            ref[0:8, :] = jnp.zeros((8, S * S), jnp.float32)
            ref[40:48, :] = jnp.zeros((8, S * S), jnp.float32)

    for i in range(2):
        at, to = 16 * i, base + 16 * i
        diff = RATE * k_ref[at : at + 16, :].astype(jnp.float32)
        pot = (0.5 * RATE) * v_ref[at : at + 16, :].astype(jnp.float32)
        dens = u_ref[at : at + 16, :]
        p[to : to + 16, :] = diff + pot
        q[to : to + 16, :] = diff - pot
        u0[to : to + 16, :] = dens
        w0[to : to + 16, :] = (diff + pot) * dens
    q[7:8, :] = q[8:9, :]
    q[40:41, :] = q[39:40, :]

    def chosen(n):
        first = from_next[k, 8 * n : 8 * n + 8, :]
        second = from_prev[k, 8 * n : 8 * n + 8, :]
        third = from_own[k, 8 * n : 8 * n + 8, :]
        return jnp.where(is_own, third, jnp.where(is_prev, second, first))

    x_faces = chosen(0)
    rim[pl.ds(0, 8, 2), :] = chosen(1)
    rim[pl.ds(1, 8, 2), :] = chosen(1)
    rim[pl.ds(16, 8, 2), :] = chosen(2)
    rim[pl.ds(17, 8, 2), :] = chosen(2)
    x_wide = [gather_lanes(x_faces, (2 * n + (lanes >> 6)) * H + (z >> 1)) for n in range(4)]
    z_here = z == (S - 1) * (1 - oz)
    y_here = {0: lanes < S * oy, GROUPS - 1: lanes >= LANES - S + LANES * oy}

    def ghosts(i, j, step):
        faces = rim[8 * i : 8 * i + 8, :]
        total = jnp.where(z_here, gather_lanes(faces, S + H * step + 2 * j + (lanes >> 6)), 0.0)
        if j in y_here:
            total = total + jnp.where(y_here[j], gather_lanes(faces, H * step + (z >> 1)), 0.0)
        line = 2 * step + 4 * (j // 4)
        if i == 0:
            total = total + jnp.where(rows == 0, x_wide[j % 4][line : line + 1, :], 0.0)
        if i == 3:
            total = total + jnp.where(rows == 7, x_wide[j % 4][line + 1 : line + 2, :], 0.0)
        return total

    for step, (u, w) in enumerate(((u0, w0), (u1, w1))):
        for i in range(4):
            at = base + 8 * i
            uc, wc, pc, qc = (lane_groups(ref, at) for ref in (u, w, p, q))
            ul, wl = (lane_groups(ref, at - 1) for ref in (u, w))
            uh, wh = (lane_groups(ref, at + 1) for ref in (u, w))
            sum_u = sum_yz(uc, lanes, False)
            sum_w = sum_yz(wc, lanes, False)
            if step == 0:
                ql, qh = lane_groups(q, at - 1), lane_groups(q, at + 1)
                sum_q = sum_yz(qc, lanes, True)
            for j in range(GROUPS):
                there = slice(LANES * j, LANES * (j + 1))
                if step == 0:
                    keep = (1.0 - 6.0 * pc[j]) - (sum_q[j] + (ql[j] + qh[j]))
                    c[8 * i : 8 * i + 8, there] = keep
                else:
                    keep = c[8 * i : 8 * i + 8, there]
                near_u = sum_u[j] + (ul[j] + uh[j])
                near_w = sum_w[j] + (wl[j] + wh[j])
                new = (keep * uc[j] + (qc[j] * near_u + near_w)) + (pc[j] + qc[j]) * ghosts(i, j, step)
                if step == 0:
                    u1[at : at + 8, there] = new
                    w1[at : at + 8, there] = pc[j] * new
                else:
                    out_ref[8 * i : 8 * i + 8, there] = new
                    u0[at : at + 8, there] = new

    index = ((lanes >> 4) & 1) * 64 + (lanes & (H - 1)) * 2
    for t in range(2):
        for half in range(2):
            made = None
            for s in range(4):
                j = 4 * half + s
                there = slice(LANES * j, LANES * (j + 1))
                first = u0[base + 16 * t : base + 16 * t + 8, there]
                second = u0[base + 16 * t + 8 : base + 16 * t + 16, there]
                first = first + pltpu.roll(first, 7, 0)
                second = second + pltpu.roll(second, 7, 0)
                rim[0:8, :] = first
                rim[8:16, :] = second
                pairs = rim[pl.ds(0, 8, 2), :]
                pairs = pairs + pltpu.roll(pairs, LANES - S, 1)
                pairs = pairs + pltpu.roll(pairs, LANES - 1, 1)
                moved = gather_lanes(pairs, index)
                made = moved if made is None else jnp.where((lanes >> 5) == s, moved, made)
            avg_ref[k, 8 * t : 8 * t + 8, LANES * half : LANES * (half + 1)] = 0.125 * made


def merge_kernel(parents, mid_ref, from_prev, from_own, from_next, out_ref, *, boxes, octants):
    dev, devices = lax.axis_index("dev"), lax.axis_size("dev")
    groups = lax.axis_size("group")
    lanes = lane_ids()

    @pl.loop(0, out_ref.shape[0] // 8)
    def _(i):
        at = pl.multiple_of(i * 8, 8)
        out_ref[pl.ds(at, 8), :] = mid_ref[pl.ds(at, 8), :]

    for ref, step in ((from_prev, devices - 1), (from_own, 0), (from_next, 1)):
        source = lax.rem(dev + step, devices)

        @pl.loop(0, groups * boxes)
        def _(n):
            from_group = n // boxes
            local_id = parents[(from_group * devices + source) * boxes + (n - from_group * boxes)] - dev * octants

            @pl.when(jnp.logical_and(local_id >= 0, local_id < octants))
            def _():
                start, oy, oz = octant_place(local_id)
                here = ((lanes >> 4) & 1) == oz
                for t in range(2):
                    at = pl.multiple_of(start + 8 * t, 8)
                    for s in range(4):
                        there = pl.ds(pl.multiple_of(oy * (S * H) + LANES * s, LANES), LANES)
                        half = s // 2
                        tile = ref[n, 8 * t : 8 * t + 8, LANES * half : LANES * (half + 1)]
                        moved = gather_lanes(tile, (s % 2) * 64 + (lanes >> 5) * H + (lanes & (H - 1)))
                        out_ref[pl.ds(at, 8), there] = jnp.where(here, moved, out_ref[pl.ds(at, 8), there])


def params():
    return pltpu.CompilerParams(vmem_limit_bytes=VMEM_LIMIT)


def f32(*shape):
    return jax.ShapeDtypeStruct(shape, jnp.float32)


def vmem(*shape):
    return pltpu.VMEM(shape, jnp.float32)


def whole():
    return pl.BlockSpec(memory_space=pltpu.VMEM)


def on_device(coarse_dens, coarse_diff, coarse_pot, fine_dens, fine_diff, fine_pot, parents):
    devices = lax.axis_size("dev")
    groups = lax.axis_size("group")
    up = [(i, (i + 1) % devices) for i in range(devices)]
    down = [(j, i) for i, j in up]
    rows = coarse_dens.shape[0]
    boxes = fine_dens.shape[0] // S
    octants = OCTANTS * (rows // S)
    wide = S * S

    first, last = pl.pallas_call(
        edges_kernel,
        grid=(1,),
        in_specs=[
            pl.BlockSpec((8, wide), lambda i: (0, 0)),
            pl.BlockSpec((16, wide), lambda i: (0, 0)),
            pl.BlockSpec((16, wide), lambda i: (0, 0)),
            pl.BlockSpec((8, wide), lambda i: (rows // 8 - 1, 0)),
            pl.BlockSpec((16, wide), lambda i: (rows // 16 - 1, 0)),
            pl.BlockSpec((16, wide), lambda i: (rows // 16 - 1, 0)),
        ],
        out_specs=[pl.BlockSpec((8, wide), lambda i: (0, 0))] * 2,
        out_shape=[f32(8, wide)] * 2,
        name="edges",
    )(coarse_dens, coarse_diff, coarse_pot, coarse_dens, coarse_diff, coarse_pot)
    before = lax.ppermute(last, "dev", up)
    after = lax.ppermute(first, "dev", down)

    packs = f32(boxes, PACK, LANES)
    mid, to_prev, own, to_next = pl.pallas_call(
        functools.partial(coarse_kernel, boxes=boxes),
        grid_spec=pltpu.PrefetchScalarGridSpec(
            num_scalar_prefetch=1,
            grid=(),
            in_specs=[whole()] * 5,
            out_specs=[whole()] * 4,
            scratch_shapes=[vmem(rows + 32, wide)] * 4 + [vmem(8, S * H)],
        ),
        out_shape=[f32(rows, wide), packs, packs, packs],
        compiler_params=params(),
        name="coarse",
    )(parents, coarse_dens, coarse_diff, coarse_pot, before, after)
    from_prev = lax.ppermute(to_next, "dev", up)
    from_next = lax.ppermute(to_prev, "dev", down)

    box = pl.BlockSpec((S, wide), lambda k, ids: (k, 0))
    pack = pl.BlockSpec((boxes, PACK, LANES), lambda k, ids: (0, 0, 0))
    fine_out, averages = pl.pallas_call(
        functools.partial(fine_kernel, boxes=boxes, octants=octants),
        grid_spec=pltpu.PrefetchScalarGridSpec(
            num_scalar_prefetch=1,
            grid=(boxes,),
            in_specs=[box, box, box, pack, pack, pack],
            out_specs=[box, pl.BlockSpec((boxes, H, H * H), lambda k, ids: (0, 0, 0))],
            scratch_shapes=[vmem(48, wide)] * 6 + [vmem(S, wide), vmem(S, LANES)],
        ),
        out_shape=[f32(boxes * S, wide), f32(boxes, H, H * H)],
        compiler_params=params(),
        name="fine",
    )(parents, fine_dens, fine_diff, fine_pot, from_prev, own, from_next)

    by_group = lax.all_gather(averages, "group", axis=0, tiled=True)
    avg_prev = lax.ppermute(by_group, "dev", up)
    avg_next = lax.ppermute(by_group, "dev", down)
    coarse_out = pl.pallas_call(
        functools.partial(merge_kernel, boxes=boxes, octants=octants),
        grid_spec=pltpu.PrefetchScalarGridSpec(
            num_scalar_prefetch=1,
            grid=(),
            in_specs=[whole()] * 4,
            out_specs=whole(),
        ),
        out_shape=f32(rows, wide),
        compiler_params=params(),
        name="merge",
    )(parents, mid, avg_prev, by_group, avg_next)
    return coarse_out, fine_out


def solution(mesh):
    in_specs = (
        P("dev", None),
        P("dev", None),
        P("dev", None),
        P(("group", "dev"), None),
        P(("group", "dev"), None),
        P(("group", "dev"), None),
        P(),
    )
    out_specs = (P("dev", None), P(("group", "dev"), None))
    return jax.shard_map(on_device, mesh=mesh, in_specs=in_specs, out_specs=out_specs, check_vma=False)
```

```python
import functools

import jax
import jax.numpy as jnp
from jax import lax
from jax.experimental import pallas as pl
from jax.experimental.pallas import tpu as pltpu
from jax.sharding import PartitionSpec as P

S = 32
H = 16
LANES = 128
GROUPS = 8
OCTANTS = 8
PACK = 24
RATE = 0.06
VMEM_LIMIT = 48 * 1024 * 1024


def lane_ids():
    return lax.broadcasted_iota(jnp.int32, (8, LANES), 1)


def row_ids():
    return lax.broadcasted_iota(jnp.int32, (8, LANES), 0)


def gather_lanes(tile, index):
    return jnp.take_along_axis(tile, index, axis=1, mode="promise_in_bounds")


def lane_groups(ref, row):
    return [ref[row : row + 8, LANES * j : LANES * (j + 1)] for j in range(GROUPS)]


def sum_yz(tiles, lanes, edge):
    z = lanes & (S - 1)
    up = [pltpu.roll(t, S, 1) for t in tiles]
    down = [pltpu.roll(t, LANES - S, 1) for t in tiles]
    out = []
    for j, tile in enumerate(tiles):
        fill = tile if edge else jnp.zeros_like(tile)
        low = jnp.where(lanes >= S, up[j], up[j - 1] if j > 0 else fill)
        high = jnp.where(lanes < LANES - S, down[j], down[j + 1] if j + 1 < GROUPS else fill)
        left = jnp.where(z != 0, pltpu.roll(tile, 1, 1), fill)
        right = jnp.where(z != S - 1, pltpu.roll(tile, LANES - 1, 1), fill)
        out.append((low + high) + (left + right))
    return out


def octant_place(local_id):
    box = local_id >> 3
    return box * S + ((local_id >> 2) & 1) * H, (local_id >> 1) & 1, local_id & 1


def edges_kernel(u0, k0, v0, u1, k1, v1, first_ref, last_ref):
    first_ref[0:2, :] = u0[0:2, :]
    first_ref[2:4, :] = k0[...].astype(jnp.float32)[0:2, :]
    first_ref[4:6, :] = v0[...].astype(jnp.float32)[0:2, :]
    first_ref[6:8, :] = u0[0:2, :]
    last_ref[0:2, :] = u1[6:8, :]
    last_ref[2:4, :] = k1[...].astype(jnp.float32)[14:16, :]
    last_ref[4:6, :] = v1[...].astype(jnp.float32)[14:16, :]
    last_ref[6:8, :] = u1[6:8, :]


def pack_rims(old, mid, xs, pack_ref, slot, local_id, base):
    lanes, rows = lane_ids(), row_ids()
    start, oy, oz = octant_place(local_id)
    start = start + base
    half = pl.multiple_of(oy * (S * H), LANES)
    for n, (ref, shift, row) in enumerate(((old, -8, 7), (old, H, 0), (mid, -8, 7), (mid, H, 0))):
        tile = ref[pl.ds(pl.multiple_of(start + shift, 8), 8), pl.ds(half, S * H)]
        line = tile[row : row + 1, :]
        xs[n : n + 1, :] = line
        xs[n + 4 : n + 5, :] = line
    index_x = ((lanes >> 4) & 3) * S + oz * H + (lanes & (H - 1))
    picked = [gather_lanes(xs[:, LANES * s : LANES * (s + 1)], index_x) for s in range(4)]
    low = jnp.where(lanes < 64, picked[0], picked[1])
    high = jnp.where(lanes < 64, picked[2], picked[3])
    faces = jnp.where(rows < 4, low, high)
    mean = 0.5 * (faces + pltpu.roll(faces, 2, 0))
    pack_ref[slot, 0:8, :] = jnp.where((rows & 2) == 0, faces, mean)
    index_y = oy * (LANES - S) + oz * H + (lanes & (H - 1))
    index_z = (lanes & 3) * S + H - oz
    y_group = pl.multiple_of(S * H - LANES * oy, LANES)
    for t in range(2):
        at = pl.multiple_of(start + 8 * t, 8)
        values = []
        for ref in (old, mid):
            y_face = gather_lanes(ref[pl.ds(at, 8), pl.ds(y_group, LANES)], index_y)
            parts = [
                gather_lanes(ref[pl.ds(at, 8), pl.ds(pl.multiple_of(half + LANES * s, LANES), LANES)], index_z)
                for s in range(4)
            ]
            which = (lanes >> 2) & 3
            z_face = jnp.where(
                which < 2,
                jnp.where(which == 0, parts[0], parts[1]),
                jnp.where(which == 2, parts[2], parts[3]),
            )
            values.append(jnp.where(lanes < S, y_face, z_face))
        pack_ref[slot, 8 + 8 * t : 16 + 8 * t, :] = jnp.where(
            (lanes & H) == 0, values[0], 0.5 * (values[0] + values[1])
        )


def lists_kernel_part(parents, hits, boxes, octants, split):
    dev, devices = lax.axis_index("dev"), lax.axis_size("dev")
    group, groups = lax.axis_index("group"), lax.axis_size("group")
    for r in range(3):
        source = lax.rem(dev + devices + r - 1, devices)
        for s in range(groups):
            first = (lax.rem(group + groups - s, groups) * devices + source) * boxes
            for part, (low, high) in enumerate(((0, split), (split, boxes))):
                row = (r * groups + s) * 2 + part
                count = jnp.int32(0)
                for k in range(low, high):
                    local_id = parents[first + k] - dev * octants
                    hits[row, count] = (k - low) * octants + local_id
                    inside = jnp.logical_and(local_id >= 0, local_id < octants)
                    count = count + inside.astype(jnp.int32)
                hits[row, 7] = count


def step_tile(uc, pc, qc, ul, pll, ql, uh, ph, qh, lanes):
    sum_u = sum_yz(uc, lanes, False)
    sum_w = sum_yz([a * b for a, b in zip(pc, uc)], lanes, False)
    sum_q = sum_yz(qc, lanes, True)
    out = []
    for j in range(GROUPS):
        keep = (1.0 - 6.0 * pc[j]) - (sum_q[j] + (ql[j] + qh[j]))
        near_u = sum_u[j] + (ul[j] + uh[j])
        near_w = sum_w[j] + (pll[j] * ul[j] + ph[j] * uh[j])
        out.append(keep * uc[j] + (qc[j] * near_u + near_w))
    return out


def coarse_kernel(parents, u_any, k_ref, v_ref, mid_out, hits, u, p, q, sem, *, boxes, split):
    rows = k_ref.shape[0]
    base = 8
    rate = 0.5 * RATE
    copy = pltpu.make_async_copy(u_any, u.at[pl.ds(base, rows), :], sem)
    copy.start()
    lists_kernel_part(parents, hits, boxes, OCTANTS * (rows // S), split)
    for ref in (u, p, q):
        ref[0:8, :] = jnp.zeros((8, S * S), jnp.float32)
        ref[base + rows : base + rows + 8, :] = jnp.zeros((8, S * S), jnp.float32)

    @pl.loop(0, rows // 16)
    def _(i):
        at = pl.multiple_of(i * 16, 16)
        to = pl.multiple_of(base + i * 16, 8)
        diff = rate * k_ref[pl.ds(at, 16), :].astype(jnp.float32)
        pot = rate * v_ref[pl.ds(at, 16), :].astype(jnp.float32)
        p[pl.ds(to, 16), :] = diff + pot
        q[pl.ds(to, 16), :] = diff - pot

    copy.wait()
    lanes = lane_ids()

    @pl.loop(0, rows // 8)
    def _(i):
        at = pl.multiple_of(i * 8, 8)
        views = [ref.at[pl.ds(at, 24), :] for ref in (u, p, q)]
        tiles = [lane_groups(view, row) for row in (8, 7, 9) for view in views]
        for j, new in enumerate(step_tile(*tiles, lanes)):
            mid_out[pl.ds(at, 8), LANES * j : LANES * (j + 1)] = new


def rims_kernel(parents, u_any, mid_any, k_first, v_first, k_last, v_last, before, after, to_prev, to_own, to_next, fixed, u, m, e, xs, sems, *, boxes):
    rows = u_any.shape[0]
    base = 16
    rate = 0.5 * RATE
    dev, devices = lax.axis_index("dev"), lax.axis_size("dev")
    group = lax.axis_index("group")
    octants = OCTANTS * (rows // S)
    copies = [
        pltpu.make_async_copy(u_any, u.at[pl.ds(base, rows), :], sems.at[0]),
        pltpu.make_async_copy(mid_any, m.at[pl.ds(base, rows), :], sems.at[1]),
    ]
    for copy in copies:
        copy.start()
    lanes = lane_ids()
    for copy in copies:
        copy.wait()
    u[base - 2 : base, :] = before[0:2, :]
    u[base + rows : base + rows + 2, :] = after[0:2, :]
    for n, (far, k_ref, v_ref, own, top) in enumerate(
        ((before, k_first, v_first, 0, base - 2), (after, k_last, v_last, 14, base + rows - 2))
    ):
        e[0, 7:11, :] = u[top : top + 4, :]
        own_diff = rate * k_ref[...].astype(jnp.float32)[own : own + 2, :]
        own_pot = rate * v_ref[...].astype(jnp.float32)[own : own + 2, :]
        far_diff, far_pot = rate * far[2:4, :], rate * far[4:6, :]
        there, here = (7, 9) if n == 0 else (9, 7)
        e[1, there : there + 2, :] = far_diff + far_pot
        e[2, there : there + 2, :] = far_diff - far_pot
        e[1, here : here + 2, :] = own_diff + own_pot
        e[2, here : here + 2, :] = own_diff - own_pot
        tiles = [lane_groups(e.at[f], row) for row in (8, 7, 9) for f in range(3)]
        for j, new in enumerate(step_tile(*tiles, lanes)):
            m[top + 1 : top + 3, LANES * j : LANES * (j + 1)] = new[0:2, :]
    fixed[0:8, :] = m[base : base + 8, :]
    fixed[8:16, :] = m[base + rows - 8 : base + rows, :]

    for ref, step in ((to_prev, devices - 1), (to_next, 1), (to_own, 0)):
        target = lax.rem(dev + step, devices)
        for k in range(boxes):
            local_id = parents[(group * devices + target) * boxes + k] - dev * octants
            local_id = jnp.minimum(jnp.maximum(local_id, 0), octants - 1)
            pack_rims(u, m, xs, ref, k, local_id, base)


def coefficients(k_ref, v_ref, p, q, base):
    for i in range(2):
        at, to = 16 * i, base + 16 * i
        diff = RATE * k_ref[at : at + 16, :].astype(jnp.float32)
        pot = (0.5 * RATE) * v_ref[at : at + 16, :].astype(jnp.float32)
        p[to : to + 16, :] = diff + pot
        q[to : to + 16, :] = diff - pot


def fine_first_kernel(u_ref, k_ref, v_ref, out_ref, c_ref, u0, w0, p, q):
    lanes = lane_ids()
    base = 8

    @pl.when(pl.program_id(0) == 0)
    def _():
        for ref in (u0, w0):
            ref[0:8, :] = jnp.zeros((8, S * S), jnp.float32)
            ref[40:48, :] = jnp.zeros((8, S * S), jnp.float32)

    coefficients(k_ref, v_ref, p, q, base)
    u0[base : base + S, :] = u_ref[...]
    w0[base : base + S, :] = p[base : base + S, :] * u_ref[...]
    q[7:8, :] = q[8:9, :]
    q[40:41, :] = q[39:40, :]
    for i in range(4):
        at = base + 8 * i
        uc, wc, pc, qc = (lane_groups(ref, at) for ref in (u0, w0, p, q))
        ul, wl, ql = (lane_groups(ref, at - 1) for ref in (u0, w0, q))
        uh, wh, qh = (lane_groups(ref, at + 1) for ref in (u0, w0, q))
        sum_u = sum_yz(uc, lanes, False)
        sum_w = sum_yz(wc, lanes, False)
        sum_q = sum_yz(qc, lanes, True)
        for j in range(GROUPS):
            there = slice(LANES * j, LANES * (j + 1))
            keep = (1.0 - 6.0 * pc[j]) - (sum_q[j] + (ql[j] + qh[j]))
            near_u = sum_u[j] + (ul[j] + uh[j])
            near_w = sum_w[j] + (wl[j] + wh[j])
            c_ref[8 * i : 8 * i + 8, there] = keep
            out_ref[8 * i : 8 * i + 8, there] = keep * uc[j] + (qc[j] * near_u + near_w)


def fine_second_kernel(parents, u_ref, c_ref, k_ref, v_ref, from_prev, from_own, from_next, *rest, boxes, octants, skip):
    out_ref, avg_ref, u1, w1, p, q, rim = rest[-7:]
    dev, devices = lax.axis_index("dev"), lax.axis_size("dev")
    group = lax.axis_index("group")
    k = pl.program_id(0)
    parent = parents[(group * devices + dev) * boxes + k + skip]
    prev_id = parent - lax.rem(dev + devices - 1, devices) * octants
    own_id = parent - dev * octants
    is_own = jnp.logical_and(own_id >= 0, own_id < octants)
    is_prev = jnp.logical_and(prev_id >= 0, prev_id < octants)
    oy, oz = (parent >> 1) & 1, parent & 1
    lanes, rows = lane_ids(), row_ids()
    z = lanes & (S - 1)
    base = 8

    @pl.when(k == 0)
    def _():
        for ref in (u1, w1):
            ref[0:8, :] = jnp.zeros((8, S * S), jnp.float32)
            ref[40:48, :] = jnp.zeros((8, S * S), jnp.float32)

    coefficients(k_ref, v_ref, p, q, base)

    def chosen(n):
        first = from_next[k + skip, 8 * n : 8 * n + 8, :]
        second = from_prev[k + skip, 8 * n : 8 * n + 8, :]
        third = from_own[k + skip, 8 * n : 8 * n + 8, :]
        return jnp.where(is_own, third, jnp.where(is_prev, second, first))

    x_faces = chosen(0)
    for n in range(2):
        faces = chosen(n + 1)
        rim[pl.ds(16 * n, 8, 2), :] = faces
        rim[pl.ds(16 * n + 1, 8, 2), :] = faces
    x_wide = [gather_lanes(x_faces, (2 * n + (lanes >> 6)) * H + (z >> 1)) for n in range(4)]
    z_here = z == (S - 1) * (1 - oz)
    y_here = {0: lanes < S * oy, GROUPS - 1: lanes >= LANES - S + LANES * oy}

    def ghosts(i, j, step):
        faces = rim[8 * i : 8 * i + 8, :]
        total = jnp.where(z_here, gather_lanes(faces, S + H * step + 2 * j + (lanes >> 6)), 0.0)
        if j in y_here:
            total = total + jnp.where(y_here[j], gather_lanes(faces, H * step + (z >> 1)), 0.0)
        line = 2 * step + 4 * (j // 4)
        if i == 0:
            total = total + jnp.where(rows == 0, x_wide[j % 4][line : line + 1, :], 0.0)
        if i == 3:
            total = total + jnp.where(rows == 7, x_wide[j % 4][line + 1 : line + 2, :], 0.0)
        return total

    for i in range(4):
        at = base + 8 * i
        for j in range(GROUPS):
            there = slice(LANES * j, LANES * (j + 1))
            pc = p[at : at + 8, there]
            new = u_ref[8 * i : 8 * i + 8, there] + (pc + q[at : at + 8, there]) * ghosts(i, j, 0)
            u1[at : at + 8, there] = new
            w1[at : at + 8, there] = pc * new

    index = ((lanes >> 4) & 1) * 64 + (lanes & (H - 1)) * 2
    for t in range(2):
        made = [None, None]
        news = []
        for i in (2 * t, 2 * t + 1):
            at = base + 8 * i
            uc, wc, pc, qc = (lane_groups(ref, at) for ref in (u1, w1, p, q))
            ul, wl = (lane_groups(ref, at - 1) for ref in (u1, w1))
            uh, wh = (lane_groups(ref, at + 1) for ref in (u1, w1))
            sum_u = sum_yz(uc, lanes, False)
            sum_w = sum_yz(wc, lanes, False)
            row = []
            for j in range(GROUPS):
                there = slice(LANES * j, LANES * (j + 1))
                keep = c_ref[8 * i : 8 * i + 8, there]
                near_u = sum_u[j] + (ul[j] + uh[j])
                near_w = sum_w[j] + (wl[j] + wh[j])
                new = (keep * uc[j] + (qc[j] * near_u + near_w)) + (pc[j] + qc[j]) * ghosts(i, j, 1)
                out_ref[8 * i : 8 * i + 8, there] = new
                row.append(new)
            news.append(row)
        for j in range(GROUPS):
            half, s = divmod(j, 4)
            slot = 32 + 16 * ((t * GROUPS + j) % 4)
            for i in range(2):
                rim[slot + 8 * i : slot + 8 * i + 8, :] = news[i][j]
            pairs = rim[pl.ds(slot, 8, 2), :] + rim[pl.ds(slot + 1, 8, 2), :]
            pairs = pairs + pltpu.roll(pairs, LANES - S, 1)
            pairs = pairs + pltpu.roll(pairs, LANES - 1, 1)
            moved = gather_lanes(pairs, index)
            made[half] = moved if s == 0 else jnp.where((lanes >> 5) == s, moved, made[half])
        for half in range(2):
            avg_ref[k, 8 * t : 8 * t + 8, LANES * half : LANES * (half + 1)] = 0.125 * made[half]


def put_averages(hits, pieces, out_ref, octants):
    lanes = lane_ids()
    for ref, row in pieces:

        @pl.loop(0, hits[row, 7])
        def _(n):
            entry = hits[row, n]
            box = lax.div(entry, jnp.int32(octants))
            start, oy, oz = octant_place(entry - box * octants)
            here = ((lanes >> 4) & 1) == oz
            for t in range(2):
                at = pl.multiple_of(start + 8 * t, 8)
                for s in range(4):
                    there = pl.ds(pl.multiple_of(oy * (S * H) + LANES * s, LANES), LANES)
                    half = s // 2
                    tile = ref[box, 8 * t : 8 * t + 8, LANES * half : LANES * (half + 1)]
                    moved = gather_lanes(tile, (s % 2) * 64 + (lanes >> 5) * H + (lanes & (H - 1)))
                    out_ref[pl.ds(at, 8), there] = jnp.where(here, moved, out_ref[pl.ds(at, 8), there])


def merge_own_kernel(hits, mid_ref, fixed, *rest, lines, octants):
    *pieces, out_ref = rest
    rows = out_ref.shape[0]

    @pl.loop(1, rows // 8 - 1)
    def _(i):
        at = pl.multiple_of(i * 8, 8)
        out_ref[pl.ds(at, 8), :] = mid_ref[pl.ds(at, 8), :]

    out_ref[0:8, :] = fixed[0:8, :]
    out_ref[rows - 8 : rows, :] = fixed[8:16, :]
    put_averages(hits, list(zip(pieces, lines)), out_ref, octants)


def merge_far_kernel(hits, held_ref, *rest, lines, octants):
    *pieces, out_ref = rest

    @pl.loop(0, out_ref.shape[0] // 8)
    def _(i):
        at = pl.multiple_of(i * 8, 8)
        out_ref[pl.ds(at, 8), :] = held_ref[pl.ds(at, 8), :]

    put_averages(hits, list(zip(pieces, lines)), out_ref, octants)


def params():
    return pltpu.CompilerParams(vmem_limit_bytes=VMEM_LIMIT)


def cost(flops, size):
    return pl.CostEstimate(flops=flops, bytes_accessed=size, transcendentals=0)


def f32(*shape):
    return jax.ShapeDtypeStruct(shape, jnp.float32)


def vmem(*shape):
    return pltpu.VMEM(shape, jnp.float32)


def whole():
    return pl.BlockSpec(memory_space=pltpu.VMEM)


def on_device(coarse_dens, coarse_diff, coarse_pot, fine_dens, fine_diff, fine_pot, parents):
    devices = lax.axis_size("dev")
    groups = lax.axis_size("group")
    up = [(i, (i + 1) % devices) for i in range(devices)]
    down = [(j, i) for i, j in up]
    rows = coarse_dens.shape[0]
    boxes = fine_dens.shape[0] // S
    octants = OCTANTS * (rows // S)
    wide = S * S

    first, last = pl.pallas_call(
        edges_kernel,
        grid=(1,),
        in_specs=[
            pl.BlockSpec((8, wide), lambda i: (0, 0)),
            pl.BlockSpec((16, wide), lambda i: (0, 0)),
            pl.BlockSpec((16, wide), lambda i: (0, 0)),
            pl.BlockSpec((8, wide), lambda i: (rows // 8 - 1, 0)),
            pl.BlockSpec((16, wide), lambda i: (rows // 16 - 1, 0)),
            pl.BlockSpec((16, wide), lambda i: (rows // 16 - 1, 0)),
        ],
        out_specs=[pl.BlockSpec((8, wide), lambda i: (0, 0))] * 2,
        out_shape=[f32(8, wide)] * 2,
        name="edges",
    )(coarse_dens, coarse_diff, coarse_pot, coarse_dens, coarse_diff, coarse_pot)
    before = lax.ppermute(last, "dev", up)
    after = lax.ppermute(first, "dev", down)
    split = boxes - boxes // 2
    lists = jax.ShapeDtypeStruct((6 * groups, 8), jnp.int32)
    smem = pl.BlockSpec(memory_space=pltpu.SMEM)
    anywhere = pl.BlockSpec(memory_space=pl.ANY)

    mid, hits = pl.pallas_call(
        functools.partial(coarse_kernel, boxes=boxes, split=split),
        grid_spec=pltpu.PrefetchScalarGridSpec(
            num_scalar_prefetch=1,
            grid=(),
            in_specs=[anywhere, whole(), whole()],
            out_specs=[whole(), smem],
            scratch_shapes=[vmem(rows + 16, wide)] * 3 + [pltpu.SemaphoreType.DMA],
        ),
        out_shape=[f32(rows, wide), lists],
        compiler_params=params(),
        cost_estimate=cost(rows * wide * 40, rows * wide * 12),
        name="coarse",
    )(parents, coarse_dens, coarse_diff, coarse_pot)

    packs = f32(boxes, PACK, LANES)
    top = pl.BlockSpec((16, wide), lambda i, ids: (0, 0))
    bottom = pl.BlockSpec((16, wide), lambda i, ids: (rows // 16 - 1, 0))
    edge = pl.BlockSpec((8, wide), lambda i, ids: (0, 0))
    pack = pl.BlockSpec((boxes, PACK, LANES), lambda i, ids: (0, 0, 0))
    to_prev, own, to_next, fixed = pl.pallas_call(
        functools.partial(rims_kernel, boxes=boxes),
        grid_spec=pltpu.PrefetchScalarGridSpec(
            num_scalar_prefetch=1,
            grid=(1,),
            in_specs=[anywhere, anywhere, top, top, bottom, bottom, edge, edge],
            out_specs=[pack, pack, pack, pl.BlockSpec((16, wide), lambda i, ids: (0, 0))],
            scratch_shapes=[vmem(rows + 32, wide)] * 2
            + [vmem(3, 24, wide), vmem(8, S * H), pltpu.SemaphoreType.DMA((2,))],
        ),
        out_shape=[packs, packs, packs, f32(16, wide)],
        compiler_params=params(),
        cost_estimate=cost(rows * wide * 8, rows * wide * 8),
        name="rims",
    )(parents, coarse_dens, mid, coarse_diff, coarse_pot, coarse_diff, coarse_pot, before, after)
    from_prev = lax.ppermute(to_next, "dev", up)
    from_next = lax.ppermute(to_prev, "dev", down)

    box = pl.BlockSpec((S, wide), lambda k: (k, 0))
    fine_first, keep = pl.pallas_call(
        fine_first_kernel,
        grid=(boxes,),
        in_specs=[box] * 3,
        out_specs=[box] * 2,
        out_shape=[f32(boxes * S, wide)] * 2,
        scratch_shapes=[vmem(48, wide)] * 4,
        compiler_params=params(),
        cost_estimate=cost(boxes * S * wide * 40, boxes * S * wide * 16),
        name="fine_first",
    )(fine_dens, fine_diff, fine_pot)

    fine_out, parts = None, []
    for skip, count in ((0, split), (split, boxes - split)):
        there = pl.BlockSpec((S, wide), lambda k, ids, skip=skip: (k + skip, 0))
        held = [] if fine_out is None else [fine_out]
        fine_out, part = pl.pallas_call(
            functools.partial(fine_second_kernel, boxes=boxes, octants=octants, skip=skip),
            grid_spec=pltpu.PrefetchScalarGridSpec(
                num_scalar_prefetch=1,
                grid=(count,),
                in_specs=[there] * 4 + [pack] * 3 + [anywhere] * len(held),
                out_specs=[there, pl.BlockSpec((count, H, H * H), lambda k, ids: (0, 0, 0))],
                scratch_shapes=[vmem(48, wide)] * 4 + [vmem(96, LANES)],
            ),
            out_shape=[f32(boxes * S, wide), f32(count, H, H * H)],
            input_output_aliases={8: 0} if held else {},
            compiler_params=params(),
            cost_estimate=cost(count * S * wide * 60, count * S * wide * 16),
            name="fine_second",
        )(parents, fine_first, keep, fine_diff, fine_pot, from_prev, own, from_next, *held)
        parts.append(part)

    own_parts, own_lines, far_parts, far_lines = [], [], [], []
    for n, part in enumerate(parts):
        for s in range(groups):
            turn = [(i, (i + s) % groups) for i in range(groups)]
            piece = part if s == 0 else lax.ppermute(part, "group", turn)
            own_parts.append(piece)
            own_lines.append((groups + s) * 2 + n)
            far_parts += [lax.ppermute(piece, "dev", up), lax.ppermute(piece, "dev", down)]
            far_lines += [s * 2 + n, (2 * groups + s) * 2 + n]

    def merge(kernel, first, pieces, lines, name):
        return pl.pallas_call(
            functools.partial(kernel, lines=lines, octants=octants),
            grid_spec=pltpu.PrefetchScalarGridSpec(
                num_scalar_prefetch=1,
                grid=(),
                in_specs=[whole()] * (len(first) + len(pieces)),
                out_specs=whole(),
            ),
            out_shape=f32(rows, wide),
            compiler_params=params(),
            cost_estimate=cost(rows * wide * 4, rows * wide * 12),
            name=name,
        )(hits, *first, *pieces)

    merged = merge(merge_own_kernel, (mid, fixed), own_parts, own_lines, "merge_own")
    coarse_out = merge(merge_far_kernel, (merged,), far_parts, far_lines, "merge_far")
    return coarse_out, fine_out


def solution(mesh):
    in_specs = (
        P("dev", None),
        P("dev", None),
        P("dev", None),
        P(("group", "dev"), None),
        P(("group", "dev"), None),
        P(("group", "dev"), None),
        P(),
    )
    out_specs = (P("dev", None), P(("group", "dev"), None))
    return jax.shard_map(on_device, mesh=mesh, in_specs=in_specs, out_specs=out_specs, check_vma=False)
```

```python
import functools

import jax
import jax.numpy as jnp
import numpy as np
from jax import lax
from jax.experimental import pallas as pl
from jax.experimental.pallas import tpu as pltpu
from jax.sharding import PartitionSpec as P

S = 32
H = 16
LANES = 128
GROUPS = 8
OCTANTS = 8
PACK = 24
RATE = 0.06
VMEM_LIMIT = 48 * 1024 * 1024


def neighbour_matrix():
    source, target = np.arange(512)[:, None] - LANES, np.arange(256)[None, :]
    step = source - target
    same_y = source // S == target // S
    return jnp.asarray((np.abs(step) == S) | ((np.abs(step) == 1) & same_y), jnp.bfloat16)


def ghost_matrices():
    source, target = np.arange(LANES)[:, None], np.arange(S * S)[None, :]
    part, place = (source >> 4) & 3, source & (H - 1)
    y, z = target // S, target % S
    faces = (
        ((part == 0) & (z == S - 1) & (y // 2 == place))
        | ((part == 1) & (z == 0) & (y // 2 == place))
        | ((part == 2) & (y == S - 1) & (z // 2 == place))
        | ((part == 3) & (y == 0) & (z // 2 == place))
    )
    return jnp.asarray(np.stack([faces & (source // 64 == step) for step in range(2)]), jnp.bfloat16)


def average_matrix():
    source, target = np.arange(S * S)[:, None], np.arange(H * H)[None, :]
    return jnp.asarray((source // S // 2 == target // H) & (source % S // 2 == target % H), jnp.bfloat16)


def pieces_of(value):
    high = value.astype(jnp.bfloat16)
    return high, (value - high.astype(jnp.float32)).astype(jnp.bfloat16)


def product(left, right):
    return jnp.dot(left, right, preferred_element_type=jnp.float32)


def sides():
    dev, devices = lax.axis_index("dev"), lax.axis_size("dev")
    odd = dev & 1
    near = dev + 1 - 2 * odd
    far = lax.rem(dev + devices - 1 + 2 * odd, devices)
    return dev, near, far, odd


def edge_count():
    lane = lax.broadcasted_iota(jnp.int32, (1, S * S), 1)
    z, y = lane & (S - 1), lane >> 5
    return sum((at == end).astype(jnp.float32) for at in (z, y) for end in (0, S - 1))


def lane_ids():
    return lax.broadcasted_iota(jnp.int32, (8, LANES), 1)


def row_ids():
    return lax.broadcasted_iota(jnp.int32, (8, LANES), 0)


def gather_lanes(tile, index):
    return jnp.take_along_axis(tile, index, axis=1, mode="promise_in_bounds")


def lane_groups(ref, row):
    return [ref[row : row + 8, LANES * j : LANES * (j + 1)] for j in range(GROUPS)]


def sum_yz(tiles, lanes, edge):
    z = lanes & (S - 1)
    up = [pltpu.roll(t, S, 1) for t in tiles]
    down = [pltpu.roll(t, LANES - S, 1) for t in tiles]
    out = []
    for j, tile in enumerate(tiles):
        fill = tile if edge else jnp.zeros_like(tile)
        low = jnp.where(lanes >= S, up[j], up[j - 1] if j > 0 else fill)
        high = jnp.where(lanes < LANES - S, down[j], down[j + 1] if j + 1 < GROUPS else fill)
        left = jnp.where(z != 0, pltpu.roll(tile, 1, 1), fill)
        right = jnp.where(z != S - 1, pltpu.roll(tile, LANES - 1, 1), fill)
        out.append((low + high) + (left + right))
    return out


def octant_place(local_id):
    box = local_id >> 3
    return box * S + ((local_id >> 2) & 1) * H, (local_id >> 1) & 1, local_id & 1


def edges_kernel(u0, k0, v0, u1, k1, v1, near_ref, far_ref):
    _, _, _, odd = sides()
    first = (u0[0:2, :], k0[...].astype(jnp.float32)[0:2, :], v0[...].astype(jnp.float32)[0:2, :])
    last = (u1[6:8, :], k1[...].astype(jnp.float32)[14:16, :], v1[...].astype(jnp.float32)[14:16, :])
    is_odd = odd == 1
    for n, (low, high) in enumerate(zip(first, last)):
        near_ref[2 * n : 2 * n + 2, :] = jnp.where(is_odd, low, high)
        far_ref[2 * n : 2 * n + 2, :] = jnp.where(is_odd, high, low)
    for ref in (near_ref, far_ref):
        ref[6:8, :] = jnp.zeros((2, S * S), jnp.float32)


def pack_rims(old, mid, xs, pack_ref, slot, local_id, base):
    lanes, rows = lane_ids(), row_ids()
    start, oy, oz = octant_place(local_id)
    start = start + base
    half = pl.multiple_of(oy * (S * H), LANES)
    for n, (ref, shift, row) in enumerate(((old, -8, 7), (old, H, 0), (mid, -8, 7), (mid, H, 0))):
        tile = ref[pl.ds(pl.multiple_of(start + shift, 8), 8), pl.ds(half, S * H)]
        line = tile[row : row + 1, :]
        xs[n : n + 1, :] = line
        xs[n + 4 : n + 5, :] = line
    index_x = ((lanes >> 4) & 3) * S + oz * H + (lanes & (H - 1))
    picked = [gather_lanes(xs[:, LANES * s : LANES * (s + 1)], index_x) for s in range(4)]
    low = jnp.where(lanes < 64, picked[0], picked[1])
    high = jnp.where(lanes < 64, picked[2], picked[3])
    faces = jnp.where(rows < 4, low, high)
    mean = 0.5 * (faces + pltpu.roll(faces, 2, 0))
    pack_ref[slot, 0:8, :] = jnp.where((rows & 2) == 0, faces, mean)
    index_y = oy * (LANES - S) + oz * H + (lanes & (H - 1))
    index_z = (lanes & 3) * S + H - oz
    y_group = pl.multiple_of(S * H - LANES * oy, LANES)
    for t in range(2):
        at = pl.multiple_of(start + 8 * t, 8)
        values = []
        for ref in (old, mid):
            y_face = gather_lanes(ref[pl.ds(at, 8), pl.ds(y_group, LANES)], index_y)
            parts = [
                gather_lanes(ref[pl.ds(at, 8), pl.ds(pl.multiple_of(half + LANES * s, LANES), LANES)], index_z)
                for s in range(4)
            ]
            which = (lanes >> 2) & 3
            z_face = jnp.where(
                which < 2,
                jnp.where(which == 0, parts[0], parts[1]),
                jnp.where(which == 2, parts[2], parts[3]),
            )
            values.append(jnp.where((lanes & S) == 0, z_face, y_face))
        face = jnp.where(lanes < 64, values[0], 0.5 * (values[0] + values[1]))
        used = ((lanes >> 4) & 1) == jnp.where((lanes & S) == 0, oz, oy)
        pack_ref[slot, 8 + 8 * t : 16 + 8 * t, :] = jnp.where(used, face, 0.0)


def list_boxes(parents, hits, boxes, octants):
    dev, devices = lax.axis_index("dev"), lax.axis_size("dev")
    group, groups = lax.axis_index("group"), lax.axis_size("group")
    for r in range(3):
        source = lax.rem(dev + devices + r - 1, devices)
        for s in range(groups):
            first = (lax.rem(group + groups - s, groups) * devices + source) * boxes
            row = r * groups + s
            count = jnp.int32(0)
            for k in range(boxes):
                local_id = parents[first + k] - dev * octants
                hits[row, count] = k * octants + local_id
                inside = jnp.logical_and(local_id >= 0, local_id < octants)
                count = count + inside.astype(jnp.int32)
            hits[row, boxes] = count


def step_tile(uc, pc, qc, ul, pll, ql, uh, ph, qh, lanes):
    sum_u = sum_yz(uc, lanes, False)
    sum_w = sum_yz([a * b for a, b in zip(pc, uc)], lanes, False)
    sum_q = sum_yz(qc, lanes, True)
    out = []
    for j in range(GROUPS):
        keep = (1.0 - 6.0 * pc[j]) - (sum_q[j] + (ql[j] + qh[j]))
        near_u = sum_u[j] + (ul[j] + uh[j])
        near_w = sum_w[j] + (pll[j] * ul[j] + ph[j] * uh[j])
        out.append(keep * uc[j] + (qc[j] * near_u + near_w))
    return out


def coarse_kernel(parents, u_any, k_any, v_any, near_sum, mid_out, hits, u, p, q, kv, split, sums, sems, *, boxes):
    rows, wide = mid_out.shape
    base = 8
    rate = 0.5 * RATE
    inner = slice(LANES, LANES + wide)
    copies = [
        pltpu.make_async_copy(k_any, kv.at[0:rows, inner], sems.at[0]),
        pltpu.make_async_copy(v_any, kv.at[rows : 2 * rows, inner], sems.at[1]),
        pltpu.make_async_copy(u_any, u.at[base : base + rows, :], sems.at[2]),
    ]
    for copy in copies:
        copy.start()
    for ref in (kv, split):
        for lane in (0, LANES + wide):
            ref[:, lane : lane + LANES] = jnp.zeros((ref.shape[0], LANES), jnp.bfloat16)
    for ref in (u, p, q):
        for row in (0, base + rows):
            ref[row : row + 8, :] = jnp.zeros((8, wide), jnp.float32)
    list_boxes(parents, hits, boxes, OCTANTS * (rows // S))
    for copy in copies:
        copy.wait()

    @pl.loop(0, rows // 16)
    def _(i):
        at = pl.multiple_of(i * 16, 16)
        to = pl.multiple_of(base + i * 16, 8)
        diff = rate * kv[pl.ds(at, 16), inner].astype(jnp.float32)
        pot = rate * kv[pl.ds(pl.multiple_of(rows + at, 16), 16), inner].astype(jnp.float32)
        dens = u[pl.ds(to, 16), :]
        p[pl.ds(to, 16), :] = diff + pot
        q[pl.ds(to, 16), :] = diff - pot
        for n, part in enumerate(pieces_of(dens) + pieces_of((diff + pot) * dens)):
            split[pl.ds(pl.multiple_of(n * rows + at, 16), 16), inner] = part

    near = near_sum[...]
    for n in range(4):
        window, out = slice(256 * n, 256 * n + 512), slice(256 * n, 256 * n + 256)
        sums[0:rows, out] = rate * (product(kv[0:rows, window], near) - product(kv[rows : 2 * rows, window], near))
        for f in (0, 2):
            sums[(f // 2 + 1) * rows : (f // 2 + 2) * rows, out] = product(
                split[f * rows : (f + 1) * rows, window], near
            ) + product(split[(f + 1) * rows : (f + 2) * rows, window], near)

    ends = edge_count()

    @pl.loop(0, rows // 8)
    def _(i):
        at = pl.multiple_of(i * 8, 8)
        uv, pv, qv = (ref.at[pl.ds(at, 24), :] for ref in (u, p, q))
        sum_q, sum_u, sum_w = (sums[pl.ds(pl.multiple_of(n * rows + at, 8), 8), :] for n in range(3))
        uc, pc, qc = (view[8:16, :] for view in (uv, pv, qv))
        ul, uh = uv[7:15, :], uv[9:17, :]
        keep = (1.0 - 6.0 * pc) - (sum_q + ends * qc + (qv[7:15, :] + qv[9:17, :]))
        near_u = sum_u + (ul + uh)
        near_w = sum_w + (pv[7:15, :] * ul + pv[9:17, :] * uh)
        mid_out[pl.ds(at, 8), :] = keep * uc + (qc * near_u + near_w)


def rims_kernel(parents, u_any, mid_any, k_first, v_first, k_last, v_last, near_edge, far_edge, to_near, to_own, to_far, fixed, u, m, e, xs, sems, *, boxes):
    rows = u_any.shape[0]
    base = 16
    rate = 0.5 * RATE
    devices = lax.axis_size("dev")
    dev, near_dev, far_dev, odd = sides()
    group = lax.axis_index("group")
    octants = OCTANTS * (rows // S)
    copies = [
        pltpu.make_async_copy(u_any, u.at[pl.ds(base, rows), :], sems.at[0]),
        pltpu.make_async_copy(mid_any, m.at[pl.ds(base, rows), :], sems.at[1]),
    ]
    for copy in copies:
        copy.start()
    lanes = lane_ids()
    for copy in copies:
        copy.wait()
    before = jnp.where(odd == 1, near_edge[...], far_edge[...])
    after = jnp.where(odd == 1, far_edge[...], near_edge[...])
    u[base - 2 : base, :] = before[0:2, :]
    u[base + rows : base + rows + 2, :] = after[0:2, :]
    for n, (far, k_ref, v_ref, own, top) in enumerate(
        ((before, k_first, v_first, 0, base - 2), (after, k_last, v_last, 14, base + rows - 2))
    ):
        e[0, 7:11, :] = u[top : top + 4, :]
        own_diff = rate * k_ref[...].astype(jnp.float32)[own : own + 2, :]
        own_pot = rate * v_ref[...].astype(jnp.float32)[own : own + 2, :]
        far_diff, far_pot = rate * far[2:4, :], rate * far[4:6, :]
        there, here = (7, 9) if n == 0 else (9, 7)
        e[1, there : there + 2, :] = far_diff + far_pot
        e[2, there : there + 2, :] = far_diff - far_pot
        e[1, here : here + 2, :] = own_diff + own_pot
        e[2, here : here + 2, :] = own_diff - own_pot
        tiles = [lane_groups(e.at[f], row) for row in (8, 7, 9) for f in range(3)]
        for j, new in enumerate(step_tile(*tiles, lanes)):
            m[top + 1 : top + 3, LANES * j : LANES * (j + 1)] = new[0:2, :]
    fixed[0:8, :] = m[base : base + 8, :]
    fixed[8:16, :] = m[base + rows - 8 : base + rows, :]

    for ref, target in ((to_far, far_dev), (to_near, near_dev), (to_own, dev)):
        for k in range(boxes):
            local_id = parents[(group * devices + target) * boxes + k] - dev * octants
            local_id = jnp.minimum(jnp.maximum(local_id, 0), octants - 1)
            pack_rims(u, m, xs, ref, k, local_id, base)


def fine_kernel(parents, u_any, k_any, v_any, near_sum, ghost_sum, block_sum, from_near, from_own, from_far, out_any, avg_ref, u0, w0, u1, w1, p, q, keep, kv, split, sums, ghosts, faces, dup, res, means, sems, out_sems, *, boxes, octants):
    devices = lax.axis_size("dev")
    dev, near_dev, _, _ = sides()
    group = lax.axis_index("group")
    rows, wide = res.shape
    base = 8
    inner = slice(LANES, LANES + wide)
    copies = [
        pltpu.make_async_copy(k_any, kv.at[0:rows, inner], sems.at[0]),
        pltpu.make_async_copy(v_any, kv.at[rows : 2 * rows, inner], sems.at[1]),
        pltpu.make_async_copy(u_any, res, sems.at[2]),
    ]
    for copy in copies:
        copy.start()
    for ref in (kv, split):
        for lane in (0, LANES + wide):
            ref[:, lane : lane + LANES] = jnp.zeros((ref.shape[0], LANES), jnp.bfloat16)

    lanes = lane_ids()
    z = lanes & (S - 1)
    wide_faces = []
    for k in range(boxes):
        parent = parents[(group * devices + dev) * boxes + k]
        own_id, near_id = parent - dev * octants, parent - near_dev * octants
        is_own = jnp.logical_and(own_id >= 0, own_id < octants)
        is_near = jnp.logical_and(near_id >= 0, near_id < octants)

        def chosen(n):
            there = slice(8 * n, 8 * n + 8)
            other = jnp.where(is_near, from_near[k, there, :], from_far[k, there, :])
            return jnp.where(is_own, from_own[k, there, :], other)

        for n in range(2):
            face = chosen(n + 1)
            dup[pl.ds(S * k + 16 * n, 8, 2), :] = face
            dup[pl.ds(S * k + 16 * n + 1, 8, 2), :] = face
        for n, part in enumerate(pieces_of(dup[S * k : S * k + S, :])):
            faces[n * rows + S * k : n * rows + S * k + S, :] = part
        x_faces = chosen(0)
        for n in range(4):
            spread = gather_lanes(x_faces, (2 * n + (lanes >> 6)) * H + (z >> 1))
            for half in range(2):
                j = 4 * half + n
                there = slice(LANES * j, LANES * (j + 1))
                u0[k, 7:8, there] = spread[4 * half : 4 * half + 1, :]
                u0[k, 40:41, there] = spread[4 * half + 1 : 4 * half + 2, :]
                u1[k, 7:8, there] = spread[4 * half + 2 : 4 * half + 3, :]
                u1[k, 40:41, there] = spread[4 * half + 3 : 4 * half + 4, :]
    for copy in copies:
        copy.wait()

    def store_split(k, i, dens, other):
        for n, part in enumerate(pieces_of(dens) + pieces_of(other)):
            split[pl.ds(pl.multiple_of(n * rows + S * k + 16 * i, 16), 16), inner] = part

    @pl.loop(0, boxes)
    def _(k):
        for i in range(2):
            at, to = pl.multiple_of(S * k + 16 * i, 16), base + 16 * i
            diff = RATE * kv[pl.ds(at, 16), inner].astype(jnp.float32)
            pot = (0.5 * RATE) * kv[pl.ds(pl.multiple_of(rows + at, 16), 16), inner].astype(jnp.float32)
            dens = res[pl.ds(at, 16), :]
            p[k, to : to + 16, :] = diff + pot
            q[k, to : to + 16, :] = diff - pot
            u0[k, to : to + 16, :] = dens
            w0[k, to : to + 16, :] = (diff + pot) * dens
            store_split(k, i, dens, (diff + pot) * dens)
        for ghost, cell in ((7, 8), (40, 39)):
            q[k, ghost : ghost + 1, :] = q[k, cell : cell + 1, :]
            for u, w in ((u0, w0), (u1, w1)):
                w[k, ghost : ghost + 1, :] = p[k, cell : cell + 1, :] * u[k, ghost : ghost + 1, :]

    near = near_sum[...]

    def sum_all(step):
        for n in range(4):
            window, out = slice(256 * n, 256 * n + 512), slice(256 * n, 256 * n + 256)
            for f in range(2):
                high, low = (split[(2 * f + h) * rows : (2 * f + h + 1) * rows, window] for h in range(2))
                sums[f * rows : (f + 1) * rows, out] = product(high, near) + product(low, near)
            if step == 0:
                sums[2 * rows : 3 * rows, out] = RATE * product(kv[0:rows, window], near) - (0.5 * RATE) * product(
                    kv[rows : 2 * rows, window], near
                )
            matrix = ghost_sum[step, :, out]
            ghosts[:, out] = product(faces[0:rows, :], matrix) + product(faces[rows : 2 * rows, :], matrix)

    ends = edge_count()
    outs = []
    for step, (u, w) in enumerate(((u0, w0), (u1, w1))):
        sum_all(step)

        @pl.loop(0, boxes)
        def _(k):
            for i in range(2):
                at, to = pl.multiple_of(S * k + 16 * i, 16), base + 16 * i
                here, low, high = (slice(to + m, to + m + 16) for m in (0, -1, 1))
                sum_u = sums[pl.ds(at, 16), :] + (u[k, low, :] + u[k, high, :])
                sum_w = sums[pl.ds(pl.multiple_of(rows + at, 16), 16), :] + (w[k, low, :] + w[k, high, :])
                pc, qc, uc = p[k, here, :], q[k, here, :], u[k, here, :]
                if step == 0:
                    sum_q = sums[pl.ds(pl.multiple_of(2 * rows + at, 16), 16), :] + (q[k, low, :] + q[k, high, :])
                    stay = (1.0 - 6.0 * pc) - (sum_q + ends * qc)
                    keep[pl.ds(at, 16), :] = stay
                else:
                    stay = keep[pl.ds(at, 16), :]
                new = (stay * uc + (qc * sum_u + sum_w)) + (pc + qc) * ghosts[pl.ds(at, 16), :]
                if step == 0:
                    u1[k, here, :] = new
                    w1[k, here, :] = pc * new
                    store_split(k, i, new, pc * new)
                else:
                    res[pl.ds(at, 16), :] = new
                    for n, part in enumerate(pieces_of(new)):
                        split[pl.ds(pl.multiple_of(n * rows + at, 16), 16), inner] = part

    out_copy = pltpu.make_async_copy(res, out_any, out_sems.at[0])
    out_copy.start()
    blocks = block_sum[...]
    total = product(split[0:rows, inner], blocks) + product(split[rows : 2 * rows, inner], blocks)
    for half in range(2):
        means[half, :, :] = total[:, LANES * half : LANES * (half + 1)]
    for half in range(2):
        for k in range(boxes):
            for t in range(2):
                at = S * k + 16 * t
                pair = means[half, pl.ds(at, 8, 2), :] + means[half, pl.ds(at + 1, 8, 2), :]
                avg_ref[k, 8 * t : 8 * t + 8, LANES * half : LANES * (half + 1)] = 0.125 * pair
    out_copy.wait()


def join_kernel(*refs):
    *pieces, out_ref = refs
    count = pieces[0].shape[0]
    for n, piece in enumerate(pieces):
        out_ref[n * count : (n + 1) * count] = piece[...]


def put_averages(hits, ref, first, row, out_ref, boxes, octants):
    lanes = lane_ids()

    @pl.loop(0, hits[row, boxes])
    def _(n):
        entry = hits[row, n]
        box = lax.div(entry, jnp.int32(octants))
        start, oy, oz = octant_place(entry - box * octants)
        here = ((lanes >> 4) & 1) == oz
        for t in range(2):
            at = pl.multiple_of(start + 8 * t, 8)
            for s in range(4):
                there = pl.ds(pl.multiple_of(oy * (S * H) + LANES * s, LANES), LANES)
                half = s // 2
                tile = ref[first + box, 8 * t : 8 * t + 8, LANES * half : LANES * (half + 1)]
                moved = gather_lanes(tile, (s % 2) * 64 + (lanes >> 5) * H + (lanes & (H - 1)))
                out_ref[pl.ds(at, 8), there] = jnp.where(here, moved, out_ref[pl.ds(at, 8), there])


def merge_own_kernel(hits, mid_ref, fixed, own, out_ref, *, boxes, octants):
    groups = lax.axis_size("group")
    rows = out_ref.shape[0]

    @pl.loop(1, rows // 8 - 1)
    def _(i):
        at = pl.multiple_of(i * 8, 8)
        out_ref[pl.ds(at, 8), :] = mid_ref[pl.ds(at, 8), :]

    out_ref[0:8, :] = fixed[0:8, :]
    out_ref[rows - 8 : rows, :] = fixed[8:16, :]
    for s in range(groups):
        put_averages(hits, own, s * boxes, groups + s, out_ref, boxes, octants)


def merge_far_kernel(hits, held_any, near_ref, far_ref, out_ref, sem, *, boxes, octants):
    groups = lax.axis_size("group")
    _, _, _, odd = sides()
    copy = pltpu.make_async_copy(held_any, out_ref, sem)
    copy.start()
    copy.wait()
    for ref, r in ((near_ref, 2 - 2 * odd), (far_ref, 2 * odd)):
        for s in range(groups):
            put_averages(hits, ref, s * boxes, r * groups + s, out_ref, boxes, octants)


def params():
    return pltpu.CompilerParams(vmem_limit_bytes=VMEM_LIMIT)


def cost(flops, size):
    return pl.CostEstimate(flops=flops, bytes_accessed=size, transcendentals=0)


def f32(*shape):
    return jax.ShapeDtypeStruct(shape, jnp.float32)


def vmem(*shape):
    return pltpu.VMEM(shape, jnp.float32)


def bf16(*shape):
    return pltpu.VMEM(shape, jnp.bfloat16)


def whole():
    return pl.BlockSpec(memory_space=pltpu.VMEM)


def on_device(coarse_dens, coarse_diff, coarse_pot, fine_dens, fine_diff, fine_pot, parents):
    devices = lax.axis_size("dev")
    groups = lax.axis_size("group")
    rows = coarse_dens.shape[0]
    boxes = fine_dens.shape[0] // S
    fine_rows = boxes * S
    octants = OCTANTS * (rows // S)
    wide = S * S
    smem = pl.BlockSpec(memory_space=pltpu.SMEM)
    anywhere = pl.BlockSpec(memory_space=pl.ANY)
    dma = pltpu.SemaphoreType.DMA
    near_pairs = [(i, i ^ 1) for i in range(devices)]
    far_pairs = [(i, (i + devices - 1 + 2 * (i & 1)) % devices) for i in range(devices)]

    def swap(near, far):
        got_far = lax.ppermute(far, "dev", far_pairs)
        return lax.ppermute(near, "dev", near_pairs), got_far

    near_edge, far_edge = pl.pallas_call(
        edges_kernel,
        grid=(1,),
        in_specs=[
            pl.BlockSpec((8, wide), lambda i: (0, 0)),
            pl.BlockSpec((16, wide), lambda i: (0, 0)),
            pl.BlockSpec((16, wide), lambda i: (0, 0)),
            pl.BlockSpec((8, wide), lambda i: (rows // 8 - 1, 0)),
            pl.BlockSpec((16, wide), lambda i: (rows // 16 - 1, 0)),
            pl.BlockSpec((16, wide), lambda i: (rows // 16 - 1, 0)),
        ],
        out_specs=[pl.BlockSpec((8, wide), lambda i: (0, 0))] * 2,
        out_shape=[f32(8, wide)] * 2,
        name="edges",
    )(coarse_dens, coarse_diff, coarse_pot, coarse_dens, coarse_diff, coarse_pot)
    near_edge, far_edge = swap(near_edge, far_edge)

    near_sum = neighbour_matrix()
    mid, hits = pl.pallas_call(
        functools.partial(coarse_kernel, boxes=boxes),
        grid_spec=pltpu.PrefetchScalarGridSpec(
            num_scalar_prefetch=1,
            grid=(),
            in_specs=[anywhere] * 3 + [whole()],
            out_specs=[whole(), smem],
            scratch_shapes=[vmem(rows + 16, wide)] * 3
            + [bf16(2 * rows, wide + 2 * LANES), bf16(4 * rows, wide + 2 * LANES), vmem(3 * rows, wide), dma((3,))],
        ),
        out_shape=[f32(rows, wide), jax.ShapeDtypeStruct((3 * groups, boxes + 1), jnp.int32)],
        compiler_params=params(),
        cost_estimate=cost(rows * wide * 40, rows * wide * 12),
        name="coarse",
    )(parents, coarse_dens, coarse_diff, coarse_pot, near_sum)

    packs = f32(boxes, PACK, LANES)
    top = pl.BlockSpec((16, wide), lambda i, ids: (0, 0))
    bottom = pl.BlockSpec((16, wide), lambda i, ids: (rows // 16 - 1, 0))
    edge = pl.BlockSpec((8, wide), lambda i, ids: (0, 0))
    pack = pl.BlockSpec((boxes, PACK, LANES), lambda i, ids: (0, 0, 0))
    to_near, own, to_far, fixed = pl.pallas_call(
        functools.partial(rims_kernel, boxes=boxes),
        grid_spec=pltpu.PrefetchScalarGridSpec(
            num_scalar_prefetch=1,
            grid=(1,),
            in_specs=[anywhere, anywhere, top, top, bottom, bottom, edge, edge],
            out_specs=[pack, pack, pack, pl.BlockSpec((16, wide), lambda i, ids: (0, 0))],
            scratch_shapes=[vmem(rows + 32, wide)] * 2 + [vmem(3, 24, wide), vmem(8, S * H), dma((2,))],
        ),
        out_shape=[packs, packs, packs, f32(16, wide)],
        compiler_params=params(),
        cost_estimate=cost(rows * wide * 8, rows * wide * 8),
        name="rims",
    )(parents, coarse_dens, mid, coarse_diff, coarse_pot, coarse_diff, coarse_pot, near_edge, far_edge)
    from_near, from_far = swap(to_near, to_far)

    fine_out, averages = pl.pallas_call(
        functools.partial(fine_kernel, boxes=boxes, octants=octants),
        grid_spec=pltpu.PrefetchScalarGridSpec(
            num_scalar_prefetch=1,
            grid=(),
            in_specs=[anywhere] * 3 + [whole()] * 6,
            out_specs=[anywhere, whole()],
            scratch_shapes=[vmem(boxes, 48, wide)] * 6
            + [
                vmem(fine_rows, wide),
                bf16(2 * fine_rows, wide + 2 * LANES),
                bf16(4 * fine_rows, wide + 2 * LANES),
                vmem(3 * fine_rows, wide),
                vmem(fine_rows, wide),
                bf16(2 * fine_rows, LANES),
                vmem(fine_rows, LANES),
                vmem(fine_rows, wide),
                vmem(2, fine_rows, LANES),
                dma((3,)),
                dma((1,)),
            ],
        ),
        out_shape=[f32(fine_rows, wide), f32(boxes, H, H * H)],
        compiler_params=params(),
        cost_estimate=cost(fine_rows * wide * 80, fine_rows * wide * 12),
        name="fine",
    )(parents, fine_dens, fine_diff, fine_pot, near_sum, ghost_matrices(), average_matrix(), from_near, own, from_far)

    pieces = [averages]
    for s in range(1, groups):
        pieces.append(lax.ppermute(averages, "group", [(i, (i + s) % groups) for i in range(groups)]))
    joined = pl.pallas_call(
        join_kernel,
        in_specs=[whole()] * groups,
        out_specs=whole(),
        out_shape=f32(groups * boxes, H, H * H),
        compiler_params=params(),
        name="join",
    )(*pieces)
    near_avg, far_avg = swap(joined, joined)

    def merge(kernel, specs, scratch, name):
        return pl.pallas_call(
            functools.partial(kernel, boxes=boxes, octants=octants),
            grid_spec=pltpu.PrefetchScalarGridSpec(
                num_scalar_prefetch=1, grid=(), in_specs=specs, out_specs=whole(), scratch_shapes=scratch
            ),
            out_shape=f32(rows, wide),
            compiler_params=params(),
            cost_estimate=cost(rows * wide * 4, rows * wide * 12),
            name=name,
        )

    merged = merge(merge_own_kernel, [whole()] * 3, [], "merge_own")(hits, mid, fixed, joined)
    coarse_out = merge(merge_far_kernel, [anywhere, whole(), whole()], [dma], "merge_far")(
        hits, merged, near_avg, far_avg
    )
    return coarse_out, fine_out


def solution(mesh):
    in_specs = (
        P("dev", None),
        P("dev", None),
        P("dev", None),
        P(("group", "dev"), None),
        P(("group", "dev"), None),
        P(("group", "dev"), None),
        P(),
    )
    out_specs = (P("dev", None), P(("group", "dev"), None))
    return jax.shard_map(on_device, mesh=mesh, in_specs=in_specs, out_specs=out_specs, check_vma=False)
```

```python
import functools

import jax
import jax.numpy as jnp
import numpy as np
from jax import lax
from jax.experimental import pallas as pl
from jax.experimental.pallas import tpu as pltpu
from jax.sharding import PartitionSpec as P

S = 32
H = 16
LANES = 128
GROUPS = 8
OCTANTS = 8
PACK = 24
RATE = 0.06
VMEM_LIMIT = 48 * 1024 * 1024


def neighbour_matrix():
    source, target = np.arange(512)[:, None] - LANES, np.arange(256)[None, :]
    step = source - target
    same_y = source // S == target // S
    return jnp.asarray((np.abs(step) == S) | ((np.abs(step) == 1) & same_y), jnp.bfloat16)


def ghost_matrices():
    source, target = np.arange(LANES)[:, None], np.arange(S * S)[None, :]
    part, place = (source >> 4) & 3, source & (H - 1)
    y, z = target // S, target % S
    faces = (
        ((part == 0) & (z == S - 1) & (y // 2 == place))
        | ((part == 1) & (z == 0) & (y // 2 == place))
        | ((part == 2) & (y == S - 1) & (z // 2 == place))
        | ((part == 3) & (y == 0) & (z // 2 == place))
    )
    return jnp.asarray(np.stack([faces & (source // 64 == step) for step in range(2)]), jnp.bfloat16)


def average_matrix():
    source, target = np.arange(S * S)[:, None], np.arange(H * H)[None, :]
    return jnp.asarray((source // S // 2 == target // H) & (source % S // 2 == target % H), jnp.bfloat16)


def pieces_of(value):
    high = value.astype(jnp.bfloat16)
    return high, (value - high.astype(jnp.float32)).astype(jnp.bfloat16)


def product(left, right):
    return jnp.dot(left, right, preferred_element_type=jnp.float32)


def sides():
    dev, devices = lax.axis_index("dev"), lax.axis_size("dev")
    odd = dev & 1
    near = dev + 1 - 2 * odd
    far = lax.rem(dev + devices - 1 + 2 * odd, devices)
    return dev, near, far, odd


def edge_count():
    lane = lax.broadcasted_iota(jnp.int32, (1, S * S), 1)
    z, y = lane & (S - 1), lane >> 5
    return sum((at == end).astype(jnp.float32) for at in (z, y) for end in (0, S - 1))


def lane_ids():
    return lax.broadcasted_iota(jnp.int32, (8, LANES), 1)


def row_ids():
    return lax.broadcasted_iota(jnp.int32, (8, LANES), 0)


def gather_lanes(tile, index):
    return jnp.take_along_axis(tile, index, axis=1, mode="promise_in_bounds")


def lane_groups(ref, row):
    return [ref[row : row + 8, LANES * j : LANES * (j + 1)] for j in range(GROUPS)]


def sum_yz(tiles, lanes, edge):
    z = lanes & (S - 1)
    up = [pltpu.roll(t, S, 1) for t in tiles]
    down = [pltpu.roll(t, LANES - S, 1) for t in tiles]
    out = []
    for j, tile in enumerate(tiles):
        fill = tile if edge else jnp.zeros_like(tile)
        low = jnp.where(lanes >= S, up[j], up[j - 1] if j > 0 else fill)
        high = jnp.where(lanes < LANES - S, down[j], down[j + 1] if j + 1 < GROUPS else fill)
        left = jnp.where(z != 0, pltpu.roll(tile, 1, 1), fill)
        right = jnp.where(z != S - 1, pltpu.roll(tile, LANES - 1, 1), fill)
        out.append((low + high) + (left + right))
    return out


def octant_place(local_id):
    box = local_id >> 3
    return box * S + ((local_id >> 2) & 1) * H, (local_id >> 1) & 1, local_id & 1


def edges_kernel(u0, k0, v0, u1, k1, v1, near_ref, far_ref):
    _, _, _, odd = sides()
    first = (u0[0:2, :], k0[...].astype(jnp.float32)[0:2, :], v0[...].astype(jnp.float32)[0:2, :])
    last = (u1[6:8, :], k1[...].astype(jnp.float32)[14:16, :], v1[...].astype(jnp.float32)[14:16, :])
    is_odd = odd == 1
    for n, (low, high) in enumerate(zip(first, last)):
        near_ref[2 * n : 2 * n + 2, :] = jnp.where(is_odd, low, high)
        far_ref[2 * n : 2 * n + 2, :] = jnp.where(is_odd, high, low)
    for ref in (near_ref, far_ref):
        ref[6:8, :] = jnp.zeros((2, S * S), jnp.float32)


def pack_rims(old, mid, xs, pack_ref, slot, local_id, base):
    lanes, rows = lane_ids(), row_ids()
    start, oy, oz = octant_place(local_id)
    start = start + base
    half = pl.multiple_of(oy * (S * H), LANES)
    for n, (ref, shift, row) in enumerate(((old, -8, 7), (old, H, 0), (mid, -8, 7), (mid, H, 0))):
        tile = ref[pl.ds(pl.multiple_of(start + shift, 8), 8), pl.ds(half, S * H)]
        line = tile[row : row + 1, :]
        xs[n : n + 1, :] = line
        xs[n + 4 : n + 5, :] = line
    index_x = ((lanes >> 4) & 3) * S + oz * H + (lanes & (H - 1))
    picked = [gather_lanes(xs[:, LANES * s : LANES * (s + 1)], index_x) for s in range(4)]
    low = jnp.where(lanes < 64, picked[0], picked[1])
    high = jnp.where(lanes < 64, picked[2], picked[3])
    faces = jnp.where(rows < 4, low, high)
    mean = 0.5 * (faces + pltpu.roll(faces, 2, 0))
    pack_ref[slot, 0:8, :] = jnp.where((rows & 2) == 0, faces, mean)
    index_y = oy * (LANES - S) + oz * H + (lanes & (H - 1))
    index_z = (lanes & 3) * S + H - oz
    y_group = pl.multiple_of(S * H - LANES * oy, LANES)
    for t in range(2):
        at = pl.multiple_of(start + 8 * t, 8)
        values = []
        for ref in (old, mid):
            y_face = gather_lanes(ref[pl.ds(at, 8), pl.ds(y_group, LANES)], index_y)
            parts = [
                gather_lanes(ref[pl.ds(at, 8), pl.ds(pl.multiple_of(half + LANES * s, LANES), LANES)], index_z)
                for s in range(4)
            ]
            which = (lanes >> 2) & 3
            z_face = jnp.where(
                which < 2,
                jnp.where(which == 0, parts[0], parts[1]),
                jnp.where(which == 2, parts[2], parts[3]),
            )
            values.append(jnp.where((lanes & S) == 0, z_face, y_face))
        face = jnp.where(lanes < 64, values[0], 0.5 * (values[0] + values[1]))
        used = ((lanes >> 4) & 1) == jnp.where((lanes & S) == 0, oz, oy)
        pack_ref[slot, 8 + 8 * t : 16 + 8 * t, :] = jnp.where(used, face, 0.0)


def find_boxes(parents, covers, boxes, octants):
    dev, devices = lax.axis_index("dev"), lax.axis_size("dev")
    group, groups = lax.axis_index("group"), lax.axis_size("group")
    for n in range(octants + 1):
        covers[n] = jnp.int32(-1)
    for r in range(3):
        source = lax.rem(dev + devices + r - 1, devices)
        for s in range(groups):
            first = (lax.rem(group + groups - s, groups) * devices + source) * boxes
            for k in range(boxes):
                local_id = parents[first + k] - dev * octants
                inside = jnp.logical_and(local_id >= 0, local_id < octants)
                covers[jnp.where(inside, local_id, octants)] = jnp.int32((r * groups + s) * boxes + k)


def step_tile(uc, pc, qc, ul, pll, ql, uh, ph, qh, lanes):
    sum_u = sum_yz(uc, lanes, False)
    sum_w = sum_yz([a * b for a, b in zip(pc, uc)], lanes, False)
    sum_q = sum_yz(qc, lanes, True)
    out = []
    for j in range(GROUPS):
        keep = (1.0 - 6.0 * pc[j]) - (sum_q[j] + (ql[j] + qh[j]))
        near_u = sum_u[j] + (ul[j] + uh[j])
        near_w = sum_w[j] + (pll[j] * ul[j] + ph[j] * uh[j])
        out.append(keep * uc[j] + (qc[j] * near_u + near_w))
    return out


def coarse_kernel(parents, u_any, k_any, v_any, near_sum, mid_out, covers, u, p, q, kv, split, sums, sems, *, boxes):
    rows, wide = mid_out.shape
    base = 8
    rate = 0.5 * RATE
    inner = slice(LANES, LANES + wide)
    copies = [
        pltpu.make_async_copy(k_any, kv.at[0:rows, inner], sems.at[0]),
        pltpu.make_async_copy(v_any, kv.at[rows : 2 * rows, inner], sems.at[1]),
        pltpu.make_async_copy(u_any, u.at[base : base + rows, :], sems.at[2]),
    ]
    for copy in copies:
        copy.start()
    for ref in (kv, split):
        for lane in (0, LANES + wide):
            ref[:, lane : lane + LANES] = jnp.zeros((ref.shape[0], LANES), jnp.bfloat16)
    for ref in (u, p, q):
        for row in (0, base + rows):
            ref[row : row + 8, :] = jnp.zeros((8, wide), jnp.float32)
    find_boxes(parents, covers, boxes, OCTANTS * (rows // S))
    for copy in copies:
        copy.wait()

    @pl.loop(0, rows // 16)
    def _(i):
        at = pl.multiple_of(i * 16, 16)
        to = pl.multiple_of(base + i * 16, 8)
        diff = rate * kv[pl.ds(at, 16), inner].astype(jnp.float32)
        pot = rate * kv[pl.ds(pl.multiple_of(rows + at, 16), 16), inner].astype(jnp.float32)
        dens = u[pl.ds(to, 16), :]
        p[pl.ds(to, 16), :] = diff + pot
        q[pl.ds(to, 16), :] = diff - pot
        for n, part in enumerate(pieces_of(dens) + pieces_of((diff + pot) * dens)):
            split[pl.ds(pl.multiple_of(n * rows + at, 16), 16), inner] = part

    near = near_sum[...]
    for n in range(4):
        window, out = slice(256 * n, 256 * n + 512), slice(256 * n, 256 * n + 256)
        sums[0:rows, out] = rate * (product(kv[0:rows, window], near) - product(kv[rows : 2 * rows, window], near))
        for f in (0, 2):
            sums[(f // 2 + 1) * rows : (f // 2 + 2) * rows, out] = product(
                split[f * rows : (f + 1) * rows, window], near
            ) + product(split[(f + 1) * rows : (f + 2) * rows, window], near)

    ends = edge_count()

    @pl.loop(0, rows // 8)
    def _(i):
        at = pl.multiple_of(i * 8, 8)
        uv, pv, qv = (ref.at[pl.ds(at, 24), :] for ref in (u, p, q))
        sum_q, sum_u, sum_w = (sums[pl.ds(pl.multiple_of(n * rows + at, 8), 8), :] for n in range(3))
        uc, pc, qc = (view[8:16, :] for view in (uv, pv, qv))
        ul, uh = uv[7:15, :], uv[9:17, :]
        keep = (1.0 - 6.0 * pc) - (sum_q + ends * qc + (qv[7:15, :] + qv[9:17, :]))
        near_u = sum_u + (ul + uh)
        near_w = sum_w + (pv[7:15, :] * ul + pv[9:17, :] * uh)
        mid_out[pl.ds(at, 8), :] = keep * uc + (qc * near_u + near_w)


def rims_kernel(parents, u_any, mid_any, k_first, v_first, k_last, v_last, near_edge, far_edge, to_near, to_own, to_far, fixed, u, m, e, xs, sems, *, boxes):
    rows = u_any.shape[0]
    base = 16
    rate = 0.5 * RATE
    devices = lax.axis_size("dev")
    dev, near_dev, far_dev, odd = sides()
    group = lax.axis_index("group")
    octants = OCTANTS * (rows // S)
    copies = [
        pltpu.make_async_copy(u_any, u.at[pl.ds(base, rows), :], sems.at[0]),
        pltpu.make_async_copy(mid_any, m.at[pl.ds(base, rows), :], sems.at[1]),
    ]
    for copy in copies:
        copy.start()
    lanes = lane_ids()
    for copy in copies:
        copy.wait()
    before = jnp.where(odd == 1, near_edge[...], far_edge[...])
    after = jnp.where(odd == 1, far_edge[...], near_edge[...])
    u[base - 2 : base, :] = before[0:2, :]
    u[base + rows : base + rows + 2, :] = after[0:2, :]
    for n, (far, k_ref, v_ref, own, top) in enumerate(
        ((before, k_first, v_first, 0, base - 2), (after, k_last, v_last, 14, base + rows - 2))
    ):
        e[0, 7:11, :] = u[top : top + 4, :]
        own_diff = rate * k_ref[...].astype(jnp.float32)[own : own + 2, :]
        own_pot = rate * v_ref[...].astype(jnp.float32)[own : own + 2, :]
        far_diff, far_pot = rate * far[2:4, :], rate * far[4:6, :]
        there, here = (7, 9) if n == 0 else (9, 7)
        e[1, there : there + 2, :] = far_diff + far_pot
        e[2, there : there + 2, :] = far_diff - far_pot
        e[1, here : here + 2, :] = own_diff + own_pot
        e[2, here : here + 2, :] = own_diff - own_pot
        tiles = [lane_groups(e.at[f], row) for row in (8, 7, 9) for f in range(3)]
        for j, new in enumerate(step_tile(*tiles, lanes)):
            m[top + 1 : top + 3, LANES * j : LANES * (j + 1)] = new[0:2, :]
    fixed[0:8, :] = m[base : base + 8, :]
    fixed[8:16, :] = m[base + rows - 8 : base + rows, :]

    for ref, target in ((to_far, far_dev), (to_near, near_dev), (to_own, dev)):
        for k in range(boxes):
            local_id = parents[(group * devices + target) * boxes + k] - dev * octants
            local_id = jnp.minimum(jnp.maximum(local_id, 0), octants - 1)
            pack_rims(u, m, xs, ref, k, local_id, base)


def load_padded(k_any, v_any, kv, split, rows, sems):
    inner = slice(LANES, LANES + S * S)
    copies = [
        pltpu.make_async_copy(k_any, kv.at[0:rows, inner], sems.at[0]),
        pltpu.make_async_copy(v_any, kv.at[rows : 2 * rows, inner], sems.at[1]),
    ]
    for copy in copies:
        copy.start()
    for ref in (kv, split):
        for lane in (0, LANES + S * S):
            ref[:, lane : lane + LANES] = jnp.zeros((ref.shape[0], LANES), jnp.bfloat16)
    return copies


def fine_rates(kv, rows, at):
    inner = slice(LANES, LANES + S * S)
    diff = RATE * kv[pl.ds(at, 16), inner].astype(jnp.float32)
    pot = (0.5 * RATE) * kv[pl.ds(pl.multiple_of(rows + at, 16), 16), inner].astype(jnp.float32)
    return diff + pot, diff - pot


def store_split(split, rows, at, *values):
    parts = [part for value in values for part in pieces_of(value)]
    for n, part in enumerate(parts):
        split[pl.ds(pl.multiple_of(n * rows + at, 16), 16), LANES : LANES + S * S] = part


def sum_two(split, sums, near, rows, n):
    window, out = slice(256 * n, 256 * n + 512), slice(256 * n, 256 * n + 256)
    for f in range(2):
        high, low = (split[(2 * f + h) * rows : (2 * f + h + 1) * rows, window] for h in range(2))
        sums[f * rows : (f + 1) * rows, out] = product(high, near) + product(low, near)


def fine_first_kernel(u_any, k_any, v_any, near_sum, out_ref, keep_ref, u, w, p, q, kv, split, sums, sems, *, boxes):
    rows, wide = out_ref.shape
    base = 8
    copies = load_padded(k_any, v_any, kv, split, rows, sems)
    copies.append(pltpu.make_async_copy(u_any, out_ref, sems.at[2]))
    copies[2].start()
    for copy in copies:
        copy.wait()

    @pl.loop(0, boxes)
    def _(k):
        for ref in (u, w):
            for ghost in (7, 40):
                ref[k, ghost : ghost + 1, :] = jnp.zeros((1, wide), jnp.float32)
        for i in range(2):
            at, to = pl.multiple_of(S * k + 16 * i, 16), base + 16 * i
            pc, qc = fine_rates(kv, rows, at)
            dens = out_ref[pl.ds(at, 16), :]
            p[k, to : to + 16, :] = pc
            q[k, to : to + 16, :] = qc
            u[k, to : to + 16, :] = dens
            w[k, to : to + 16, :] = pc * dens
            store_split(split, rows, at, dens, pc * dens)
        for ghost, cell in ((7, 8), (40, 39)):
            q[k, ghost : ghost + 1, :] = q[k, cell : cell + 1, :]

    near = near_sum[...]
    for n in range(4):
        window, out = slice(256 * n, 256 * n + 512), slice(256 * n, 256 * n + 256)
        sum_two(split, sums, near, rows, n)
        sums[2 * rows : 3 * rows, out] = RATE * product(kv[0:rows, window], near) - (0.5 * RATE) * product(
            kv[rows : 2 * rows, window], near
        )
    ends = edge_count()

    @pl.loop(0, boxes)
    def _(k):
        for i in range(2):
            at, to = pl.multiple_of(S * k + 16 * i, 16), base + 16 * i
            here, low, high = (slice(to + m, to + m + 16) for m in (0, -1, 1))
            sum_u, sum_w, sum_q = (
                sums[pl.ds(pl.multiple_of(n * rows + at, 16), 16), :] + (ref[k, low, :] + ref[k, high, :])
                for n, ref in enumerate((u, w, q))
            )
            qc = q[k, here, :]
            stay = (1.0 - 6.0 * p[k, here, :]) - (sum_q + ends * qc)
            keep_ref[pl.ds(at, 16), :] = stay
            out_ref[pl.ds(at, 16), :] = stay * u[k, here, :] + (qc * sum_u + sum_w)


def fine_second_kernel(parents, u_any, keep_any, k_any, v_any, near_sum, ghost_sum, block_sum, from_near, from_own, from_far, out_any, avg_ref, u, w, p, q, lines, kv, split, sums, ghosts, faces, dup, keep, res, means, sems, out_sems, *, boxes, octants):
    devices = lax.axis_size("dev")
    dev, near_dev, _, _ = sides()
    group = lax.axis_index("group")
    rows, wide = res.shape
    base = 8
    copies = load_padded(k_any, v_any, kv, split, rows, sems)
    copies.append(pltpu.make_async_copy(u_any, res, sems.at[2]))
    copies.append(pltpu.make_async_copy(keep_any, keep, sems.at[3]))
    for copy in copies[2:]:
        copy.start()

    lanes = lane_ids()
    z = lanes & (S - 1)
    for k in range(boxes):
        parent = parents[(group * devices + dev) * boxes + k]
        own_id, near_id = parent - dev * octants, parent - near_dev * octants
        is_own = jnp.logical_and(own_id >= 0, own_id < octants)
        is_near = jnp.logical_and(near_id >= 0, near_id < octants)

        def chosen(n):
            there = slice(8 * n, 8 * n + 8)
            other = jnp.where(is_near, from_near[k, there, :], from_far[k, there, :])
            return jnp.where(is_own, from_own[k, there, :], other)

        for n in range(2):
            face = chosen(n + 1)
            dup[pl.ds(S * k + 16 * n, 8, 2), :] = face
            dup[pl.ds(S * k + 16 * n + 1, 8, 2), :] = face
        for n, part in enumerate(pieces_of(dup[S * k : S * k + S, :])):
            faces[n * rows + S * k : n * rows + S * k + S, :] = part
        x_faces = chosen(0)
        for n in range(4):
            spread = gather_lanes(x_faces, (2 * n + (lanes >> 6)) * H + (z >> 1))
            for half in range(2):
                j = 4 * half + n
                there = slice(LANES * j, LANES * (j + 1))
                lines[k, 0:2, there] = spread[4 * half : 4 * half + 2, :]
                u[k, 7:8, there] = spread[4 * half + 2 : 4 * half + 3, :]
                u[k, 40:41, there] = spread[4 * half + 3 : 4 * half + 4, :]
    for n in range(4):
        out = slice(256 * n, 256 * n + 256)
        for step in range(2):
            matrix = ghost_sum[step, :, out]
            ghosts[step * rows : (step + 1) * rows, out] = product(faces[0:rows, :], matrix) + product(
                faces[rows : 2 * rows, :], matrix
            )
    for copy in copies:
        copy.wait()

    row = lax.broadcasted_iota(jnp.int32, (16, wide), 0)

    @pl.loop(0, boxes)
    def _(k):
        for i in range(2):
            at, to = pl.multiple_of(S * k + 16 * i, 16), base + 16 * i
            pc, qc = fine_rates(kv, rows, at)
            beside = ghosts[pl.ds(at, 16), :] + jnp.where(row == 15 * i, lines[k, i : i + 1, :], 0.0)
            new = res[pl.ds(at, 16), :] + (pc + qc) * beside
            p[k, to : to + 16, :] = pc
            q[k, to : to + 16, :] = qc
            u[k, to : to + 16, :] = new
            w[k, to : to + 16, :] = pc * new
            store_split(split, rows, at, new, pc * new)
        for ghost, cell in ((7, 8), (40, 39)):
            w[k, ghost : ghost + 1, :] = p[k, cell : cell + 1, :] * u[k, ghost : ghost + 1, :]

    near = near_sum[...]
    for n in range(4):
        sum_two(split, sums, near, rows, n)

    @pl.loop(0, boxes)
    def _(k):
        for i in range(2):
            at, to = pl.multiple_of(S * k + 16 * i, 16), base + 16 * i
            here, low, high = (slice(to + m, to + m + 16) for m in (0, -1, 1))
            sum_u, sum_w = (
                sums[pl.ds(pl.multiple_of(n * rows + at, 16), 16), :] + (ref[k, low, :] + ref[k, high, :])
                for n, ref in enumerate((u, w))
            )
            pc, qc = p[k, here, :], q[k, here, :]
            beside = ghosts[pl.ds(pl.multiple_of(rows + at, 16), 16), :]
            new = (keep[pl.ds(at, 16), :] * u[k, here, :] + (qc * sum_u + sum_w)) + (pc + qc) * beside
            res[pl.ds(at, 16), :] = new
            store_split(split, rows, at, new)

    out_copy = pltpu.make_async_copy(res, out_any, out_sems.at[0])
    out_copy.start()
    inner = slice(LANES, LANES + wide)
    blocks = block_sum[...]
    total = product(split[0:rows, inner], blocks) + product(split[rows : 2 * rows, inner], blocks)
    for half in range(2):
        means[half, :, :] = total[:, LANES * half : LANES * (half + 1)]
    for half in range(2):
        for k in range(boxes):
            for t in range(2):
                at = S * k + 16 * t
                pair = means[half, pl.ds(at, 8, 2), :] + means[half, pl.ds(at + 1, 8, 2), :]
                avg_ref[k, 8 * t : 8 * t + 8, LANES * half : LANES * (half + 1)] = 0.125 * pair
    out_copy.wait()


def join_kernel(*refs):
    *pieces, out_ref = refs
    count = pieces[0].shape[0]
    for n, piece in enumerate(pieces):
        out_ref[n * count : (n + 1) * count] = piece[...]


def put_average(ref, slot, octant, out_ref):
    lanes = lane_ids()
    start, oy, oz = octant // 8 * S + (octant >> 2) % 2 * H, (octant >> 1) % 2, octant % 2
    here = ((lanes >> 4) & 1) == oz
    for t in range(2):
        at = start + 8 * t
        for s in range(4):
            lane = oy * (S * H) + LANES * s
            half = s // 2
            tile = ref[slot, 8 * t : 8 * t + 8, LANES * half : LANES * (half + 1)]
            moved = gather_lanes(tile, (s % 2) * 64 + (lanes >> 5) * H + (lanes & (H - 1)))
            out_ref[at : at + 8, lane : lane + LANES] = jnp.where(here, moved, out_ref[at : at + 8, lane : lane + LANES])


def merge_own_kernel(covers, mid_ref, fixed, own, out_ref):
    rows = out_ref.shape[0]
    count = own.shape[0]

    @pl.loop(1, rows // 8 - 1)
    def _(i):
        at = pl.multiple_of(i * 8, 8)
        out_ref[pl.ds(at, 8), :] = mid_ref[pl.ds(at, 8), :]

    out_ref[0:8, :] = fixed[0:8, :]
    out_ref[rows - 8 : rows, :] = fixed[8:16, :]
    for octant in range(OCTANTS * (rows // S)):
        slot = covers[octant] - count

        @pl.when(jnp.logical_and(slot >= 0, slot < count))
        def _():
            put_average(own, slot, octant, out_ref)


def merge_far_kernel(covers, held_any, near_any, far_any, out_any, held, both, in_sems, out_sems, sems):
    rows = held.shape[0]
    count = both.shape[0] // 2
    _, _, _, odd = sides()

    def rows_of(ref, box):
        return ref.at[box * S : (box + 1) * S, :]

    pieces = [
        pltpu.make_async_copy(ref, both.at[n * count : (n + 1) * count], sems.at[n])
        for n, ref in enumerate((near_any, far_any))
    ]
    loads = [
        pltpu.make_async_copy(rows_of(held_any, box), rows_of(held, box), in_sems.at[box]) for box in range(rows // S)
    ]
    stores = [
        pltpu.make_async_copy(rows_of(held, box), rows_of(out_any, box), out_sems.at[box]) for box in range(rows // S)
    ]
    for copy in pieces + loads:
        copy.start()
    for copy in pieces:
        copy.wait()
    for box in range(rows // S):
        loads[box].wait()
        for octant in range(OCTANTS * box, OCTANTS * (box + 1)):
            place = covers[octant]
            is_next = (place >= 2 * count).astype(jnp.int32)
            is_far = jnp.where(odd == 1, is_next, 1 - is_next)
            slot = place - 2 * count * is_next + count * is_far

            @pl.when(jnp.logical_and(place >= 0, jnp.logical_or(place < count, is_next == 1)))
            def _():
                put_average(both, slot, octant, held)

        stores[box].start()
    for copy in stores:
        copy.wait()


def params():
    return pltpu.CompilerParams(vmem_limit_bytes=VMEM_LIMIT)


def cost(flops, size):
    return pl.CostEstimate(flops=flops, bytes_accessed=size, transcendentals=0)


def f32(*shape):
    return jax.ShapeDtypeStruct(shape, jnp.float32)


def vmem(*shape):
    return pltpu.VMEM(shape, jnp.float32)


def bf16(*shape):
    return pltpu.VMEM(shape, jnp.bfloat16)


def whole():
    return pl.BlockSpec(memory_space=pltpu.VMEM)


def on_device(coarse_dens, coarse_diff, coarse_pot, fine_dens, fine_diff, fine_pot, parents):
    devices = lax.axis_size("dev")
    groups = lax.axis_size("group")
    rows = coarse_dens.shape[0]
    boxes = fine_dens.shape[0] // S
    fine_rows = boxes * S
    octants = OCTANTS * (rows // S)
    wide = S * S
    smem = pl.BlockSpec(memory_space=pltpu.SMEM)
    anywhere = pl.BlockSpec(memory_space=pl.ANY)
    dma = pltpu.SemaphoreType.DMA
    near_pairs = [(i, i ^ 1) for i in range(devices)]
    far_pairs = [(i, (i + devices - 1 + 2 * (i & 1)) % devices) for i in range(devices)]

    def swap(near, far):
        got_far = lax.ppermute(far, "dev", far_pairs)
        return lax.ppermute(near, "dev", near_pairs), got_far

    near_edge, far_edge = pl.pallas_call(
        edges_kernel,
        grid=(1,),
        in_specs=[
            pl.BlockSpec((8, wide), lambda i: (0, 0)),
            pl.BlockSpec((16, wide), lambda i: (0, 0)),
            pl.BlockSpec((16, wide), lambda i: (0, 0)),
            pl.BlockSpec((8, wide), lambda i: (rows // 8 - 1, 0)),
            pl.BlockSpec((16, wide), lambda i: (rows // 16 - 1, 0)),
            pl.BlockSpec((16, wide), lambda i: (rows // 16 - 1, 0)),
        ],
        out_specs=[pl.BlockSpec((8, wide), lambda i: (0, 0))] * 2,
        out_shape=[f32(8, wide)] * 2,
        name="edges",
    )(coarse_dens, coarse_diff, coarse_pot, coarse_dens, coarse_diff, coarse_pot)
    near_edge, far_edge = swap(near_edge, far_edge)

    near_sum = neighbour_matrix()
    mid, covers = pl.pallas_call(
        functools.partial(coarse_kernel, boxes=boxes),
        grid_spec=pltpu.PrefetchScalarGridSpec(
            num_scalar_prefetch=1,
            grid=(),
            in_specs=[anywhere] * 3 + [whole()],
            out_specs=[whole(), smem],
            scratch_shapes=[vmem(rows + 16, wide)] * 3
            + [bf16(2 * rows, wide + 2 * LANES), bf16(4 * rows, wide + 2 * LANES), vmem(3 * rows, wide), dma((3,))],
        ),
        out_shape=[f32(rows, wide), jax.ShapeDtypeStruct((octants + 1,), jnp.int32)],
        compiler_params=params(),
        cost_estimate=cost(rows * wide * 40, rows * wide * 12),
        name="coarse",
    )(parents, coarse_dens, coarse_diff, coarse_pot, near_sum)

    packs = f32(boxes, PACK, LANES)
    top = pl.BlockSpec((16, wide), lambda i, ids: (0, 0))
    bottom = pl.BlockSpec((16, wide), lambda i, ids: (rows // 16 - 1, 0))
    edge = pl.BlockSpec((8, wide), lambda i, ids: (0, 0))
    pack = pl.BlockSpec((boxes, PACK, LANES), lambda i, ids: (0, 0, 0))
    to_near, own, to_far, fixed = pl.pallas_call(
        functools.partial(rims_kernel, boxes=boxes),
        grid_spec=pltpu.PrefetchScalarGridSpec(
            num_scalar_prefetch=1,
            grid=(1,),
            in_specs=[anywhere, anywhere, top, top, bottom, bottom, edge, edge],
            out_specs=[pack, pack, pack, pl.BlockSpec((16, wide), lambda i, ids: (0, 0))],
            scratch_shapes=[vmem(rows + 32, wide)] * 2 + [vmem(3, 24, wide), vmem(8, S * H), dma((2,))],
        ),
        out_shape=[packs, packs, packs, f32(16, wide)],
        compiler_params=params(),
        cost_estimate=cost(rows * wide * 8, rows * wide * 8),
        name="rims",
    )(parents, coarse_dens, mid, coarse_diff, coarse_pot, coarse_diff, coarse_pot, near_edge, far_edge)
    from_near, from_far = swap(to_near, to_far)

    fine_first, keep = pl.pallas_call(
        functools.partial(fine_first_kernel, boxes=boxes),
        in_specs=[anywhere] * 3 + [whole()],
        out_specs=[whole()] * 2,
        scratch_shapes=[vmem(boxes, 48, wide)] * 4
        + [
            bf16(2 * fine_rows, wide + 2 * LANES),
            bf16(4 * fine_rows, wide + 2 * LANES),
            vmem(3 * fine_rows, wide),
            dma((3,)),
        ],
        out_shape=[f32(fine_rows, wide)] * 2,
        compiler_params=params(),
        cost_estimate=cost(fine_rows * wide * 40, fine_rows * wide * 16),
        name="fine_first",
    )(fine_dens, fine_diff, fine_pot, near_sum)

    fine_out, averages = pl.pallas_call(
        functools.partial(fine_second_kernel, boxes=boxes, octants=octants),
        grid_spec=pltpu.PrefetchScalarGridSpec(
            num_scalar_prefetch=1,
            grid=(),
            in_specs=[anywhere] * 4 + [whole()] * 6,
            out_specs=[anywhere, whole()],
            scratch_shapes=[vmem(boxes, 48, wide)] * 4
            + [
                vmem(boxes, 8, wide),
                bf16(2 * fine_rows, wide + 2 * LANES),
                bf16(4 * fine_rows, wide + 2 * LANES),
                vmem(2 * fine_rows, wide),
                vmem(2 * fine_rows, wide),
                bf16(2 * fine_rows, LANES),
                vmem(fine_rows, LANES),
                vmem(fine_rows, wide),
                vmem(fine_rows, wide),
                vmem(2, fine_rows, LANES),
                dma((4,)),
                dma((1,)),
            ],
        ),
        out_shape=[f32(fine_rows, wide), f32(boxes, H, H * H)],
        compiler_params=params(),
        cost_estimate=cost(fine_rows * wide * 60, fine_rows * wide * 16),
        name="fine_second",
    )(
        parents,
        fine_first,
        keep,
        fine_diff,
        fine_pot,
        near_sum,
        ghost_matrices(),
        average_matrix(),
        from_near,
        own,
        from_far,
    )

    pieces = [averages]
    for s in range(1, groups):
        pieces.append(lax.ppermute(averages, "group", [(i, (i + s) % groups) for i in range(groups)]))
    joined = pl.pallas_call(
        join_kernel,
        in_specs=[whole()] * groups,
        out_specs=whole(),
        out_shape=f32(groups * boxes, H, H * H),
        compiler_params=params(),
        name="join",
    )(*pieces)
    near_avg, far_avg = swap(joined, joined)

    def merge(kernel, in_specs, out_spec, scratch, name):
        return pl.pallas_call(
            kernel,
            grid_spec=pltpu.PrefetchScalarGridSpec(
                num_scalar_prefetch=1, grid=(), in_specs=in_specs, out_specs=out_spec, scratch_shapes=scratch
            ),
            out_shape=f32(rows, wide),
            compiler_params=params(),
            cost_estimate=cost(rows * wide * 4, rows * wide * 12),
            name=name,
        )

    merged = merge(merge_own_kernel, [whole()] * 3, whole(), [], "merge_own")(covers, mid, fixed, joined)
    scratch = [vmem(rows, wide), vmem(2 * groups * boxes, H, H * H), dma((rows // S,)), dma((rows // S,)), dma((2,))]
    coarse_out = merge(merge_far_kernel, [anywhere] * 3, anywhere, scratch, "merge_far")(
        covers, merged, near_avg, far_avg
    )
    return coarse_out, fine_out


def solution(mesh):
    in_specs = (
        P("dev", None),
        P("dev", None),
        P("dev", None),
        P(("group", "dev"), None),
        P(("group", "dev"), None),
        P(("group", "dev"), None),
        P(),
    )
    out_specs = (P("dev", None), P(("group", "dev"), None))
    return jax.shard_map(on_device, mesh=mesh, in_specs=in_specs, out_specs=out_specs, check_vma=False)
```

```python
import functools

import jax
import jax.numpy as jnp
import numpy as np
from jax import lax
from jax.experimental import pallas as pl
from jax.experimental.pallas import tpu as pltpu
from jax.sharding import PartitionSpec as P

S = 32
H = 16
LANES = 128
GROUPS = 8
OCTANTS = 8
PACK = 24
RATE = 0.06
VMEM_LIMIT = 32 * 1024 * 1024


def neighbour_matrix():
    source, target = np.arange(512)[:, None] - LANES, np.arange(256)[None, :]
    step = source - target
    same_y = source // S == target // S
    return jnp.asarray((np.abs(step) == S) | ((np.abs(step) == 1) & same_y), jnp.bfloat16)


def ghost_matrices():
    source, target = np.arange(LANES)[:, None], np.arange(S * S)[None, :]
    part, place = (source >> 4) & 3, source & (H - 1)
    y, z = target // S, target % S
    faces = (
        ((part == 0) & (z == S - 1) & (y // 2 == place))
        | ((part == 1) & (z == 0) & (y // 2 == place))
        | ((part == 2) & (y == S - 1) & (z // 2 == place))
        | ((part == 3) & (y == 0) & (z // 2 == place))
    )
    return jnp.asarray(np.stack([faces & (source // 64 == step) for step in range(2)]), jnp.bfloat16)


def average_matrix():
    source, target = np.arange(S * S)[:, None], np.arange(H * H)[None, :]
    return jnp.asarray((source // S // 2 == target // H) & (source % S // 2 == target % H), jnp.bfloat16)


def pieces_of(value):
    high = value.astype(jnp.bfloat16)
    return high, (value - high.astype(jnp.float32)).astype(jnp.bfloat16)


def windows():
    for n in range(4):
        low, high = max(256 * n - LANES, 0), min(256 * n + 256 + LANES, S * S)
        first = low - (256 * n - LANES)
        yield slice(low, high), slice(first, first + high - low), slice(256 * n, 256 * n + 256)


def product(left, right):
    return jnp.dot(left, right, preferred_element_type=jnp.float32)


def sides():
    dev, devices = lax.axis_index("dev"), lax.axis_size("dev")
    odd = dev & 1
    near = dev + 1 - 2 * odd
    far = lax.rem(dev + devices - 1 + 2 * odd, devices)
    return dev, near, far, odd


def edge_count():
    lane = lax.broadcasted_iota(jnp.int32, (1, S * S), 1)
    z, y = lane & (S - 1), lane >> 5
    return sum((at == end).astype(jnp.float32) for at in (z, y) for end in (0, S - 1))


def lane_ids():
    return lax.broadcasted_iota(jnp.int32, (8, LANES), 1)


def row_ids():
    return lax.broadcasted_iota(jnp.int32, (8, LANES), 0)


def gather_lanes(tile, index):
    return jnp.take_along_axis(tile, index, axis=1, mode="promise_in_bounds")


def lane_groups(ref, row):
    return [ref[row : row + 8, LANES * j : LANES * (j + 1)] for j in range(GROUPS)]


def sum_yz(tiles, lanes, edge):
    z = lanes & (S - 1)
    up = [pltpu.roll(t, S, 1) for t in tiles]
    down = [pltpu.roll(t, LANES - S, 1) for t in tiles]
    out = []
    for j, tile in enumerate(tiles):
        fill = tile if edge else jnp.zeros_like(tile)
        low = jnp.where(lanes >= S, up[j], up[j - 1] if j > 0 else fill)
        high = jnp.where(lanes < LANES - S, down[j], down[j + 1] if j + 1 < GROUPS else fill)
        left = jnp.where(z != 0, pltpu.roll(tile, 1, 1), fill)
        right = jnp.where(z != S - 1, pltpu.roll(tile, LANES - 1, 1), fill)
        out.append((low + high) + (left + right))
    return out


def octant_place(local_id):
    box = local_id >> 3
    return box * S + ((local_id >> 2) & 1) * H, (local_id >> 1) & 1, local_id & 1


def edges_kernel(u0, k0, v0, u1, k1, v1, near_ref, far_ref):
    _, _, _, odd = sides()
    first = (u0[0:2, :], k0[...].astype(jnp.float32)[0:2, :], v0[...].astype(jnp.float32)[0:2, :])
    last = (u1[6:8, :], k1[...].astype(jnp.float32)[14:16, :], v1[...].astype(jnp.float32)[14:16, :])
    is_odd = odd == 1
    for n, (low, high) in enumerate(zip(first, last)):
        near_ref[2 * n : 2 * n + 2, :] = jnp.where(is_odd, low, high)
        far_ref[2 * n : 2 * n + 2, :] = jnp.where(is_odd, high, low)
    for ref in (near_ref, far_ref):
        ref[6:8, :] = jnp.zeros((2, S * S), jnp.float32)


def pack_rims(old, mid, xs, pack_ref, slot, local_id, base):
    lanes, rows = lane_ids(), row_ids()
    start, oy, oz = octant_place(local_id)
    start = start + base
    half = pl.multiple_of(oy * (S * H), LANES)
    for n, (ref, shift, row) in enumerate(((old, -8, 7), (old, H, 0), (mid, -8, 7), (mid, H, 0))):
        tile = ref[pl.ds(pl.multiple_of(start + shift, 8), 8), pl.ds(half, S * H)]
        line = tile[row : row + 1, :]
        xs[n : n + 1, :] = line
        xs[n + 4 : n + 5, :] = line
    index_x = ((lanes >> 4) & 3) * S + oz * H + (lanes & (H - 1))
    picked = [gather_lanes(xs[:, LANES * s : LANES * (s + 1)], index_x) for s in range(4)]
    low = jnp.where(lanes < 64, picked[0], picked[1])
    high = jnp.where(lanes < 64, picked[2], picked[3])
    faces = jnp.where(rows < 4, low, high)
    mean = 0.5 * (faces + pltpu.roll(faces, 2, 0))
    pack_ref[slot, 0:8, :] = jnp.where((rows & 2) == 0, faces, mean)
    index_y = oy * (LANES - S) + oz * H + (lanes & (H - 1))
    index_z = (lanes & 3) * S + H - oz
    y_group = pl.multiple_of(S * H - LANES * oy, LANES)
    for t in range(2):
        at = pl.multiple_of(start + 8 * t, 8)
        values = []
        for ref in (old, mid):
            y_face = gather_lanes(ref[pl.ds(at, 8), pl.ds(y_group, LANES)], index_y)
            parts = [
                gather_lanes(ref[pl.ds(at, 8), pl.ds(pl.multiple_of(half + LANES * s, LANES), LANES)], index_z)
                for s in range(4)
            ]
            which = (lanes >> 2) & 3
            z_face = jnp.where(
                which < 2,
                jnp.where(which == 0, parts[0], parts[1]),
                jnp.where(which == 2, parts[2], parts[3]),
            )
            values.append(jnp.where((lanes & S) == 0, z_face, y_face))
        face = jnp.where(lanes < 64, values[0], 0.5 * (values[0] + values[1]))
        used = ((lanes >> 4) & 1) == jnp.where((lanes & S) == 0, oz, oy)
        pack_ref[slot, 8 + 8 * t : 16 + 8 * t, :] = jnp.where(used, face, 0.0)


def find_boxes(parents, covers, boxes, octants):
    dev, devices = lax.axis_index("dev"), lax.axis_size("dev")
    group, groups = lax.axis_index("group"), lax.axis_size("group")
    for n in range(octants + 1):
        covers[n] = jnp.int32(-1)
    for r in range(3):
        source = lax.rem(dev + devices + r - 1, devices)
        for s in range(groups):
            first = (lax.rem(group + groups - s, groups) * devices + source) * boxes
            for k in range(boxes):
                local_id = parents[first + k] - dev * octants
                inside = jnp.logical_and(local_id >= 0, local_id < octants)
                covers[jnp.where(inside, local_id, octants)] = jnp.int32((r * groups + s) * boxes + k)


def step_tile(uc, pc, qc, ul, pll, ql, uh, ph, qh, lanes):
    sum_u = sum_yz(uc, lanes, False)
    sum_w = sum_yz([a * b for a, b in zip(pc, uc)], lanes, False)
    sum_q = sum_yz(qc, lanes, True)
    out = []
    for j in range(GROUPS):
        keep = (1.0 - 6.0 * pc[j]) - (sum_q[j] + (ql[j] + qh[j]))
        near_u = sum_u[j] + (ul[j] + uh[j])
        near_w = sum_w[j] + (pll[j] * ul[j] + ph[j] * uh[j])
        out.append(keep * uc[j] + (qc[j] * near_u + near_w))
    return out


def coarse_kernel(parents, u_ref, k_ref, v_ref, near_sum, mid_out, covers, u, p, q, split, sums, *, boxes):
    rows, wide = mid_out.shape
    base = 8
    rate = 0.5 * RATE
    for ref in (u, p, q):
        for row in (0, base + rows):
            ref[row : row + 8, :] = jnp.zeros((8, wide), jnp.float32)
    find_boxes(parents, covers, boxes, OCTANTS * (rows // S))

    @pl.loop(0, rows // 16)
    def _(i):
        at = pl.multiple_of(i * 16, 16)
        to = pl.multiple_of(base + i * 16, 8)
        diff = rate * k_ref[pl.ds(at, 16), :].astype(jnp.float32)
        pot = rate * v_ref[pl.ds(at, 16), :].astype(jnp.float32)
        dens = u_ref[pl.ds(at, 16), :]
        u[pl.ds(to, 16), :] = dens
        p[pl.ds(to, 16), :] = diff + pot
        q[pl.ds(to, 16), :] = diff - pot
        store_split(split, rows, at, dens, (diff + pot) * dens)

    for window, part, out in windows():
        near = near_sum[part, :]
        sums[0:rows, out] = rate * (product(k_ref[:, window], near) - product(v_ref[:, window], near))
        sum_two(split, sums, near, rows, window, out, rows)

    ends = edge_count()

    @pl.loop(0, rows // 8)
    def _(i):
        at = pl.multiple_of(i * 8, 8)
        uv, pv, qv = (ref.at[pl.ds(at, 24), :] for ref in (u, p, q))
        sum_q, sum_u, sum_w = (sums[pl.ds(pl.multiple_of(n * rows + at, 8), 8), :] for n in range(3))
        uc, pc, qc = (view[8:16, :] for view in (uv, pv, qv))
        ul, uh = uv[7:15, :], uv[9:17, :]
        keep = (1.0 - 6.0 * pc) - (sum_q + ends * qc + (qv[7:15, :] + qv[9:17, :]))
        near_u = sum_u + (ul + uh)
        near_w = sum_w + (pv[7:15, :] * ul + pv[9:17, :] * uh)
        mid_out[pl.ds(at, 8), :] = keep * uc + (qc * near_u + near_w)


def rims_kernel(parents, u_any, mid_any, k_first, v_first, k_last, v_last, near_edge, far_edge, to_near, to_own, to_far, fixed, u, m, e, xs, sems, *, boxes):
    rows = u_any.shape[0]
    base = 16
    rate = 0.5 * RATE
    devices = lax.axis_size("dev")
    dev, near_dev, far_dev, odd = sides()
    group = lax.axis_index("group")
    octants = OCTANTS * (rows // S)
    copies = [
        pltpu.make_async_copy(u_any, u.at[pl.ds(base, rows), :], sems.at[0]),
        pltpu.make_async_copy(mid_any, m.at[pl.ds(base, rows), :], sems.at[1]),
    ]
    for copy in copies:
        copy.start()
    lanes = lane_ids()
    for copy in copies:
        copy.wait()
    before = jnp.where(odd == 1, near_edge[...], far_edge[...])
    after = jnp.where(odd == 1, far_edge[...], near_edge[...])
    u[base - 2 : base, :] = before[0:2, :]
    u[base + rows : base + rows + 2, :] = after[0:2, :]
    for n, (far, k_ref, v_ref, own, top) in enumerate(
        ((before, k_first, v_first, 0, base - 2), (after, k_last, v_last, 14, base + rows - 2))
    ):
        e[0, 7:11, :] = u[top : top + 4, :]
        own_diff = rate * k_ref[...].astype(jnp.float32)[own : own + 2, :]
        own_pot = rate * v_ref[...].astype(jnp.float32)[own : own + 2, :]
        far_diff, far_pot = rate * far[2:4, :], rate * far[4:6, :]
        there, here = (7, 9) if n == 0 else (9, 7)
        e[1, there : there + 2, :] = far_diff + far_pot
        e[2, there : there + 2, :] = far_diff - far_pot
        e[1, here : here + 2, :] = own_diff + own_pot
        e[2, here : here + 2, :] = own_diff - own_pot
        tiles = [lane_groups(e.at[f], row) for row in (8, 7, 9) for f in range(3)]
        for j, new in enumerate(step_tile(*tiles, lanes)):
            m[top + 1 : top + 3, LANES * j : LANES * (j + 1)] = new[0:2, :]
    fixed[0:8, :] = m[base : base + 8, :]
    fixed[8:16, :] = m[base + rows - 8 : base + rows, :]

    for ref, target in ((to_far, far_dev), (to_near, near_dev), (to_own, dev)):
        for k in range(boxes):
            local_id = parents[(group * devices + target) * boxes + k] - dev * octants
            local_id = jnp.minimum(jnp.maximum(local_id, 0), octants - 1)
            pack_rims(u, m, xs, ref, k, local_id, base)


def fine_rates(k_ref, v_ref, at):
    diff = RATE * k_ref[pl.ds(at, 16), :].astype(jnp.float32)
    pot = (0.5 * RATE) * v_ref[pl.ds(at, 16), :].astype(jnp.float32)
    return diff + pot, diff - pot


def store_split(split, rows, at, *values):
    parts = [part for value in values for part in pieces_of(value)]
    for n, part in enumerate(parts):
        split[pl.ds(pl.multiple_of(n * rows + at, 16), 16), :] = part


def sum_two(split, sums, near, rows, window, out, first=0):
    for f in range(2):
        high, low = (split[(2 * f + h) * rows : (2 * f + h + 1) * rows, window] for h in range(2))
        sums[first + f * rows : first + (f + 1) * rows, out] = product(high, near) + product(low, near)


def fine_first_kernel(u_ref, k_ref, v_ref, near_sum, out_ref, keep_ref, u, w, p, q, split, sums, *, boxes):
    rows, wide = out_ref.shape
    base = 8
    @pl.loop(0, boxes)
    def _(k):
        for ref in (u, w):
            for ghost in (7, 40):
                ref[k, ghost : ghost + 1, :] = jnp.zeros((1, wide), jnp.float32)
        for i in range(2):
            at, to = pl.multiple_of(S * k + 16 * i, 16), base + 16 * i
            pc, qc = fine_rates(k_ref, v_ref, at)
            dens = u_ref[pl.ds(at, 16), :]
            p[k, to : to + 16, :] = pc
            q[k, to : to + 16, :] = qc
            u[k, to : to + 16, :] = dens
            w[k, to : to + 16, :] = pc * dens
            store_split(split, rows, at, dens, pc * dens)
        for ghost, cell in ((7, 8), (40, 39)):
            q[k, ghost : ghost + 1, :] = q[k, cell : cell + 1, :]

    for window, part, out in windows():
        near = near_sum[part, :]
        sum_two(split, sums, near, rows, window, out)
        sums[2 * rows : 3 * rows, out] = RATE * product(k_ref[:, window], near) - (0.5 * RATE) * product(
            v_ref[:, window], near
        )
    ends = edge_count()

    @pl.loop(0, boxes)
    def _(k):
        for i in range(2):
            at, to = pl.multiple_of(S * k + 16 * i, 16), base + 16 * i
            here, low, high = (slice(to + m, to + m + 16) for m in (0, -1, 1))
            sum_u, sum_w, sum_q = (
                sums[pl.ds(pl.multiple_of(n * rows + at, 16), 16), :] + (ref[k, low, :] + ref[k, high, :])
                for n, ref in enumerate((u, w, q))
            )
            qc = q[k, here, :]
            stay = (1.0 - 6.0 * p[k, here, :]) - (sum_q + ends * qc)
            keep_ref[pl.ds(at, 16), :] = stay
            out_ref[pl.ds(at, 16), :] = stay * u[k, here, :] + (qc * sum_u + sum_w)


def fine_second_kernel(parents, first, keep, k_ref, v_ref, near_sum, ghost_sum, block_sum, from_near, from_own, from_far, out_any, avg_ref, u, w, p, q, lines, split, sums, ghosts, faces, dup, res, means, out_sems, *, boxes, octants):
    devices = lax.axis_size("dev")
    dev, near_dev, _, _ = sides()
    group = lax.axis_index("group")
    rows, wide = res.shape
    base = 8
    lanes = lane_ids()
    z = lanes & (S - 1)
    for k in range(boxes):
        parent = parents[(group * devices + dev) * boxes + k]
        own_id, near_id = parent - dev * octants, parent - near_dev * octants
        is_own = jnp.logical_and(own_id >= 0, own_id < octants)
        is_near = jnp.logical_and(near_id >= 0, near_id < octants)

        def chosen(n):
            there = slice(8 * n, 8 * n + 8)
            other = jnp.where(is_near, from_near[k, there, :], from_far[k, there, :])
            return jnp.where(is_own, from_own[k, there, :], other)

        for n in range(2):
            face = chosen(n + 1)
            dup[pl.ds(S * k + 16 * n, 8, 2), :] = face
            dup[pl.ds(S * k + 16 * n + 1, 8, 2), :] = face
        for n, part in enumerate(pieces_of(dup[S * k : S * k + S, :])):
            faces[n * rows + S * k : n * rows + S * k + S, :] = part
        x_faces = chosen(0)
        for n in range(4):
            spread = gather_lanes(x_faces, (2 * n + (lanes >> 6)) * H + (z >> 1))
            for half in range(2):
                j = 4 * half + n
                there = slice(LANES * j, LANES * (j + 1))
                lines[k, 0:2, there] = spread[4 * half : 4 * half + 2, :]
                u[k, 7:8, there] = spread[4 * half + 2 : 4 * half + 3, :]
                u[k, 40:41, there] = spread[4 * half + 3 : 4 * half + 4, :]
    for n in range(4):
        out = slice(256 * n, 256 * n + 256)
        for step in range(2):
            matrix = ghost_sum[step, :, out]
            ghosts[step * rows : (step + 1) * rows, out] = product(faces[0:rows, :], matrix) + product(
                faces[rows : 2 * rows, :], matrix
            )
    row = lax.broadcasted_iota(jnp.int32, (16, wide), 0)

    @pl.loop(0, boxes)
    def _(k):
        for i in range(2):
            at, to = pl.multiple_of(S * k + 16 * i, 16), base + 16 * i
            pc, qc = fine_rates(k_ref, v_ref, at)
            beside = ghosts[pl.ds(at, 16), :] + jnp.where(row == 15 * i, lines[k, i : i + 1, :], 0.0)
            new = first[pl.ds(at, 16), :] + (pc + qc) * beside
            p[k, to : to + 16, :] = pc
            q[k, to : to + 16, :] = qc
            u[k, to : to + 16, :] = new
            w[k, to : to + 16, :] = pc * new
            store_split(split, rows, at, new, pc * new)
        for ghost, cell in ((7, 8), (40, 39)):
            w[k, ghost : ghost + 1, :] = p[k, cell : cell + 1, :] * u[k, ghost : ghost + 1, :]

    for window, part, out in windows():
        sum_two(split, sums, near_sum[part, :], rows, window, out)

    @pl.loop(0, boxes)
    def _(k):
        for i in range(2):
            at, to = pl.multiple_of(S * k + 16 * i, 16), base + 16 * i
            here, low, high = (slice(to + m, to + m + 16) for m in (0, -1, 1))
            sum_u, sum_w = (
                sums[pl.ds(pl.multiple_of(n * rows + at, 16), 16), :] + (ref[k, low, :] + ref[k, high, :])
                for n, ref in enumerate((u, w))
            )
            pc, qc = p[k, here, :], q[k, here, :]
            beside = ghosts[pl.ds(pl.multiple_of(rows + at, 16), 16), :]
            new = (keep[pl.ds(at, 16), :] * u[k, here, :] + (qc * sum_u + sum_w)) + (pc + qc) * beside
            res[pl.ds(at, 16), :] = new
            store_split(split, rows, at, new)

    out_copy = pltpu.make_async_copy(res, out_any, out_sems.at[0])
    out_copy.start()
    blocks = block_sum[...]
    total = product(split[0:rows, :], blocks) + product(split[rows : 2 * rows, :], blocks)
    for half in range(2):
        means[half, :, :] = total[:, LANES * half : LANES * (half + 1)]
    for half in range(2):
        for k in range(boxes):
            for t in range(2):
                at = S * k + 16 * t
                pair = means[half, pl.ds(at, 8, 2), :] + means[half, pl.ds(at + 1, 8, 2), :]
                avg_ref[k, 8 * t : 8 * t + 8, LANES * half : LANES * (half + 1)] = 0.125 * pair
    out_copy.wait()


def join_kernel(*refs):
    *pieces, out_ref = refs
    count = pieces[0].shape[0]
    for n, piece in enumerate(pieces):
        out_ref[n * count : (n + 1) * count] = piece[...]


def put_average(ref, slot, octant, out_ref):
    lanes = lane_ids()
    start, oy, oz = octant // 8 * S + (octant >> 2) % 2 * H, (octant >> 1) % 2, octant % 2
    here = ((lanes >> 4) & 1) == oz
    for t in range(2):
        at = start + 8 * t
        for s in range(4):
            lane = oy * (S * H) + LANES * s
            half = s // 2
            tile = ref[slot, 8 * t : 8 * t + 8, LANES * half : LANES * (half + 1)]
            moved = gather_lanes(tile, (s % 2) * 64 + (lanes >> 5) * H + (lanes & (H - 1)))
            out_ref[at : at + 8, lane : lane + LANES] = jnp.where(here, moved, out_ref[at : at + 8, lane : lane + LANES])


def merge_own_kernel(covers, mid_ref, fixed, own, out_ref):
    rows = out_ref.shape[0]
    count = own.shape[0]

    @pl.loop(1, rows // 8 - 1)
    def _(i):
        at = pl.multiple_of(i * 8, 8)
        out_ref[pl.ds(at, 8), :] = mid_ref[pl.ds(at, 8), :]

    out_ref[0:8, :] = fixed[0:8, :]
    out_ref[rows - 8 : rows, :] = fixed[8:16, :]
    for octant in range(OCTANTS * (rows // S)):
        slot = covers[octant] - count

        @pl.when(jnp.logical_and(slot >= 0, slot < count))
        def _():
            put_average(own, slot, octant, out_ref)


def merge_far_kernel(covers, held, near_ref, far_ref, out_any, made, out_sems):
    rows = held.shape[0]
    count = near_ref.shape[0]
    _, _, _, odd = sides()
    near_first, far_first = 2 * count * (1 - odd), 2 * count * odd
    stores = []
    for box in range(rows // S):
        there = slice(box * S, (box + 1) * S)
        made[there, :] = held[there, :]
        for octant in range(OCTANTS * box, OCTANTS * (box + 1)):
            for ref, first in ((near_ref, near_first), (far_ref, far_first)):
                slot = covers[octant] - first

                @pl.when(jnp.logical_and(slot >= 0, slot < count))
                def _():
                    put_average(ref, slot, octant, made)

        stores.append(pltpu.make_async_copy(made.at[there, :], out_any.at[there, :], out_sems.at[box]))
        stores[-1].start()
    for copy in stores:
        copy.wait()


def params():
    return pltpu.CompilerParams(vmem_limit_bytes=VMEM_LIMIT)


def cost(flops, size):
    return pl.CostEstimate(flops=flops, bytes_accessed=size, transcendentals=0)


def f32(*shape):
    return jax.ShapeDtypeStruct(shape, jnp.float32)


def vmem(*shape):
    return pltpu.VMEM(shape, jnp.float32)


def bf16(*shape):
    return pltpu.VMEM(shape, jnp.bfloat16)


def whole():
    return pl.BlockSpec(memory_space=pltpu.VMEM)


def on_device(coarse_dens, coarse_diff, coarse_pot, fine_dens, fine_diff, fine_pot, parents):
    devices = lax.axis_size("dev")
    groups = lax.axis_size("group")
    rows = coarse_dens.shape[0]
    boxes = fine_dens.shape[0] // S
    fine_rows = boxes * S
    octants = OCTANTS * (rows // S)
    wide = S * S
    smem = pl.BlockSpec(memory_space=pltpu.SMEM)
    anywhere = pl.BlockSpec(memory_space=pl.ANY)
    dma = pltpu.SemaphoreType.DMA
    near_pairs = [(i, i ^ 1) for i in range(devices)]
    far_pairs = [(i, (i + devices - 1 + 2 * (i & 1)) % devices) for i in range(devices)]

    def swap(near, far):
        got_far = lax.ppermute(far, "dev", far_pairs)
        return lax.ppermute(near, "dev", near_pairs), got_far

    near_edge, far_edge = pl.pallas_call(
        edges_kernel,
        grid=(1,),
        in_specs=[
            pl.BlockSpec((8, wide), lambda i: (0, 0)),
            pl.BlockSpec((16, wide), lambda i: (0, 0)),
            pl.BlockSpec((16, wide), lambda i: (0, 0)),
            pl.BlockSpec((8, wide), lambda i: (rows // 8 - 1, 0)),
            pl.BlockSpec((16, wide), lambda i: (rows // 16 - 1, 0)),
            pl.BlockSpec((16, wide), lambda i: (rows // 16 - 1, 0)),
        ],
        out_specs=[pl.BlockSpec((8, wide), lambda i: (0, 0))] * 2,
        out_shape=[f32(8, wide)] * 2,
        name="edges",
    )(coarse_dens, coarse_diff, coarse_pot, coarse_dens, coarse_diff, coarse_pot)
    near_edge, far_edge = swap(near_edge, far_edge)

    near_sum = neighbour_matrix()
    mid, covers = pl.pallas_call(
        functools.partial(coarse_kernel, boxes=boxes),
        grid_spec=pltpu.PrefetchScalarGridSpec(
            num_scalar_prefetch=1,
            grid=(),
            in_specs=[whole()] * 4,
            out_specs=[whole(), smem],
            scratch_shapes=[vmem(rows + 16, wide)] * 3 + [bf16(4 * rows, wide), vmem(3 * rows, wide)],
        ),
        out_shape=[f32(rows, wide), jax.ShapeDtypeStruct((octants + 1,), jnp.int32)],
        compiler_params=params(),
        cost_estimate=cost(rows * wide * 40, rows * wide * 12),
        name="coarse",
    )(parents, coarse_dens, coarse_diff, coarse_pot, near_sum)

    packs = f32(boxes, PACK, LANES)
    top = pl.BlockSpec((16, wide), lambda i, ids: (0, 0))
    bottom = pl.BlockSpec((16, wide), lambda i, ids: (rows // 16 - 1, 0))
    edge = pl.BlockSpec((8, wide), lambda i, ids: (0, 0))
    pack = pl.BlockSpec((boxes, PACK, LANES), lambda i, ids: (0, 0, 0))
    to_near, own, to_far, fixed = pl.pallas_call(
        functools.partial(rims_kernel, boxes=boxes),
        grid_spec=pltpu.PrefetchScalarGridSpec(
            num_scalar_prefetch=1,
            grid=(1,),
            in_specs=[anywhere, anywhere, top, top, bottom, bottom, edge, edge],
            out_specs=[pack, pack, pack, pl.BlockSpec((16, wide), lambda i, ids: (0, 0))],
            scratch_shapes=[vmem(rows + 32, wide)] * 2 + [vmem(3, 24, wide), vmem(8, S * H), dma((2,))],
        ),
        out_shape=[packs, packs, packs, f32(16, wide)],
        compiler_params=params(),
        cost_estimate=cost(rows * wide * 8, rows * wide * 8),
        name="rims",
    )(parents, coarse_dens, mid, coarse_diff, coarse_pot, coarse_diff, coarse_pot, near_edge, far_edge)
    from_near, from_far = swap(to_near, to_far)

    fine_first, keep = pl.pallas_call(
        functools.partial(fine_first_kernel, boxes=boxes),
        in_specs=[whole()] * 4,
        out_specs=[whole()] * 2,
        scratch_shapes=[vmem(boxes, 48, wide)] * 4 + [bf16(4 * fine_rows, wide), vmem(3 * fine_rows, wide)],
        out_shape=[f32(fine_rows, wide)] * 2,
        compiler_params=params(),
        cost_estimate=cost(fine_rows * wide * 40, fine_rows * wide * 16),
        name="fine_first",
    )(fine_dens, fine_diff, fine_pot, near_sum)

    fine_out, averages = pl.pallas_call(
        functools.partial(fine_second_kernel, boxes=boxes, octants=octants),
        grid_spec=pltpu.PrefetchScalarGridSpec(
            num_scalar_prefetch=1,
            grid=(),
            in_specs=[whole()] * 10,
            out_specs=[anywhere, whole()],
            scratch_shapes=[vmem(boxes, 48, wide)] * 4
            + [
                vmem(boxes, 8, wide),
                bf16(4 * fine_rows, wide),
                vmem(2 * fine_rows, wide),
                vmem(2 * fine_rows, wide),
                bf16(2 * fine_rows, LANES),
                vmem(fine_rows, LANES),
                vmem(fine_rows, wide),
                vmem(2, fine_rows, LANES),
                dma((1,)),
            ],
        ),
        out_shape=[f32(fine_rows, wide), f32(boxes, H, H * H)],
        compiler_params=params(),
        cost_estimate=cost(fine_rows * wide * 60, fine_rows * wide * 16),
        name="fine_second",
    )(
        parents,
        fine_first,
        keep,
        fine_diff,
        fine_pot,
        near_sum,
        ghost_matrices(),
        average_matrix(),
        from_near,
        own,
        from_far,
    )

    pieces = [averages]
    for s in range(1, groups):
        pieces.append(lax.ppermute(averages, "group", [(i, (i + s) % groups) for i in range(groups)]))
    joined = pl.pallas_call(
        join_kernel,
        in_specs=[whole()] * groups,
        out_specs=whole(),
        out_shape=f32(groups * boxes, H, H * H),
        compiler_params=params(),
        name="join",
    )(*pieces)
    near_avg, far_avg = swap(joined, joined)

    def merge(kernel, in_specs, out_spec, scratch, name):
        return pl.pallas_call(
            kernel,
            grid_spec=pltpu.PrefetchScalarGridSpec(
                num_scalar_prefetch=1, grid=(), in_specs=in_specs, out_specs=out_spec, scratch_shapes=scratch
            ),
            out_shape=f32(rows, wide),
            compiler_params=params(),
            cost_estimate=cost(rows * wide * 4, rows * wide * 12),
            name=name,
        )

    merged = merge(merge_own_kernel, [whole()] * 3, whole(), [], "merge_own")(covers, mid, fixed, joined)
    scratch = [vmem(rows, wide), dma((rows // S,))]
    coarse_out = merge(merge_far_kernel, [whole()] * 3, anywhere, scratch, "merge_far")(
        covers, merged, near_avg, far_avg
    )
    return coarse_out, fine_out


def solution(mesh):
    in_specs = (
        P("dev", None),
        P("dev", None),
        P("dev", None),
        P(("group", "dev"), None),
        P(("group", "dev"), None),
        P(("group", "dev"), None),
        P(),
    )
    out_specs = (P("dev", None), P(("group", "dev"), None))
    return jax.shard_map(on_device, mesh=mesh, in_specs=in_specs, out_specs=out_specs, check_vma=False)
```

```python
import functools

import jax
import jax.numpy as jnp
import numpy as np
from jax import lax
from jax.experimental import pallas as pl
from jax.experimental.pallas import tpu as pltpu
from jax.sharding import PartitionSpec as P

S = 32
H = 16
LANES = 128
GROUPS = 8
OCTANTS = 8
MARGIN = 16
PACK = 24
RATE = 0.06
VMEM_LIMIT = 32 * 1024 * 1024


def neighbour_matrix():
    source, target = np.arange(512)[:, None] - LANES, np.arange(256)[None, :]
    step = source - target
    same_y = source // S == target // S
    return jnp.asarray((np.abs(step) == S) | ((np.abs(step) == 1) & same_y), jnp.bfloat16)


def ghost_matrices():
    source, target = np.arange(LANES)[:, None], np.arange(S * S)[None, :]
    part, place = (source >> 4) & 3, source & (H - 1)
    y, z = target // S, target % S
    faces = (
        ((part == 0) & (z == S - 1) & (y // 2 == place))
        | ((part == 1) & (z == 0) & (y // 2 == place))
        | ((part == 2) & (y == S - 1) & (z // 2 == place))
        | ((part == 3) & (y == 0) & (z // 2 == place))
    )
    return jnp.asarray(np.stack([faces & (source // 64 == step) for step in range(2)]), jnp.bfloat16)


def average_matrix():
    source, target = np.arange(S * S)[:, None], np.arange(H * H)[None, :]
    return jnp.asarray((source // S // 2 == target // H) & (source % S // 2 == target % H), jnp.bfloat16)


def pieces_of(value):
    high = value.astype(jnp.bfloat16)
    return high, (value - high.astype(jnp.float32)).astype(jnp.bfloat16)


def windows():
    for n in range(4):
        low, high = max(256 * n - LANES, 0), min(256 * n + 256 + LANES, S * S)
        first = low - (256 * n - LANES)
        yield slice(low, high), slice(first, first + high - low), slice(256 * n, 256 * n + 256)


def product(left, right):
    return jnp.dot(left, right, preferred_element_type=jnp.float32)


def sides():
    dev, devices = lax.axis_index("dev"), lax.axis_size("dev")
    odd = dev & 1
    near = dev + 1 - 2 * odd
    far = lax.rem(dev + devices - 1 + 2 * odd, devices)
    return dev, near, far, odd


def edge_count():
    lane = lax.broadcasted_iota(jnp.int32, (1, S * S), 1)
    z, y = lane & (S - 1), lane >> 5
    return sum((at == end).astype(jnp.float32) for at in (z, y) for end in (0, S - 1))


def lane_ids():
    return lax.broadcasted_iota(jnp.int32, (8, LANES), 1)


def row_ids():
    return lax.broadcasted_iota(jnp.int32, (8, LANES), 0)


def gather_lanes(tile, index):
    return jnp.take_along_axis(tile, index, axis=1, mode="promise_in_bounds")


def lane_groups(ref, row):
    return [ref[row : row + 8, LANES * j : LANES * (j + 1)] for j in range(GROUPS)]


def sum_yz(tiles, lanes, edge):
    z = lanes & (S - 1)
    up = [pltpu.roll(t, S, 1) for t in tiles]
    down = [pltpu.roll(t, LANES - S, 1) for t in tiles]
    out = []
    for j, tile in enumerate(tiles):
        fill = tile if edge else jnp.zeros_like(tile)
        low = jnp.where(lanes >= S, up[j], up[j - 1] if j > 0 else fill)
        high = jnp.where(lanes < LANES - S, down[j], down[j + 1] if j + 1 < GROUPS else fill)
        left = jnp.where(z != 0, pltpu.roll(tile, 1, 1), fill)
        right = jnp.where(z != S - 1, pltpu.roll(tile, LANES - 1, 1), fill)
        out.append((low + high) + (left + right))
    return out


def octant_place(local_id):
    box = local_id >> 3
    return box * S + ((local_id >> 2) & 1) * H, (local_id >> 1) & 1, local_id & 1


def edges_kernel(u0, k0, v0, u1, k1, v1, near_ref, far_ref):
    _, _, _, odd = sides()
    first = (u0[0:2, :], k0[...].astype(jnp.float32)[0:2, :], v0[...].astype(jnp.float32)[0:2, :])
    last = (u1[6:8, :], k1[...].astype(jnp.float32)[14:16, :], v1[...].astype(jnp.float32)[14:16, :])
    is_odd = odd == 1
    for n, (low, high) in enumerate(zip(first, last)):
        near_ref[2 * n : 2 * n + 2, :] = jnp.where(is_odd, low, high)
        far_ref[2 * n : 2 * n + 2, :] = jnp.where(is_odd, high, low)
    for ref in (near_ref, far_ref):
        ref[6:8, :] = jnp.zeros((2, S * S), jnp.float32)


def pack_rims(old, mid, xs, pack_ref, slot, local_id, base):
    lanes, rows = lane_ids(), row_ids()
    start, oy, oz = octant_place(local_id)
    start = start + base
    half = pl.multiple_of(oy * (S * H), LANES)
    for n, (ref, shift, row) in enumerate(((old, -8, 7), (old, H, 0), (mid, -8, 7), (mid, H, 0))):
        tile = ref[pl.ds(pl.multiple_of(start + shift, 8), 8), pl.ds(half, S * H)]
        line = tile[row : row + 1, :]
        xs[n : n + 1, :] = line
        xs[n + 4 : n + 5, :] = line
    index_x = ((lanes >> 4) & 3) * S + oz * H + (lanes & (H - 1))
    picked = [gather_lanes(xs[:, LANES * s : LANES * (s + 1)], index_x) for s in range(4)]
    low = jnp.where(lanes < 64, picked[0], picked[1])
    high = jnp.where(lanes < 64, picked[2], picked[3])
    faces = jnp.where(rows < 4, low, high)
    mean = 0.5 * (faces + pltpu.roll(faces, 2, 0))
    pack_ref[slot, 0:8, :] = jnp.where((rows & 2) == 0, faces, mean)
    index_y = oy * (LANES - S) + oz * H + (lanes & (H - 1))
    index_z = (lanes & 3) * S + H - oz
    y_group = pl.multiple_of(S * H - LANES * oy, LANES)
    for t in range(2):
        at = pl.multiple_of(start + 8 * t, 8)
        values = []
        for ref in (old, mid):
            y_face = gather_lanes(ref[pl.ds(at, 8), pl.ds(y_group, LANES)], index_y)
            parts = [
                gather_lanes(ref[pl.ds(at, 8), pl.ds(pl.multiple_of(half + LANES * s, LANES), LANES)], index_z)
                for s in range(4)
            ]
            which = (lanes >> 2) & 3
            z_face = jnp.where(
                which < 2,
                jnp.where(which == 0, parts[0], parts[1]),
                jnp.where(which == 2, parts[2], parts[3]),
            )
            values.append(jnp.where((lanes & S) == 0, z_face, y_face))
        face = jnp.where(lanes < 64, values[0], 0.5 * (values[0] + values[1]))
        used = ((lanes >> 4) & 1) == jnp.where((lanes & S) == 0, oz, oy)
        pack_ref[slot, 8 + 8 * t : 16 + 8 * t, :] = jnp.where(used, face, 0.0)


def find_boxes(parents, covers, boxes, octants):
    dev, devices = lax.axis_index("dev"), lax.axis_size("dev")
    group, groups = lax.axis_index("group"), lax.axis_size("group")
    for n in range(octants + 1):
        covers[n] = jnp.int32(-1)
    for r in range(3):
        source = lax.rem(dev + devices + r - 1, devices)
        for s in range(groups):
            first = (lax.rem(group + groups - s, groups) * devices + source) * boxes
            for k in range(boxes):
                local_id = parents[first + k] - dev * octants
                inside = jnp.logical_and(local_id >= 0, local_id < octants)
                covers[jnp.where(inside, local_id, octants)] = jnp.int32((r * groups + s) * boxes + k)


def step_tile(uc, pc, qc, ul, pll, ql, uh, ph, qh, lanes):
    sum_u = sum_yz(uc, lanes, False)
    sum_w = sum_yz([a * b for a, b in zip(pc, uc)], lanes, False)
    sum_q = sum_yz(qc, lanes, True)
    out = []
    for j in range(GROUPS):
        keep = (1.0 - 6.0 * pc[j]) - (sum_q[j] + (ql[j] + qh[j]))
        near_u = sum_u[j] + (ul[j] + uh[j])
        near_w = sum_w[j] + (pll[j] * ul[j] + ph[j] * uh[j])
        out.append(keep * uc[j] + (qc[j] * near_u + near_w))
    return out


def coarse_kernel(parents, u_ref, k_ref, v_ref, near_sum, u, mid_out, covers, p, q, split, sums, *, boxes):
    rows, wide = u_ref.shape
    base = MARGIN
    rate = 0.5 * RATE
    for ref in (u, p, q):
        for row in (base - 8, base + rows):
            ref[row : row + 8, :] = jnp.zeros((8, wide), jnp.float32)
    find_boxes(parents, covers, boxes, OCTANTS * (rows // S))

    @pl.loop(0, rows // 16, unroll=True)
    def _(i):
        at = pl.multiple_of(i * 16, 16)
        to = pl.multiple_of(base + i * 16, 8)
        diff = rate * k_ref[pl.ds(at, 16), :].astype(jnp.float32)
        pot = rate * v_ref[pl.ds(at, 16), :].astype(jnp.float32)
        dens = u_ref[pl.ds(at, 16), :]
        u[pl.ds(to, 16), :] = dens
        p[pl.ds(to, 16), :] = diff + pot
        q[pl.ds(to, 16), :] = diff - pot
        store_split(split, rows, at, dens, (diff + pot) * dens)

    for window, part, out in windows():
        near = near_sum[part, :]
        sums[0:rows, out] = rate * (product(k_ref[:, window], near) - product(v_ref[:, window], near))
        sums[rows : 3 * rows, out] = product_of_split(split, near, window)

    ends = edge_count()

    @pl.loop(0, rows // 8, unroll=True)
    def _(i):
        at = pl.multiple_of(i * 8, 8)
        uv, pv, qv = (ref.at[pl.ds(pl.multiple_of(at + base - 8, 8), 24), :] for ref in (u, p, q))
        sum_q, sum_u, sum_w = (sums[pl.ds(pl.multiple_of(n * rows + at, 8), 8), :] for n in range(3))
        uc, pc, qc = (view[8:16, :] for view in (uv, pv, qv))
        ul, uh = uv[7:15, :], uv[9:17, :]
        keep = (1.0 - 6.0 * pc) - (sum_q + ends * qc + (qv[7:15, :] + qv[9:17, :]))
        near_u = sum_u + (ul + uh)
        near_w = sum_w + (pv[7:15, :] * ul + pv[9:17, :] * uh)
        mid_out[pl.ds(pl.multiple_of(at + base, 8), 8), :] = keep * uc + (qc * near_u + near_w)


def rims_kernel(parents, u_in, mid_in, k_ref, v_ref, near_edge, far_edge, u, m, to_near, to_own, to_far, e, xs, *, boxes):
    del u_in, mid_in
    base = MARGIN
    rows = u.shape[0] - 2 * base
    rate = 0.5 * RATE
    devices = lax.axis_size("dev")
    dev, near_dev, far_dev, odd = sides()
    group = lax.axis_index("group")
    octants = OCTANTS * (rows // S)
    lanes = lane_ids()
    before = jnp.where(odd == 1, near_edge[...], far_edge[...])
    after = jnp.where(odd == 1, far_edge[...], near_edge[...])
    u[base - 2 : base, :] = before[0:2, :]
    u[base + rows : base + rows + 2, :] = after[0:2, :]
    for n, (far, end, own, top) in enumerate(((before, 0, 0, base - 2), (after, rows - 16, 14, base + rows - 2))):
        e[0, 7:11, :] = u[top : top + 4, :]
        own_diff = rate * k_ref[end : end + 16, :].astype(jnp.float32)[own : own + 2, :]
        own_pot = rate * v_ref[end : end + 16, :].astype(jnp.float32)[own : own + 2, :]
        far_diff, far_pot = rate * far[2:4, :], rate * far[4:6, :]
        there, here = (7, 9) if n == 0 else (9, 7)
        e[1, there : there + 2, :] = far_diff + far_pot
        e[2, there : there + 2, :] = far_diff - far_pot
        e[1, here : here + 2, :] = own_diff + own_pot
        e[2, here : here + 2, :] = own_diff - own_pot
        tiles = [lane_groups(e.at[f], row) for row in (8, 7, 9) for f in range(3)]
        for j, new in enumerate(step_tile(*tiles, lanes)):
            m[top + 1 : top + 3, LANES * j : LANES * (j + 1)] = new[0:2, :]
    for ref, target in ((to_far, far_dev), (to_near, near_dev), (to_own, dev)):
        for k in range(boxes):
            local_id = parents[(group * devices + target) * boxes + k] - dev * octants
            local_id = jnp.minimum(jnp.maximum(local_id, 0), octants - 1)
            pack_rims(u, m, xs, ref, k, local_id, base)


def fine_rates(k_ref, v_ref, at):
    diff = RATE * k_ref[pl.ds(at, 16), :].astype(jnp.float32)
    pot = (0.5 * RATE) * v_ref[pl.ds(at, 16), :].astype(jnp.float32)
    return diff + pot, diff - pot


def store_split(split, rows, at, *values):
    pairs = [pieces_of(value) for value in values]
    for n, part in enumerate([high for high, _ in pairs] + [low for _, low in pairs]):
        split[pl.ds(pl.multiple_of(n * rows + at, 16), 16), :] = part


def product_of_split(split, matrix, window=slice(None)):
    half = split.shape[0] // 2
    both = product(split[:, window], matrix)
    return both[0:half] + both[half : 2 * half]


def fine_first_kernel(u_ref, k_ref, v_ref, near_sum, out_ref, keep_ref, u, w, p, q, split, sums, *, boxes):
    rows, wide = out_ref.shape
    base = 8
    @pl.loop(0, boxes, unroll=True)
    def _(k):
        for ref in (u, w):
            for ghost in (7, 40):
                ref[k, ghost : ghost + 1, :] = jnp.zeros((1, wide), jnp.float32)
        for i in range(2):
            at, to = pl.multiple_of(S * k + 16 * i, 16), base + 16 * i
            pc, qc = fine_rates(k_ref, v_ref, at)
            dens = u_ref[pl.ds(at, 16), :]
            p[k, to : to + 16, :] = pc
            q[k, to : to + 16, :] = qc
            u[k, to : to + 16, :] = dens
            w[k, to : to + 16, :] = pc * dens
            store_split(split, rows, at, dens, pc * dens)
        for ghost, cell in ((7, 8), (40, 39)):
            q[k, ghost : ghost + 1, :] = q[k, cell : cell + 1, :]

    for window, part, out in windows():
        near = near_sum[part, :]
        sums[0 : 2 * rows, out] = product_of_split(split, near, window)
        sums[2 * rows : 3 * rows, out] = RATE * product(k_ref[:, window], near) - (0.5 * RATE) * product(
            v_ref[:, window], near
        )
    ends = edge_count()

    @pl.loop(0, boxes, unroll=True)
    def _(k):
        for i in range(2):
            at, to = pl.multiple_of(S * k + 16 * i, 16), base + 16 * i
            here, low, high = (slice(to + m, to + m + 16) for m in (0, -1, 1))
            sum_u, sum_w, sum_q = (
                sums[pl.ds(pl.multiple_of(n * rows + at, 16), 16), :] + (ref[k, low, :] + ref[k, high, :])
                for n, ref in enumerate((u, w, q))
            )
            qc = q[k, here, :]
            stay = (1.0 - 6.0 * p[k, here, :]) - (sum_q + ends * qc)
            keep_ref[pl.ds(at, 16), :] = stay
            out_ref[pl.ds(at, 16), :] = stay * u[k, here, :] + (qc * sum_u + sum_w)


def fine_second_kernel(parents, first, keep, k_ref, v_ref, near_sum, ghost_sum, block_sum, from_near, from_own, from_far, out_any, avg_ref, u, w, p, q, lines, split, sums, ghosts, faces, dup, res, means, out_sems, *, boxes, octants):
    devices = lax.axis_size("dev")
    dev, near_dev, _, _ = sides()
    group = lax.axis_index("group")
    rows, wide = res.shape
    base = 8
    lanes = lane_ids()
    z = lanes & (S - 1)
    for k in range(boxes):
        parent = parents[(group * devices + dev) * boxes + k]
        own_id, near_id = parent - dev * octants, parent - near_dev * octants
        is_own = jnp.logical_and(own_id >= 0, own_id < octants)
        is_near = jnp.logical_and(near_id >= 0, near_id < octants)

        def chosen(n):
            there = slice(8 * n, 8 * n + 8)
            other = jnp.where(is_near, from_near[k, there, :], from_far[k, there, :])
            return jnp.where(is_own, from_own[k, there, :], other)

        for n in range(2):
            face = chosen(n + 1)
            dup[pl.ds(S * k + 16 * n, 8, 2), :] = face
            dup[pl.ds(S * k + 16 * n + 1, 8, 2), :] = face
        for n, part in enumerate(pieces_of(dup[S * k : S * k + S, :])):
            faces[n * rows + S * k : n * rows + S * k + S, :] = part
        x_faces = chosen(0)
        for n in range(4):
            spread = gather_lanes(x_faces, (2 * n + (lanes >> 6)) * H + (z >> 1))
            for half in range(2):
                j = 4 * half + n
                there = slice(LANES * j, LANES * (j + 1))
                lines[k, 0:2, there] = spread[4 * half : 4 * half + 2, :]
                u[k, 7:8, there] = spread[4 * half + 2 : 4 * half + 3, :]
                u[k, 40:41, there] = spread[4 * half + 3 : 4 * half + 4, :]
    for n in range(4):
        out = slice(256 * n, 256 * n + 256)
        for step in range(2):
            ghosts[step * rows : (step + 1) * rows, out] = product_of_split(faces, ghost_sum[step, :, out])
    row = lax.broadcasted_iota(jnp.int32, (16, wide), 0)

    @pl.loop(0, boxes, unroll=True)
    def _(k):
        for i in range(2):
            at, to = pl.multiple_of(S * k + 16 * i, 16), base + 16 * i
            pc, qc = fine_rates(k_ref, v_ref, at)
            beside = ghosts[pl.ds(at, 16), :] + jnp.where(row == 15 * i, lines[k, i : i + 1, :], 0.0)
            new = first[pl.ds(at, 16), :] + (pc + qc) * beside
            p[k, to : to + 16, :] = pc
            q[k, to : to + 16, :] = qc
            u[k, to : to + 16, :] = new
            w[k, to : to + 16, :] = pc * new
            store_split(split, rows, at, new, pc * new)
        for ghost, cell in ((7, 8), (40, 39)):
            w[k, ghost : ghost + 1, :] = p[k, cell : cell + 1, :] * u[k, ghost : ghost + 1, :]

    for window, part, out in windows():
        sums[:, out] = product_of_split(split, near_sum[part, :], window)

    @pl.loop(0, boxes, unroll=True)
    def _(k):
        for i in range(2):
            at, to = pl.multiple_of(S * k + 16 * i, 16), base + 16 * i
            here, low, high = (slice(to + m, to + m + 16) for m in (0, -1, 1))
            sum_u, sum_w = (
                sums[pl.ds(pl.multiple_of(n * rows + at, 16), 16), :] + (ref[k, low, :] + ref[k, high, :])
                for n, ref in enumerate((u, w))
            )
            pc, qc = p[k, here, :], q[k, here, :]
            beside = ghosts[pl.ds(pl.multiple_of(rows + at, 16), 16), :]
            new = (keep[pl.ds(at, 16), :] * u[k, here, :] + (qc * sum_u + sum_w)) + (pc + qc) * beside
            res[pl.ds(at, 16), :] = new
            store_split(split, rows, at, new)

    out_copy = pltpu.make_async_copy(res, out_any, out_sems.at[0])
    out_copy.start()
    total = product_of_split(split.at[0 : 2 * rows, :], block_sum[...])
    for half in range(2):
        means[half, :, :] = total[:, LANES * half : LANES * (half + 1)]
    for half in range(2):
        for k in range(boxes):
            for t in range(2):
                at = S * k + 16 * t
                pair = means[half, pl.ds(at, 8, 2), :] + means[half, pl.ds(at + 1, 8, 2), :]
                avg_ref[k, 8 * t : 8 * t + 8, LANES * half : LANES * (half + 1)] = 0.125 * pair
    out_copy.wait()


def join_kernel(*refs):
    *pieces, out_ref = refs
    count = pieces[0].shape[0]
    for n, piece in enumerate(pieces):
        out_ref[n * count : (n + 1) * count] = piece[...]


def put_average(ref, slot, octant, out_ref):
    lanes = lane_ids()
    start = MARGIN + octant // 8 * S + (octant >> 2) % 2 * H
    oy, oz = (octant >> 1) % 2, octant % 2
    here = ((lanes >> 4) & 1) == oz
    for t in range(2):
        at = start + 8 * t
        for s in range(4):
            lane = oy * (S * H) + LANES * s
            half = s // 2
            tile = ref[slot, 8 * t : 8 * t + 8, LANES * half : LANES * (half + 1)]
            moved = gather_lanes(tile, (s % 2) * 64 + (lanes >> 5) * H + (lanes & (H - 1)))
            out_ref[at : at + 8, lane : lane + LANES] = jnp.where(here, moved, out_ref[at : at + 8, lane : lane + LANES])


def put_all(covers, pieces, octants, held):
    for octant in octants:
        for ref, first in pieces:
            slot = covers[octant] - first

            @pl.when(jnp.logical_and(slot >= 0, slot < ref.shape[0]))
            def _():
                put_average(ref, slot, octant, held)


def merge_own_kernel(covers, mid, own, held):
    del mid
    put_all(covers, [(own, own.shape[0])], range(OCTANTS * ((held.shape[0] - 2 * MARGIN) // S)), held)


def merge_far_kernel(covers, held_in, near_ref, far_ref, held, out_any, out_sems):
    del held_in
    rows = out_any.shape[0]
    count = near_ref.shape[0]
    _, _, _, odd = sides()
    pieces = [(near_ref, 2 * count * (1 - odd)), (far_ref, 2 * count * odd)]
    stores = []
    for box in range(rows // S):
        put_all(covers, pieces, range(OCTANTS * box, OCTANTS * (box + 1)), held)
        there = held.at[MARGIN + box * S : MARGIN + (box + 1) * S, :]
        stores.append(pltpu.make_async_copy(there, out_any.at[box * S : (box + 1) * S, :], out_sems.at[box]))
        stores[-1].start()
    for copy in stores:
        copy.wait()


def params():
    return pltpu.CompilerParams(vmem_limit_bytes=VMEM_LIMIT)


def cost(flops, size):
    return pl.CostEstimate(flops=flops, bytes_accessed=size, transcendentals=0)


def f32(*shape):
    return jax.ShapeDtypeStruct(shape, jnp.float32)


def vmem(*shape):
    return pltpu.VMEM(shape, jnp.float32)


def bf16(*shape):
    return pltpu.VMEM(shape, jnp.bfloat16)


def whole():
    return pl.BlockSpec(memory_space=pltpu.VMEM)


def on_device(coarse_dens, coarse_diff, coarse_pot, fine_dens, fine_diff, fine_pot, parents):
    devices = lax.axis_size("dev")
    groups = lax.axis_size("group")
    rows = coarse_dens.shape[0]
    boxes = fine_dens.shape[0] // S
    fine_rows = boxes * S
    octants = OCTANTS * (rows // S)
    wide = S * S
    smem = pl.BlockSpec(memory_space=pltpu.SMEM)
    anywhere = pl.BlockSpec(memory_space=pl.ANY)
    dma = pltpu.SemaphoreType.DMA
    near_pairs = [(i, i ^ 1) for i in range(devices)]
    far_pairs = [(i, (i + devices - 1 + 2 * (i & 1)) % devices) for i in range(devices)]

    def swap(near, far):
        got_far = lax.ppermute(far, "dev", far_pairs)
        return lax.ppermute(near, "dev", near_pairs), got_far

    near_edge, far_edge = pl.pallas_call(
        edges_kernel,
        grid=(1,),
        in_specs=[
            pl.BlockSpec((8, wide), lambda i: (0, 0)),
            pl.BlockSpec((16, wide), lambda i: (0, 0)),
            pl.BlockSpec((16, wide), lambda i: (0, 0)),
            pl.BlockSpec((8, wide), lambda i: (rows // 8 - 1, 0)),
            pl.BlockSpec((16, wide), lambda i: (rows // 16 - 1, 0)),
            pl.BlockSpec((16, wide), lambda i: (rows // 16 - 1, 0)),
        ],
        out_specs=[pl.BlockSpec((8, wide), lambda i: (0, 0))] * 2,
        out_shape=[f32(8, wide)] * 2,
        name="edges",
    )(coarse_dens, coarse_diff, coarse_pot, coarse_dens, coarse_diff, coarse_pot)
    near_edge, far_edge = swap(near_edge, far_edge)

    near_sum = neighbour_matrix()
    ext = f32(rows + 2 * MARGIN, wide)
    held_dens, mid, covers = pl.pallas_call(
        functools.partial(coarse_kernel, boxes=boxes),
        grid_spec=pltpu.PrefetchScalarGridSpec(
            num_scalar_prefetch=1,
            grid=(),
            in_specs=[whole()] * 4,
            out_specs=[whole(), whole(), smem],
            scratch_shapes=[vmem(rows + 2 * MARGIN, wide)] * 2 + [bf16(4 * rows, wide), vmem(3 * rows, wide)],
        ),
        out_shape=[ext, ext, jax.ShapeDtypeStruct((octants + 1,), jnp.int32)],
        compiler_params=params(),
        cost_estimate=cost(rows * wide * 40, rows * wide * 12),
        name="coarse",
    )(parents, coarse_dens, coarse_diff, coarse_pot, near_sum)

    packs = f32(boxes, PACK, LANES)
    _, mid, to_near, own, to_far = pl.pallas_call(
        functools.partial(rims_kernel, boxes=boxes),
        grid_spec=pltpu.PrefetchScalarGridSpec(
            num_scalar_prefetch=1,
            grid=(),
            in_specs=[whole()] * 6,
            out_specs=[whole()] * 5,
            scratch_shapes=[vmem(3, 24, wide), vmem(8, S * H)],
        ),
        out_shape=[ext, ext, packs, packs, packs],
        input_output_aliases={1: 0, 2: 1},
        compiler_params=params(),
        cost_estimate=cost(rows * wide * 8, rows * wide * 8),
        name="rims",
    )(parents, held_dens, mid, coarse_diff, coarse_pot, near_edge, far_edge)
    from_near, from_far = swap(to_near, to_far)

    fine_first, keep = pl.pallas_call(
        functools.partial(fine_first_kernel, boxes=boxes),
        in_specs=[whole()] * 4,
        out_specs=[whole()] * 2,
        scratch_shapes=[vmem(boxes, 48, wide)] * 4 + [bf16(4 * fine_rows, wide), vmem(3 * fine_rows, wide)],
        out_shape=[f32(fine_rows, wide)] * 2,
        compiler_params=params(),
        cost_estimate=cost(fine_rows * wide * 40, fine_rows * wide * 16),
        name="fine_first",
    )(fine_dens, fine_diff, fine_pot, near_sum)

    fine_out, averages = pl.pallas_call(
        functools.partial(fine_second_kernel, boxes=boxes, octants=octants),
        grid_spec=pltpu.PrefetchScalarGridSpec(
            num_scalar_prefetch=1,
            grid=(),
            in_specs=[whole()] * 10,
            out_specs=[anywhere, whole()],
            scratch_shapes=[vmem(boxes, 48, wide)] * 4
            + [
                vmem(boxes, 8, wide),
                bf16(4 * fine_rows, wide),
                vmem(2 * fine_rows, wide),
                vmem(2 * fine_rows, wide),
                bf16(2 * fine_rows, LANES),
                vmem(fine_rows, LANES),
                vmem(fine_rows, wide),
                vmem(2, fine_rows, LANES),
                dma((1,)),
            ],
        ),
        out_shape=[f32(fine_rows, wide), f32(boxes, H, H * H)],
        compiler_params=params(),
        cost_estimate=cost(fine_rows * wide * 60, fine_rows * wide * 16),
        name="fine_second",
    )(
        parents,
        fine_first,
        keep,
        fine_diff,
        fine_pot,
        near_sum,
        ghost_matrices(),
        average_matrix(),
        from_near,
        own,
        from_far,
    )

    pieces = [averages]
    for s in range(1, groups):
        pieces.append(lax.ppermute(averages, "group", [(i, (i + s) % groups) for i in range(groups)]))
    joined = pl.pallas_call(
        join_kernel,
        in_specs=[whole()] * groups,
        out_specs=whole(),
        out_shape=f32(groups * boxes, H, H * H),
        compiler_params=params(),
        name="join",
    )(*pieces)
    near_avg, far_avg = swap(joined, joined)

    def merge(kernel, count, out_specs, out_shape, scratch, name):
        return pl.pallas_call(
            kernel,
            grid_spec=pltpu.PrefetchScalarGridSpec(
                num_scalar_prefetch=1,
                grid=(),
                in_specs=[whole()] * (1 + count),
                out_specs=[whole()] + out_specs,
                scratch_shapes=scratch,
            ),
            out_shape=[ext] + out_shape,
            input_output_aliases={1: 0},
            compiler_params=params(),
            cost_estimate=cost(rows * wide * 4, rows * wide * 12),
            name=name,
        )

    (held,) = merge(merge_own_kernel, 1, [], [], [], "merge_own")(covers, mid, joined)
    _, coarse_out = merge(
        merge_far_kernel, 2, [anywhere], [f32(rows, wide)], [dma((rows // S,))], "merge_far"
    )(covers, held, near_avg, far_avg)
    return coarse_out, fine_out


def solution(mesh):
    in_specs = (
        P("dev", None),
        P("dev", None),
        P("dev", None),
        P(("group", "dev"), None),
        P(("group", "dev"), None),
        P(("group", "dev"), None),
        P(),
    )
    out_specs = (P("dev", None), P(("group", "dev"), None))
    return jax.shard_map(on_device, mesh=mesh, in_specs=in_specs, out_specs=out_specs, check_vma=False)
```

```python
import functools

import jax
import jax.numpy as jnp
import numpy as np
from jax import lax
from jax.experimental import pallas as pl
from jax.experimental.pallas import tpu as pltpu
from jax.sharding import PartitionSpec as P

S = 32
H = 16
LANES = 128
GROUPS = 8
OCTANTS = 8
MARGIN = 16
PACK = 24
RATE = 0.06
VMEM_LIMIT = 32 * 1024 * 1024


def neighbour_matrix():
    source, target = np.arange(512)[:, None] - LANES, np.arange(256)[None, :]
    step = source - target
    same_y = source // S == target // S
    return jnp.asarray((np.abs(step) == S) | ((np.abs(step) == 1) & same_y), jnp.bfloat16)


def ghost_matrices():
    source, target = np.arange(LANES)[:, None], np.arange(S * S)[None, :]
    part, place = (source >> 4) & 3, source & (H - 1)
    y, z = target // S, target % S
    faces = (
        ((part == 0) & (z == S - 1) & (y // 2 == place))
        | ((part == 1) & (z == 0) & (y // 2 == place))
        | ((part == 2) & (y == S - 1) & (z // 2 == place))
        | ((part == 3) & (y == 0) & (z // 2 == place))
    )
    return jnp.asarray(np.stack([faces & (source // 64 == step) for step in range(2)]), jnp.bfloat16)


def average_matrix():
    source, target = np.arange(S * S)[:, None], np.arange(H * H)[None, :]
    return jnp.asarray((source // S // 2 == target // H) & (source % S // 2 == target % H), jnp.bfloat16)


def pieces_of(value):
    high = value.astype(jnp.bfloat16)
    return high, (value - high.astype(jnp.float32)).astype(jnp.bfloat16)


def windows():
    for n in range(4):
        low, high = max(256 * n - LANES, 0), min(256 * n + 256 + LANES, S * S)
        first = low - (256 * n - LANES)
        yield slice(low, high), slice(first, first + high - low), slice(256 * n, 256 * n + 256)


def product(left, right):
    return jnp.dot(left, right, preferred_element_type=jnp.float32)


def sides():
    dev, devices = lax.axis_index("dev"), lax.axis_size("dev")
    odd = dev & 1
    near = dev + 1 - 2 * odd
    far = lax.rem(dev + devices - 1 + 2 * odd, devices)
    return dev, near, far, odd


def edge_count():
    lane = lax.broadcasted_iota(jnp.int32, (1, S * S), 1)
    z, y = lane & (S - 1), lane >> 5
    return sum((at == end).astype(jnp.float32) for at in (z, y) for end in (0, S - 1))


def lane_ids():
    return lax.broadcasted_iota(jnp.int32, (8, LANES), 1)


def row_ids():
    return lax.broadcasted_iota(jnp.int32, (8, LANES), 0)


def gather_lanes(tile, index):
    return jnp.take_along_axis(tile, index, axis=1, mode="promise_in_bounds")


def lane_groups(ref, row):
    return [ref[row : row + 8, LANES * j : LANES * (j + 1)] for j in range(GROUPS)]


def sum_yz(tiles, lanes, edge):
    z = lanes & (S - 1)
    up = [pltpu.roll(t, S, 1) for t in tiles]
    down = [pltpu.roll(t, LANES - S, 1) for t in tiles]
    out = []
    for j, tile in enumerate(tiles):
        fill = tile if edge else jnp.zeros_like(tile)
        low = jnp.where(lanes >= S, up[j], up[j - 1] if j > 0 else fill)
        high = jnp.where(lanes < LANES - S, down[j], down[j + 1] if j + 1 < GROUPS else fill)
        left = jnp.where(z != 0, pltpu.roll(tile, 1, 1), fill)
        right = jnp.where(z != S - 1, pltpu.roll(tile, LANES - 1, 1), fill)
        out.append((low + high) + (left + right))
    return out


def octant_place(local_id):
    box = local_id >> 3
    return box * S + ((local_id >> 2) & 1) * H, (local_id >> 1) & 1, local_id & 1


def edges_kernel(u0, k0, v0, u1, k1, v1, near_ref, far_ref):
    _, _, _, odd = sides()
    first = (u0[0:2, :], k0[...].astype(jnp.float32)[0:2, :], v0[...].astype(jnp.float32)[0:2, :])
    last = (u1[6:8, :], k1[...].astype(jnp.float32)[14:16, :], v1[...].astype(jnp.float32)[14:16, :])
    is_odd = odd == 1
    for n, (low, high) in enumerate(zip(first, last)):
        near_ref[2 * n : 2 * n + 2, :] = jnp.where(is_odd, low, high)
        far_ref[2 * n : 2 * n + 2, :] = jnp.where(is_odd, high, low)
    for ref in (near_ref, far_ref):
        ref[6:8, :] = jnp.zeros((2, S * S), jnp.float32)


def pack_rims(old, mid, xs, pack_ref, slot, local_id, base):
    lanes, rows = lane_ids(), row_ids()
    start, oy, oz = octant_place(local_id)
    start = start + base
    half = pl.multiple_of(oy * (S * H), LANES)
    for n, (ref, shift, row) in enumerate(((old, -8, 7), (old, H, 0), (mid, -8, 7), (mid, H, 0))):
        tile = ref[pl.ds(pl.multiple_of(start + shift, 8), 8), pl.ds(half, S * H)]
        line = tile[row : row + 1, :]
        xs[n : n + 1, :] = line
        xs[n + 4 : n + 5, :] = line
    index_x = ((lanes >> 4) & 3) * S + oz * H + (lanes & (H - 1))
    picked = [gather_lanes(xs[:, LANES * s : LANES * (s + 1)], index_x) for s in range(4)]
    low = jnp.where(lanes < 64, picked[0], picked[1])
    high = jnp.where(lanes < 64, picked[2], picked[3])
    faces = jnp.where(rows < 4, low, high)
    mean = 0.5 * (faces + pltpu.roll(faces, 2, 0))
    pack_ref[slot, 0:8, :] = jnp.where((rows & 2) == 0, faces, mean)
    index_y = oy * (LANES - S) + oz * H + (lanes & (H - 1))
    index_z = (lanes & 3) * S + H - oz
    y_group = pl.multiple_of(S * H - LANES * oy, LANES)
    for t in range(2):
        at = pl.multiple_of(start + 8 * t, 8)
        values = []
        for ref in (old, mid):
            y_face = gather_lanes(ref[pl.ds(at, 8), pl.ds(y_group, LANES)], index_y)
            parts = [
                gather_lanes(ref[pl.ds(at, 8), pl.ds(pl.multiple_of(half + LANES * s, LANES), LANES)], index_z)
                for s in range(4)
            ]
            which = (lanes >> 2) & 3
            z_face = jnp.where(
                which < 2,
                jnp.where(which == 0, parts[0], parts[1]),
                jnp.where(which == 2, parts[2], parts[3]),
            )
            values.append(jnp.where((lanes & S) == 0, z_face, y_face))
        face = jnp.where(lanes < 64, values[0], 0.5 * (values[0] + values[1]))
        used = ((lanes >> 4) & 1) == jnp.where((lanes & S) == 0, oz, oy)
        pack_ref[slot, 8 + 8 * t : 16 + 8 * t, :] = jnp.where(used, face, 0.0)


def find_boxes(parents, covers, boxes, octants):
    dev, devices = lax.axis_index("dev"), lax.axis_size("dev")
    group, groups = lax.axis_index("group"), lax.axis_size("group")
    for n in range(octants + 1):
        covers[n] = jnp.int32(-1)
    for r in range(3):
        source = lax.rem(dev + devices + r - 1, devices)
        for s in range(groups):
            first = (lax.rem(group + groups - s, groups) * devices + source) * boxes
            for k in range(boxes):
                local_id = parents[first + k] - dev * octants
                inside = jnp.logical_and(local_id >= 0, local_id < octants)
                covers[jnp.where(inside, local_id, octants)] = jnp.int32((r * groups + s) * boxes + k)


def step_tile(uc, pc, qc, ul, pll, ql, uh, ph, qh, lanes):
    sum_u = sum_yz(uc, lanes, False)
    sum_w = sum_yz([a * b for a, b in zip(pc, uc)], lanes, False)
    sum_q = sum_yz(qc, lanes, True)
    out = []
    for j in range(GROUPS):
        keep = (1.0 - 6.0 * pc[j]) - (sum_q[j] + (ql[j] + qh[j]))
        near_u = sum_u[j] + (ul[j] + uh[j])
        near_w = sum_w[j] + (pll[j] * ul[j] + ph[j] * uh[j])
        out.append(keep * uc[j] + (qc[j] * near_u + near_w))
    return out


def coarse_kernel(u_ref, k_ref, v_ref, near_sum, u, mid_out, p, q, split, sums):
    rows, wide = u_ref.shape
    base = MARGIN
    rate = 0.5 * RATE
    for ref in (u, p, q):
        for row in (base - 8, base + rows):
            ref[row : row + 8, :] = jnp.zeros((8, wide), jnp.float32)

    @pl.loop(0, rows // 16, unroll=True)
    def _(i):
        at = pl.multiple_of(i * 16, 16)
        to = pl.multiple_of(base + i * 16, 8)
        diff = rate * k_ref[pl.ds(at, 16), :].astype(jnp.float32)
        pot = rate * v_ref[pl.ds(at, 16), :].astype(jnp.float32)
        dens = u_ref[pl.ds(at, 16), :]
        u[pl.ds(to, 16), :] = dens
        p[pl.ds(to, 16), :] = diff + pot
        q[pl.ds(to, 16), :] = diff - pot
        store_split(split, rows, at, dens, (diff + pot) * dens)

    for window, part, out in windows():
        near = near_sum[part, :]
        sums[0:rows, out] = rate * (product(k_ref[:, window], near) - product(v_ref[:, window], near))
        sums[rows : 3 * rows, out] = product_of_split(split, near, window)

    ends = edge_count()

    @pl.loop(0, rows // 8, unroll=True)
    def _(i):
        at = pl.multiple_of(i * 8, 8)
        uv, pv, qv = (ref.at[pl.ds(pl.multiple_of(at + base - 8, 8), 24), :] for ref in (u, p, q))
        sum_q, sum_u, sum_w = (sums[pl.ds(pl.multiple_of(n * rows + at, 8), 8), :] for n in range(3))
        uc, pc, qc = (view[8:16, :] for view in (uv, pv, qv))
        ul, uh = uv[7:15, :], uv[9:17, :]
        keep = (1.0 - 6.0 * pc) - (sum_q + ends * qc + (qv[7:15, :] + qv[9:17, :]))
        near_u = sum_u + (ul + uh)
        near_w = sum_w + (pv[7:15, :] * ul + pv[9:17, :] * uh)
        mid_out[pl.ds(pl.multiple_of(at + base, 8), 8), :] = keep * uc + (qc * near_u + near_w)


def rims_kernel(parents, u_in, mid_in, k_ref, v_ref, near_edge, far_edge, u, m, to_near, to_own, to_far, e, xs, *, boxes):
    del u_in, mid_in
    base = MARGIN
    rows = u.shape[0] - 2 * base
    rate = 0.5 * RATE
    devices = lax.axis_size("dev")
    dev, near_dev, far_dev, odd = sides()
    group = lax.axis_index("group")
    octants = OCTANTS * (rows // S)
    lanes = lane_ids()
    before = jnp.where(odd == 1, near_edge[...], far_edge[...])
    after = jnp.where(odd == 1, far_edge[...], near_edge[...])
    u[base - 2 : base, :] = before[0:2, :]
    u[base + rows : base + rows + 2, :] = after[0:2, :]
    for n, (far, end, own, top) in enumerate(((before, 0, 0, base - 2), (after, rows - 16, 14, base + rows - 2))):
        e[0, 7:11, :] = u[top : top + 4, :]
        own_diff = rate * k_ref[end : end + 16, :].astype(jnp.float32)[own : own + 2, :]
        own_pot = rate * v_ref[end : end + 16, :].astype(jnp.float32)[own : own + 2, :]
        far_diff, far_pot = rate * far[2:4, :], rate * far[4:6, :]
        there, here = (7, 9) if n == 0 else (9, 7)
        e[1, there : there + 2, :] = far_diff + far_pot
        e[2, there : there + 2, :] = far_diff - far_pot
        e[1, here : here + 2, :] = own_diff + own_pot
        e[2, here : here + 2, :] = own_diff - own_pot
        tiles = [lane_groups(e.at[f], row) for row in (8, 7, 9) for f in range(3)]
        for j, new in enumerate(step_tile(*tiles, lanes)):
            m[top + 1 : top + 3, LANES * j : LANES * (j + 1)] = new[0:2, :]
    for ref, target in ((to_far, far_dev), (to_near, near_dev), (to_own, dev)):
        for k in range(boxes):
            local_id = parents[(group * devices + target) * boxes + k] - dev * octants
            local_id = jnp.minimum(jnp.maximum(local_id, 0), octants - 1)
            pack_rims(u, m, xs, ref, k, local_id, base)


def fine_rates(k_ref, v_ref, at):
    diff = RATE * k_ref[pl.ds(at, 16), :].astype(jnp.float32)
    pot = (0.5 * RATE) * v_ref[pl.ds(at, 16), :].astype(jnp.float32)
    return diff + pot, diff - pot


def store_split(split, rows, at, *values):
    pairs = [pieces_of(value) for value in values]
    for n, part in enumerate([high for high, _ in pairs] + [low for _, low in pairs]):
        split[pl.ds(pl.multiple_of(n * rows + at, 16), 16), :] = part


def product_of_split(split, matrix, window=slice(None)):
    half = split.shape[0] // 2
    both = product(split[:, window], matrix)
    return both[0:half] + both[half : 2 * half]


def fine_first_kernel(u_ref, k_ref, v_ref, near_sum, out_ref, keep_ref, u, w, p, q, split, sums, *, boxes):
    rows, wide = out_ref.shape
    base = 8
    @pl.loop(0, boxes, unroll=True)
    def _(k):
        for ref in (u, w):
            for ghost in (7, 40):
                ref[k, ghost : ghost + 1, :] = jnp.zeros((1, wide), jnp.float32)
        for i in range(2):
            at, to = pl.multiple_of(S * k + 16 * i, 16), base + 16 * i
            pc, qc = fine_rates(k_ref, v_ref, at)
            dens = u_ref[pl.ds(at, 16), :]
            p[k, to : to + 16, :] = pc
            q[k, to : to + 16, :] = qc
            u[k, to : to + 16, :] = dens
            w[k, to : to + 16, :] = pc * dens
            store_split(split, rows, at, dens, pc * dens)
        for ghost, cell in ((7, 8), (40, 39)):
            q[k, ghost : ghost + 1, :] = q[k, cell : cell + 1, :]

    for window, part, out in windows():
        near = near_sum[part, :]
        sums[0 : 2 * rows, out] = product_of_split(split, near, window)
        sums[2 * rows : 3 * rows, out] = RATE * product(k_ref[:, window], near) - (0.5 * RATE) * product(
            v_ref[:, window], near
        )
    ends = edge_count()

    @pl.loop(0, boxes, unroll=True)
    def _(k):
        for i in range(2):
            at, to = pl.multiple_of(S * k + 16 * i, 16), base + 16 * i
            here, low, high = (slice(to + m, to + m + 16) for m in (0, -1, 1))
            sum_u, sum_w, sum_q = (
                sums[pl.ds(pl.multiple_of(n * rows + at, 16), 16), :] + (ref[k, low, :] + ref[k, high, :])
                for n, ref in enumerate((u, w, q))
            )
            qc = q[k, here, :]
            stay = (1.0 - 6.0 * p[k, here, :]) - (sum_q + ends * qc)
            keep_ref[pl.ds(at, 16), :] = stay
            out_ref[pl.ds(at, 16), :] = stay * u[k, here, :] + (qc * sum_u + sum_w)


def fine_second_kernel(parents, first, keep, k_ref, v_ref, near_sum, ghost_sum, block_sum, from_near, from_own, from_far, out_any, avg_ref, u, w, p, q, lines, split, sums, ghosts, faces, dup, res, means, out_sems, *, boxes, octants):
    devices = lax.axis_size("dev")
    dev, near_dev, _, _ = sides()
    group = lax.axis_index("group")
    rows, wide = res.shape
    base = 8
    lanes = lane_ids()
    z = lanes & (S - 1)
    for k in range(boxes):
        parent = parents[(group * devices + dev) * boxes + k]
        own_id, near_id = parent - dev * octants, parent - near_dev * octants
        is_own = jnp.logical_and(own_id >= 0, own_id < octants)
        is_near = jnp.logical_and(near_id >= 0, near_id < octants)

        def chosen(n):
            there = slice(8 * n, 8 * n + 8)
            other = jnp.where(is_near, from_near[k, there, :], from_far[k, there, :])
            return jnp.where(is_own, from_own[k, there, :], other)

        for n in range(2):
            face = chosen(n + 1)
            dup[pl.ds(S * k + 16 * n, 8, 2), :] = face
            dup[pl.ds(S * k + 16 * n + 1, 8, 2), :] = face
        for n, part in enumerate(pieces_of(dup[S * k : S * k + S, :])):
            faces[n * rows + S * k : n * rows + S * k + S, :] = part
        x_faces = chosen(0)
        for n in range(4):
            spread = gather_lanes(x_faces, (2 * n + (lanes >> 6)) * H + (z >> 1))
            for half in range(2):
                j = 4 * half + n
                there = slice(LANES * j, LANES * (j + 1))
                lines[k, 0:2, there] = spread[4 * half : 4 * half + 2, :]
                u[k, 7:8, there] = spread[4 * half + 2 : 4 * half + 3, :]
                u[k, 40:41, there] = spread[4 * half + 3 : 4 * half + 4, :]
    for n in range(4):
        out = slice(256 * n, 256 * n + 256)
        for step in range(2):
            ghosts[step * rows : (step + 1) * rows, out] = product_of_split(faces, ghost_sum[step, :, out])
    row = lax.broadcasted_iota(jnp.int32, (16, wide), 0)

    @pl.loop(0, boxes, unroll=True)
    def _(k):
        for i in range(2):
            at, to = pl.multiple_of(S * k + 16 * i, 16), base + 16 * i
            pc, qc = fine_rates(k_ref, v_ref, at)
            beside = ghosts[pl.ds(at, 16), :] + jnp.where(row == 15 * i, lines[k, i : i + 1, :], 0.0)
            new = first[pl.ds(at, 16), :] + (pc + qc) * beside
            p[k, to : to + 16, :] = pc
            q[k, to : to + 16, :] = qc
            u[k, to : to + 16, :] = new
            w[k, to : to + 16, :] = pc * new
            store_split(split, rows, at, new, pc * new)
        for ghost, cell in ((7, 8), (40, 39)):
            w[k, ghost : ghost + 1, :] = p[k, cell : cell + 1, :] * u[k, ghost : ghost + 1, :]

    for window, part, out in windows():
        sums[:, out] = product_of_split(split, near_sum[part, :], window)

    @pl.loop(0, boxes, unroll=True)
    def _(k):
        for i in range(2):
            at, to = pl.multiple_of(S * k + 16 * i, 16), base + 16 * i
            here, low, high = (slice(to + m, to + m + 16) for m in (0, -1, 1))
            sum_u, sum_w = (
                sums[pl.ds(pl.multiple_of(n * rows + at, 16), 16), :] + (ref[k, low, :] + ref[k, high, :])
                for n, ref in enumerate((u, w))
            )
            pc, qc = p[k, here, :], q[k, here, :]
            beside = ghosts[pl.ds(pl.multiple_of(rows + at, 16), 16), :]
            new = (keep[pl.ds(at, 16), :] * u[k, here, :] + (qc * sum_u + sum_w)) + (pc + qc) * beside
            res[pl.ds(at, 16), :] = new
            store_split(split, rows, at, new)

    out_copy = pltpu.make_async_copy(res, out_any, out_sems.at[0])
    out_copy.start()
    total = product_of_split(split.at[0 : 2 * rows, :], block_sum[...])
    for half in range(2):
        means[half, :, :] = total[:, LANES * half : LANES * (half + 1)]
    for half in range(2):
        for k in range(boxes):
            for t in range(2):
                at = S * k + 16 * t
                pair = means[half, pl.ds(at, 8, 2), :] + means[half, pl.ds(at + 1, 8, 2), :]
                avg_ref[k, 8 * t : 8 * t + 8, LANES * half : LANES * (half + 1)] = 0.125 * pair
    out_copy.wait()


def join_kernel(*refs):
    *pieces, out_ref = refs
    count = pieces[0].shape[0]
    for n, piece in enumerate(pieces):
        out_ref[n * count : (n + 1) * count] = piece[...]


LIST = 64
COUNTS = 50
OCTANT_BITS = 7


def list_octants(covers, own_list, side_list, count, octants):
    _, _, _, odd = sides()
    n_own = n_side = jnp.int32(0)
    for octant in range(octants):
        if octant % OCTANTS == 0:
            side_list[COUNTS + octant // OCTANTS] = n_side
        place = covers[octant]
        is_next = (place >= 2 * count).astype(jnp.int32)
        is_own = jnp.logical_and(place >= count, is_next == 0).astype(jnp.int32)
        is_side = jnp.logical_and(place >= 0, is_own == 0).astype(jnp.int32)
        is_far = jnp.where(odd == 1, is_next, 1 - is_next)
        own_list[n_own] = ((place - count) << OCTANT_BITS) + octant
        side_list[n_side] = (((place - 2 * count * is_next) * 2 + is_far) << OCTANT_BITS) + octant
        n_own, n_side = n_own + is_own, n_side + is_side
    side_list[COUNTS + octants // OCTANTS] = n_side
    return n_own


def put_average(tile_of, octant, held):
    lanes = lane_ids()
    start, oy, oz = octant_place(octant)
    here = ((lanes >> 4) & 1) == oz
    for t in range(2):
        at = pl.ds(pl.multiple_of(MARGIN + start + 8 * t, 8), 8)
        for s in range(4):
            lane = pl.ds(pl.multiple_of(oy * (S * H) + LANES * s, LANES), LANES)
            half = s // 2
            tile = tile_of(slice(8 * t, 8 * t + 8), slice(LANES * half, LANES * (half + 1)))
            moved = gather_lanes(tile, (s % 2) * 64 + (lanes >> 5) * H + (lanes & (H - 1)))
            held[at, lane] = jnp.where(here, moved, held[at, lane])


def merge_own_kernel(parents, mid, own, held, side_list, covers, own_list, *, boxes, octants):
    del mid
    find_boxes(parents, covers, boxes, octants)
    count = list_octants(covers, own_list, side_list, own.shape[0], octants)

    @pl.loop(0, count)
    def _(n):
        entry = own_list[n]
        slot = entry >> OCTANT_BITS
        put_average(lambda rows, lanes: own[slot, rows, lanes], entry & ((1 << OCTANT_BITS) - 1), held)


def merge_side_kernel(side_list, held_in, near_ref, far_ref, held, out_any, out_sems):
    del held_in
    stores = []
    for box in range(out_any.shape[0] // S):

        @pl.loop(side_list[COUNTS + box], side_list[COUNTS + box + 1])
        def _(n):
            entry = side_list[n]
            is_far = ((entry >> OCTANT_BITS) & 1) == 1
            slot = entry >> (OCTANT_BITS + 1)
            put_average(
                lambda rows, lanes: jnp.where(is_far, far_ref[slot, rows, lanes], near_ref[slot, rows, lanes]),
                entry & ((1 << OCTANT_BITS) - 1),
                held,
            )

        there = held.at[MARGIN + box * S : MARGIN + (box + 1) * S, :]
        stores.append(pltpu.make_async_copy(there, out_any.at[box * S : (box + 1) * S, :], out_sems.at[box]))
        stores[-1].start()
    for copy in stores:
        copy.wait()


def params():
    return pltpu.CompilerParams(vmem_limit_bytes=VMEM_LIMIT)


def cost(flops, size):
    return pl.CostEstimate(flops=flops, bytes_accessed=size, transcendentals=0)


def f32(*shape):
    return jax.ShapeDtypeStruct(shape, jnp.float32)


def vmem(*shape):
    return pltpu.VMEM(shape, jnp.float32)


def bf16(*shape):
    return pltpu.VMEM(shape, jnp.bfloat16)


def whole():
    return pl.BlockSpec(memory_space=pltpu.VMEM)


def on_device(coarse_dens, coarse_diff, coarse_pot, fine_dens, fine_diff, fine_pot, parents):
    devices = lax.axis_size("dev")
    groups = lax.axis_size("group")
    rows = coarse_dens.shape[0]
    boxes = fine_dens.shape[0] // S
    fine_rows = boxes * S
    octants = OCTANTS * (rows // S)
    wide = S * S
    smem = pl.BlockSpec(memory_space=pltpu.SMEM)
    anywhere = pl.BlockSpec(memory_space=pl.ANY)
    dma = pltpu.SemaphoreType.DMA
    near_pairs = [(i, i ^ 1) for i in range(devices)]
    far_pairs = [(i, (i + devices - 1 + 2 * (i & 1)) % devices) for i in range(devices)]

    def swap(near, far):
        got_far = lax.ppermute(far, "dev", far_pairs)
        return lax.ppermute(near, "dev", near_pairs), got_far

    near_edge, far_edge = pl.pallas_call(
        edges_kernel,
        grid=(1,),
        in_specs=[
            pl.BlockSpec((8, wide), lambda i: (0, 0)),
            pl.BlockSpec((16, wide), lambda i: (0, 0)),
            pl.BlockSpec((16, wide), lambda i: (0, 0)),
            pl.BlockSpec((8, wide), lambda i: (rows // 8 - 1, 0)),
            pl.BlockSpec((16, wide), lambda i: (rows // 16 - 1, 0)),
            pl.BlockSpec((16, wide), lambda i: (rows // 16 - 1, 0)),
        ],
        out_specs=[whole()] * 2,
        out_shape=[f32(8, wide)] * 2,
        compiler_params=params(),
        name="edges",
    )(coarse_dens, coarse_diff, coarse_pot, coarse_dens, coarse_diff, coarse_pot)
    near_edge, far_edge = swap(near_edge, far_edge)

    near_sum = neighbour_matrix()
    ext = f32(rows + 2 * MARGIN, wide)
    held_dens, mid = pl.pallas_call(
        coarse_kernel,
        in_specs=[whole()] * 4,
        out_specs=[whole()] * 2,
        scratch_shapes=[vmem(rows + 2 * MARGIN, wide)] * 2 + [bf16(4 * rows, wide), vmem(3 * rows, wide)],
        out_shape=[ext, ext],
        compiler_params=params(),
        cost_estimate=cost(rows * wide * 40, rows * wide * 12),
        name="coarse",
    )(coarse_dens, coarse_diff, coarse_pot, near_sum)

    packs = f32(boxes, PACK, LANES)
    _, mid, to_near, own, to_far = pl.pallas_call(
        functools.partial(rims_kernel, boxes=boxes),
        grid_spec=pltpu.PrefetchScalarGridSpec(
            num_scalar_prefetch=1,
            grid=(),
            in_specs=[whole()] * 6,
            out_specs=[whole()] * 5,
            scratch_shapes=[vmem(3, 24, wide), vmem(8, S * H)],
        ),
        out_shape=[ext, ext, packs, packs, packs],
        input_output_aliases={1: 0, 2: 1},
        compiler_params=params(),
        cost_estimate=cost(rows * wide * 8, rows * wide * 8),
        name="rims",
    )(parents, held_dens, mid, coarse_diff, coarse_pot, near_edge, far_edge)
    from_near, from_far = swap(to_near, to_far)

    fine_first, keep = pl.pallas_call(
        functools.partial(fine_first_kernel, boxes=boxes),
        in_specs=[whole()] * 4,
        out_specs=[whole()] * 2,
        scratch_shapes=[vmem(boxes, 48, wide)] * 4 + [bf16(4 * fine_rows, wide), vmem(3 * fine_rows, wide)],
        out_shape=[f32(fine_rows, wide)] * 2,
        compiler_params=params(),
        cost_estimate=cost(fine_rows * wide * 40, fine_rows * wide * 16),
        name="fine_first",
    )(fine_dens, fine_diff, fine_pot, near_sum)

    fine_out, averages = pl.pallas_call(
        functools.partial(fine_second_kernel, boxes=boxes, octants=octants),
        grid_spec=pltpu.PrefetchScalarGridSpec(
            num_scalar_prefetch=1,
            grid=(),
            in_specs=[whole()] * 10,
            out_specs=[anywhere, whole()],
            scratch_shapes=[vmem(boxes, 48, wide)] * 4
            + [
                vmem(boxes, 8, wide),
                bf16(4 * fine_rows, wide),
                vmem(2 * fine_rows, wide),
                vmem(2 * fine_rows, wide),
                bf16(2 * fine_rows, LANES),
                vmem(fine_rows, LANES),
                vmem(fine_rows, wide),
                vmem(2, fine_rows, LANES),
                dma((1,)),
            ],
        ),
        out_shape=[f32(fine_rows, wide), f32(boxes, H, H * H)],
        compiler_params=params(),
        cost_estimate=cost(fine_rows * wide * 60, fine_rows * wide * 16),
        name="fine_second",
    )(
        parents,
        fine_first,
        keep,
        fine_diff,
        fine_pot,
        near_sum,
        ghost_matrices(),
        average_matrix(),
        from_near,
        own,
        from_far,
    )

    pieces = [averages]
    for s in range(1, groups):
        pieces.append(lax.ppermute(averages, "group", [(i, (i + s) % groups) for i in range(groups)]))
    joined = pl.pallas_call(
        join_kernel,
        in_specs=[whole()] * groups,
        out_specs=whole(),
        out_shape=f32(groups * boxes, H, H * H),
        compiler_params=params(),
        name="join",
    )(*pieces)
    near_avg, far_avg = swap(joined, joined)

    def merge(kernel, count, out_specs, out_shape, scratch, name):
        return pl.pallas_call(
            kernel,
            grid_spec=pltpu.PrefetchScalarGridSpec(
                num_scalar_prefetch=1,
                grid=(),
                in_specs=[whole()] * (1 + count),
                out_specs=[whole()] + out_specs,
                scratch_shapes=scratch,
            ),
            out_shape=[ext] + out_shape,
            input_output_aliases={1: 0},
            compiler_params=params(),
            cost_estimate=cost(rows * wide * 4, rows * wide * 12),
            name=name,
        )

    side_list = jax.ShapeDtypeStruct((LIST,), jnp.int32)
    own_kernel = functools.partial(merge_own_kernel, boxes=boxes, octants=octants)
    lists = [pltpu.SMEM((octants + 1,), jnp.int32), pltpu.SMEM((LIST,), jnp.int32)]
    held, side_list = merge(own_kernel, 1, [smem], [side_list], lists, "merge_own")(parents, mid, joined)
    _, coarse_out = merge(merge_side_kernel, 2, [anywhere], [f32(rows, wide)], [dma((rows // S,))], "merge_side")(
        side_list, held, near_avg, far_avg
    )
    return coarse_out, fine_out


def solution(mesh):
    in_specs = (
        P("dev", None),
        P("dev", None),
        P("dev", None),
        P(("group", "dev"), None),
        P(("group", "dev"), None),
        P(("group", "dev"), None),
        P(),
    )
    out_specs = (P("dev", None), P(("group", "dev"), None))
    return jax.shard_map(on_device, mesh=mesh, in_specs=in_specs, out_specs=out_specs, check_vma=False)
```

```python
import functools

import jax
import jax.numpy as jnp
import numpy as np
from jax import lax
from jax.experimental import pallas as pl
from jax.experimental.pallas import tpu as pltpu
from jax.sharding import PartitionSpec as P

S = 32
H = 16
LANES = 128
GROUPS = 8
OCTANTS = 8
MARGIN = 16
PACK = 24
RATE = 0.06
VMEM_LIMIT = 32 * 1024 * 1024


def neighbour_matrix():
    source, target = np.arange(512)[:, None] - LANES, np.arange(256)[None, :]
    step = source - target
    same_y = source // S == target // S
    return jnp.asarray((np.abs(step) == S) | ((np.abs(step) == 1) & same_y), jnp.bfloat16)


def ghost_matrices():
    source, target = np.arange(LANES)[:, None], np.arange(S * S)[None, :]
    part, place = (source >> 4) & 3, source & (H - 1)
    y, z = target // S, target % S
    faces = (
        ((part == 0) & (z == S - 1) & (y // 2 == place))
        | ((part == 1) & (z == 0) & (y // 2 == place))
        | ((part == 2) & (y == S - 1) & (z // 2 == place))
        | ((part == 3) & (y == 0) & (z // 2 == place))
    )
    return jnp.asarray(np.stack([faces & (source // 64 == step) for step in range(2)]), jnp.bfloat16)


def average_matrix():
    source, target = np.arange(S * S)[:, None], np.arange(H * H)[None, :]
    return jnp.asarray((source // S // 2 == target // H) & (source % S // 2 == target % H), jnp.bfloat16)


def pieces_of(value):
    high = value.astype(jnp.bfloat16)
    return high, (value - high.astype(jnp.float32)).astype(jnp.bfloat16)


def windows():
    for n in range(4):
        low, high = max(256 * n - LANES, 0), min(256 * n + 256 + LANES, S * S)
        first = low - (256 * n - LANES)
        yield slice(low, high), slice(first, first + high - low), slice(256 * n, 256 * n + 256)


def product(left, right):
    return jnp.dot(left, right, preferred_element_type=jnp.float32)


def sides():
    dev, devices = lax.axis_index("dev"), lax.axis_size("dev")
    odd = dev & 1
    near = dev + 1 - 2 * odd
    far = lax.rem(dev + devices - 1 + 2 * odd, devices)
    return dev, near, far, odd


def edge_count():
    lane = lax.broadcasted_iota(jnp.int32, (1, S * S), 1)
    z, y = lane & (S - 1), lane >> 5
    return sum((at == end).astype(jnp.float32) for at in (z, y) for end in (0, S - 1))


def lane_ids():
    return lax.broadcasted_iota(jnp.int32, (8, LANES), 1)


def row_ids():
    return lax.broadcasted_iota(jnp.int32, (8, LANES), 0)


def gather_lanes(tile, index):
    return jnp.take_along_axis(tile, index, axis=1, mode="promise_in_bounds")


def lane_groups(ref, row):
    return [ref[row : row + 8, LANES * j : LANES * (j + 1)] for j in range(GROUPS)]


def sum_yz(tiles, lanes, edge):
    z = lanes & (S - 1)
    up = [pltpu.roll(t, S, 1) for t in tiles]
    down = [pltpu.roll(t, LANES - S, 1) for t in tiles]
    out = []
    for j, tile in enumerate(tiles):
        fill = tile if edge else jnp.zeros_like(tile)
        low = jnp.where(lanes >= S, up[j], up[j - 1] if j > 0 else fill)
        high = jnp.where(lanes < LANES - S, down[j], down[j + 1] if j + 1 < GROUPS else fill)
        left = jnp.where(z != 0, pltpu.roll(tile, 1, 1), fill)
        right = jnp.where(z != S - 1, pltpu.roll(tile, LANES - 1, 1), fill)
        out.append((low + high) + (left + right))
    return out


def octant_place(local_id):
    box = local_id >> 3
    return box * S + ((local_id >> 2) & 1) * H, (local_id >> 1) & 1, local_id & 1


def edges_kernel(u0, k0, v0, u1, k1, v1, near_ref, far_ref):
    _, _, _, odd = sides()
    first = (u0[0:2, :], k0[...].astype(jnp.float32)[0:2, :], v0[...].astype(jnp.float32)[0:2, :])
    last = (u1[6:8, :], k1[...].astype(jnp.float32)[14:16, :], v1[...].astype(jnp.float32)[14:16, :])
    is_odd = odd == 1
    for n, (low, high) in enumerate(zip(first, last)):
        near_ref[2 * n : 2 * n + 2, :] = jnp.where(is_odd, low, high)
        far_ref[2 * n : 2 * n + 2, :] = jnp.where(is_odd, high, low)
    for ref in (near_ref, far_ref):
        ref[6:8, :] = jnp.zeros((2, S * S), jnp.float32)


def pack_rims(old, mid, xs, pack_ref, slot, local_id, base):
    lanes, rows = lane_ids(), row_ids()
    start, oy, oz = octant_place(local_id)
    start = start + base
    half = pl.multiple_of(oy * (S * H), LANES)
    for n, (ref, shift, row) in enumerate(((old, -8, 7), (old, H, 0), (mid, -8, 7), (mid, H, 0))):
        tile = ref[pl.ds(pl.multiple_of(start + shift, 8), 8), pl.ds(half, S * H)]
        line = tile[row : row + 1, :]
        xs[n : n + 1, :] = line
        xs[n + 4 : n + 5, :] = line
    index_x = ((lanes >> 4) & 3) * S + oz * H + (lanes & (H - 1))
    picked = [gather_lanes(xs[:, LANES * s : LANES * (s + 1)], index_x) for s in range(4)]
    low = jnp.where(lanes < 64, picked[0], picked[1])
    high = jnp.where(lanes < 64, picked[2], picked[3])
    faces = jnp.where(rows < 4, low, high)
    mean = 0.5 * (faces + pltpu.roll(faces, 2, 0))
    pack_ref[slot, 0:8, :] = jnp.where((rows & 2) == 0, faces, mean)
    index_y = oy * (LANES - S) + oz * H + (lanes & (H - 1))
    index_z = (lanes & 3) * S + H - oz
    y_group = pl.multiple_of(S * H - LANES * oy, LANES)
    for t in range(2):
        at = pl.multiple_of(start + 8 * t, 8)
        values = []
        for ref in (old, mid):
            y_face = gather_lanes(ref[pl.ds(at, 8), pl.ds(y_group, LANES)], index_y)
            parts = [
                gather_lanes(ref[pl.ds(at, 8), pl.ds(pl.multiple_of(half + LANES * s, LANES), LANES)], index_z)
                for s in range(4)
            ]
            which = (lanes >> 2) & 3
            z_face = jnp.where(
                which < 2,
                jnp.where(which == 0, parts[0], parts[1]),
                jnp.where(which == 2, parts[2], parts[3]),
            )
            values.append(jnp.where((lanes & S) == 0, z_face, y_face))
        face = jnp.where(lanes < 64, values[0], 0.5 * (values[0] + values[1]))
        used = ((lanes >> 4) & 1) == jnp.where((lanes & S) == 0, oz, oy)
        pack_ref[slot, 8 + 8 * t : 16 + 8 * t, :] = jnp.where(used, face, 0.0)


def find_boxes(parents, covers, boxes, octants):
    dev, devices = lax.axis_index("dev"), lax.axis_size("dev")
    group, groups = lax.axis_index("group"), lax.axis_size("group")
    for n in range(octants + 1):
        covers[n] = jnp.int32(-1)
    for r in range(3):
        source = lax.rem(dev + devices + r - 1, devices)
        for s in range(groups):
            first = (lax.rem(group + groups - s, groups) * devices + source) * boxes
            for k in range(boxes):
                local_id = parents[first + k] - dev * octants
                inside = jnp.logical_and(local_id >= 0, local_id < octants)
                covers[jnp.where(inside, local_id, octants)] = jnp.int32((r * groups + s) * boxes + k)


def step_tile(uc, pc, qc, ul, pll, ql, uh, ph, qh, lanes):
    sum_u = sum_yz(uc, lanes, False)
    sum_w = sum_yz([a * b for a, b in zip(pc, uc)], lanes, False)
    sum_q = sum_yz(qc, lanes, True)
    out = []
    for j in range(GROUPS):
        keep = (1.0 - 6.0 * pc[j]) - (sum_q[j] + (ql[j] + qh[j]))
        near_u = sum_u[j] + (ul[j] + uh[j])
        near_w = sum_w[j] + (pll[j] * ul[j] + ph[j] * uh[j])
        out.append(keep * uc[j] + (qc[j] * near_u + near_w))
    return out


def coarse_kernel(u_ref, k_ref, v_ref, near_sum, u, mid_out, p, q, split, sums):
    rows, wide = u_ref.shape
    base = MARGIN
    rate = 0.5 * RATE
    for ref in (u, p, q):
        for row in (base - 8, base + rows):
            ref[row : row + 8, :] = jnp.zeros((8, wide), jnp.float32)

    @pl.loop(0, rows // 16, unroll=True)
    def _(i):
        at = pl.multiple_of(i * 16, 16)
        to = pl.multiple_of(base + i * 16, 8)
        diff = rate * k_ref[pl.ds(at, 16), :].astype(jnp.float32)
        pot = rate * v_ref[pl.ds(at, 16), :].astype(jnp.float32)
        dens = u_ref[pl.ds(at, 16), :]
        u[pl.ds(to, 16), :] = dens
        p[pl.ds(to, 16), :] = diff + pot
        q[pl.ds(to, 16), :] = diff - pot
        store_split(split, rows, at, dens, (diff + pot) * dens)

    for window, part, out in windows():
        near = near_sum[part, :]
        sums[0:rows, out] = rate * (product(k_ref[:, window], near) - product(v_ref[:, window], near))
        sums[rows : 3 * rows, out] = product_of_split(split, near, window)

    ends = edge_count()

    @pl.loop(0, rows // 8, unroll=True)
    def _(i):
        at = pl.multiple_of(i * 8, 8)
        uv, pv, qv = (ref.at[pl.ds(pl.multiple_of(at + base - 8, 8), 24), :] for ref in (u, p, q))
        sum_q, sum_u, sum_w = (sums[pl.ds(pl.multiple_of(n * rows + at, 8), 8), :] for n in range(3))
        uc, pc, qc = (view[8:16, :] for view in (uv, pv, qv))
        ul, uh = uv[7:15, :], uv[9:17, :]
        keep = (1.0 - 6.0 * pc) - (sum_q + ends * qc + (qv[7:15, :] + qv[9:17, :]))
        near_u = sum_u + (ul + uh)
        near_w = sum_w + (pv[7:15, :] * ul + pv[9:17, :] * uh)
        mid_out[pl.ds(pl.multiple_of(at + base, 8), 8), :] = keep * uc + (qc * near_u + near_w)


def rims_kernel(parents, u_in, mid_in, k_ref, v_ref, near_edge, far_edge, u, m, to_near, to_own, to_far, e, xs, *, boxes):
    del u_in, mid_in
    base = MARGIN
    rows = u.shape[0] - 2 * base
    rate = 0.5 * RATE
    devices = lax.axis_size("dev")
    dev, near_dev, far_dev, odd = sides()
    group = lax.axis_index("group")
    octants = OCTANTS * (rows // S)
    lanes = lane_ids()
    before = jnp.where(odd == 1, near_edge[...], far_edge[...])
    after = jnp.where(odd == 1, far_edge[...], near_edge[...])
    u[base - 2 : base, :] = before[0:2, :]
    u[base + rows : base + rows + 2, :] = after[0:2, :]
    for n, (far, end, own, top) in enumerate(((before, 0, 0, base - 2), (after, rows - 16, 14, base + rows - 2))):
        e[0, 7:11, :] = u[top : top + 4, :]
        own_diff = rate * k_ref[end : end + 16, :].astype(jnp.float32)[own : own + 2, :]
        own_pot = rate * v_ref[end : end + 16, :].astype(jnp.float32)[own : own + 2, :]
        far_diff, far_pot = rate * far[2:4, :], rate * far[4:6, :]
        there, here = (7, 9) if n == 0 else (9, 7)
        e[1, there : there + 2, :] = far_diff + far_pot
        e[2, there : there + 2, :] = far_diff - far_pot
        e[1, here : here + 2, :] = own_diff + own_pot
        e[2, here : here + 2, :] = own_diff - own_pot
        tiles = [lane_groups(e.at[f], row) for row in (8, 7, 9) for f in range(3)]
        for j, new in enumerate(step_tile(*tiles, lanes)):
            m[top + 1 : top + 3, LANES * j : LANES * (j + 1)] = new[0:2, :]
    for ref, target in ((to_far, far_dev), (to_near, near_dev), (to_own, dev)):
        for k in range(boxes):
            local_id = parents[(group * devices + target) * boxes + k] - dev * octants
            local_id = jnp.minimum(jnp.maximum(local_id, 0), octants - 1)
            pack_rims(u, m, xs, ref, k, local_id, base)


def fine_rates(k_ref, v_ref, at):
    diff = RATE * k_ref[pl.ds(at, 16), :].astype(jnp.float32)
    pot = (0.5 * RATE) * v_ref[pl.ds(at, 16), :].astype(jnp.float32)
    return diff + pot, diff - pot


def store_split(split, rows, at, *values):
    pairs = [pieces_of(value) for value in values]
    for n, part in enumerate([high for high, _ in pairs] + [low for _, low in pairs]):
        split[pl.ds(pl.multiple_of(n * rows + at, 16), 16), :] = part


def product_of_split(split, matrix, window=slice(None)):
    half = split.shape[0] // 2
    both = product(split[:, window], matrix)
    return both[0:half] + both[half : 2 * half]


def fine_first_kernel(u_ref, k_ref, v_ref, near_sum, out_ref, keep_ref, u, w, p, q, split, sums, *, boxes):
    rows, wide = out_ref.shape
    base = 8
    @pl.loop(0, boxes, unroll=True)
    def _(k):
        for ref in (u, w):
            for ghost in (7, 40):
                ref[k, ghost : ghost + 1, :] = jnp.zeros((1, wide), jnp.float32)
        for i in range(2):
            at, to = pl.multiple_of(S * k + 16 * i, 16), base + 16 * i
            pc, qc = fine_rates(k_ref, v_ref, at)
            dens = u_ref[pl.ds(at, 16), :]
            p[k, to : to + 16, :] = pc
            q[k, to : to + 16, :] = qc
            u[k, to : to + 16, :] = dens
            w[k, to : to + 16, :] = pc * dens
            store_split(split, rows, at, dens, pc * dens)
        for ghost, cell in ((7, 8), (40, 39)):
            q[k, ghost : ghost + 1, :] = q[k, cell : cell + 1, :]

    for window, part, out in windows():
        near = near_sum[part, :]
        sums[0 : 2 * rows, out] = product_of_split(split, near, window)
        sums[2 * rows : 3 * rows, out] = RATE * product(k_ref[:, window], near) - (0.5 * RATE) * product(
            v_ref[:, window], near
        )
    ends = edge_count()

    @pl.loop(0, boxes, unroll=True)
    def _(k):
        for i in range(2):
            at, to = pl.multiple_of(S * k + 16 * i, 16), base + 16 * i
            here, low, high = (slice(to + m, to + m + 16) for m in (0, -1, 1))
            sum_u, sum_w, sum_q = (
                sums[pl.ds(pl.multiple_of(n * rows + at, 16), 16), :] + (ref[k, low, :] + ref[k, high, :])
                for n, ref in enumerate((u, w, q))
            )
            qc = q[k, here, :]
            stay = (1.0 - 6.0 * p[k, here, :]) - (sum_q + ends * qc)
            keep_ref[pl.ds(at, 16), :] = stay
            out_ref[pl.ds(at, 16), :] = stay * u[k, here, :] + (qc * sum_u + sum_w)


def fine_second_kernel(parents, first, keep, k_ref, v_ref, near_sum, ghost_sum, block_sum, from_near, from_own, from_far, out_any, avg_ref, u, w, p, q, lines, split, sums, ghosts, faces, dup, res, means, out_sems, *, boxes, octants):
    devices = lax.axis_size("dev")
    dev, near_dev, _, _ = sides()
    group = lax.axis_index("group")
    rows, wide = res.shape
    base = 8
    lanes = lane_ids()
    z = lanes & (S - 1)
    for k in range(boxes):
        parent = parents[(group * devices + dev) * boxes + k]
        own_id, near_id = parent - dev * octants, parent - near_dev * octants
        is_own = jnp.logical_and(own_id >= 0, own_id < octants)
        is_near = jnp.logical_and(near_id >= 0, near_id < octants)

        def chosen(n):
            there = slice(8 * n, 8 * n + 8)
            other = jnp.where(is_near, from_near[k, there, :], from_far[k, there, :])
            return jnp.where(is_own, from_own[k, there, :], other)

        for n in range(2):
            face = chosen(n + 1)
            dup[pl.ds(S * k + 16 * n, 8, 2), :] = face
            dup[pl.ds(S * k + 16 * n + 1, 8, 2), :] = face
        for n, part in enumerate(pieces_of(dup[S * k : S * k + S, :])):
            faces[n * rows + S * k : n * rows + S * k + S, :] = part
        x_faces = chosen(0)
        for n in range(4):
            spread = gather_lanes(x_faces, (2 * n + (lanes >> 6)) * H + (z >> 1))
            for half in range(2):
                j = 4 * half + n
                there = slice(LANES * j, LANES * (j + 1))
                lines[k, 0:2, there] = spread[4 * half : 4 * half + 2, :]
                u[k, 7:8, there] = spread[4 * half + 2 : 4 * half + 3, :]
                u[k, 40:41, there] = spread[4 * half + 3 : 4 * half + 4, :]
    for n in range(4):
        out = slice(256 * n, 256 * n + 256)
        for step in range(2):
            ghosts[step * rows : (step + 1) * rows, out] = product_of_split(faces, ghost_sum[step, :, out])
    row = lax.broadcasted_iota(jnp.int32, (16, wide), 0)

    @pl.loop(0, boxes, unroll=True)
    def _(k):
        for i in range(2):
            at, to = pl.multiple_of(S * k + 16 * i, 16), base + 16 * i
            pc, qc = fine_rates(k_ref, v_ref, at)
            beside = ghosts[pl.ds(at, 16), :] + jnp.where(row == 15 * i, lines[k, i : i + 1, :], 0.0)
            new = first[pl.ds(at, 16), :] + (pc + qc) * beside
            p[k, to : to + 16, :] = pc
            q[k, to : to + 16, :] = qc
            u[k, to : to + 16, :] = new
            w[k, to : to + 16, :] = pc * new
            store_split(split, rows, at, new, pc * new)
        for ghost, cell in ((7, 8), (40, 39)):
            w[k, ghost : ghost + 1, :] = p[k, cell : cell + 1, :] * u[k, ghost : ghost + 1, :]

    for window, part, out in windows():
        sums[:, out] = product_of_split(split, near_sum[part, :], window)

    @pl.loop(0, boxes, unroll=True)
    def _(k):
        for i in range(2):
            at, to = pl.multiple_of(S * k + 16 * i, 16), base + 16 * i
            here, low, high = (slice(to + m, to + m + 16) for m in (0, -1, 1))
            sum_u, sum_w = (
                sums[pl.ds(pl.multiple_of(n * rows + at, 16), 16), :] + (ref[k, low, :] + ref[k, high, :])
                for n, ref in enumerate((u, w))
            )
            pc, qc = p[k, here, :], q[k, here, :]
            beside = ghosts[pl.ds(pl.multiple_of(rows + at, 16), 16), :]
            new = (keep[pl.ds(at, 16), :] * u[k, here, :] + (qc * sum_u + sum_w)) + (pc + qc) * beside
            res[pl.ds(at, 16), :] = new
            store_split(split, rows, at, new)

    out_copy = pltpu.make_async_copy(res, out_any, out_sems.at[0])
    out_copy.start()
    total = product_of_split(split.at[0 : 2 * rows, :], block_sum[...])
    for half in range(2):
        means[half, :, :] = total[:, LANES * half : LANES * (half + 1)]
    for half in range(2):
        for k in range(boxes):
            for t in range(2):
                at = S * k + 16 * t
                pair = means[half, pl.ds(at, 8, 2), :] + means[half, pl.ds(at + 1, 8, 2), :]
                avg_ref[k, 8 * t : 8 * t + 8, LANES * half : LANES * (half + 1)] = 0.125 * pair
    out_copy.wait()


def join_kernel(*refs):
    *pieces, out_ref = refs
    count = pieces[0].shape[0]
    for n, piece in enumerate(pieces):
        out_ref[n * count : (n + 1) * count] = piece[...]


LIST = 64
COUNTS = 50
OCTANT_BITS = 7


def list_octants(covers, chip_list, far_list, count, octants):
    _, _, _, odd = sides()
    n_chip = n_far = jnp.int32(0)
    for octant in range(octants):
        if octant % OCTANTS == 0:
            far_list[COUNTS + octant // OCTANTS] = n_far
        place = covers[octant]
        is_next = (place >= 2 * count).astype(jnp.int32)
        is_own = jnp.logical_and(place >= count, is_next == 0).astype(jnp.int32)
        is_far = jnp.logical_and(jnp.logical_and(place >= 0, is_own == 0), is_next == odd).astype(jnp.int32)
        is_chip = jnp.logical_and(place >= 0, is_far == 0).astype(jnp.int32)
        slot = place - count * is_own - 2 * count * is_next
        chip_list[n_chip] = ((slot * 2 + is_own) << OCTANT_BITS) + octant
        far_list[n_far] = (slot << OCTANT_BITS) + octant
        n_chip, n_far = n_chip + is_chip, n_far + is_far
    far_list[COUNTS + octants // OCTANTS] = n_far
    return n_chip


def put_average(tile_of, octant, held):
    lanes = lane_ids()
    start, oy, oz = octant_place(octant)
    here = ((lanes >> 4) & 1) == oz
    for t in range(2):
        at = pl.ds(pl.multiple_of(MARGIN + start + 8 * t, 8), 8)
        for s in range(4):
            lane = pl.ds(pl.multiple_of(oy * (S * H) + LANES * s, LANES), LANES)
            half = s // 2
            tile = tile_of(slice(8 * t, 8 * t + 8), slice(LANES * half, LANES * (half + 1)))
            moved = gather_lanes(tile, (s % 2) * 64 + (lanes >> 5) * H + (lanes & (H - 1)))
            held[at, lane] = jnp.where(here, moved, held[at, lane])


def merge_chip_kernel(parents, mid, own, near, held, far_list, covers, chip_list, *, boxes, octants):
    del mid
    find_boxes(parents, covers, boxes, octants)
    count = list_octants(covers, chip_list, far_list, own.shape[0], octants)

    @pl.loop(0, count)
    def _(n):
        entry = chip_list[n]
        is_own = ((entry >> OCTANT_BITS) & 1) == 1
        slot = entry >> (OCTANT_BITS + 1)
        put_average(
            lambda rows, lanes: jnp.where(is_own, own[slot, rows, lanes], near[slot, rows, lanes]),
            entry & ((1 << OCTANT_BITS) - 1),
            held,
        )


def merge_far_kernel(far_list, held_in, far, held, out_any, out_sems):
    del held_in
    stores = []
    for box in range(out_any.shape[0] // S):

        @pl.loop(far_list[COUNTS + box], far_list[COUNTS + box + 1])
        def _(n):
            entry = far_list[n]
            slot = entry >> OCTANT_BITS
            put_average(lambda rows, lanes: far[slot, rows, lanes], entry & ((1 << OCTANT_BITS) - 1), held)

        there = held.at[MARGIN + box * S : MARGIN + (box + 1) * S, :]
        stores.append(pltpu.make_async_copy(there, out_any.at[box * S : (box + 1) * S, :], out_sems.at[box]))
        stores[-1].start()
    for copy in stores:
        copy.wait()


def params():
    return pltpu.CompilerParams(vmem_limit_bytes=VMEM_LIMIT)


def cost(flops, size):
    return pl.CostEstimate(flops=flops, bytes_accessed=size, transcendentals=0)


def f32(*shape):
    return jax.ShapeDtypeStruct(shape, jnp.float32)


def vmem(*shape):
    return pltpu.VMEM(shape, jnp.float32)


def bf16(*shape):
    return pltpu.VMEM(shape, jnp.bfloat16)


def whole():
    return pl.BlockSpec(memory_space=pltpu.VMEM)


def on_device(coarse_dens, coarse_diff, coarse_pot, fine_dens, fine_diff, fine_pot, parents):
    devices = lax.axis_size("dev")
    groups = lax.axis_size("group")
    rows = coarse_dens.shape[0]
    boxes = fine_dens.shape[0] // S
    fine_rows = boxes * S
    octants = OCTANTS * (rows // S)
    wide = S * S
    smem = pl.BlockSpec(memory_space=pltpu.SMEM)
    anywhere = pl.BlockSpec(memory_space=pl.ANY)
    dma = pltpu.SemaphoreType.DMA
    near_pairs = [(i, i ^ 1) for i in range(devices)]
    far_pairs = [(i, (i + devices - 1 + 2 * (i & 1)) % devices) for i in range(devices)]

    def swap(near, far):
        got_far = lax.ppermute(far, "dev", far_pairs)
        return lax.ppermute(near, "dev", near_pairs), got_far

    near_edge, far_edge = pl.pallas_call(
        edges_kernel,
        grid=(1,),
        in_specs=[
            pl.BlockSpec((8, wide), lambda i: (0, 0)),
            pl.BlockSpec((16, wide), lambda i: (0, 0)),
            pl.BlockSpec((16, wide), lambda i: (0, 0)),
            pl.BlockSpec((8, wide), lambda i: (rows // 8 - 1, 0)),
            pl.BlockSpec((16, wide), lambda i: (rows // 16 - 1, 0)),
            pl.BlockSpec((16, wide), lambda i: (rows // 16 - 1, 0)),
        ],
        out_specs=[pl.BlockSpec((8, wide), lambda i: (0, 0))] * 2,
        out_shape=[f32(8, wide)] * 2,
        name="edges",
    )(coarse_dens, coarse_diff, coarse_pot, coarse_dens, coarse_diff, coarse_pot)
    near_edge, far_edge = swap(near_edge, far_edge)

    near_sum = neighbour_matrix()
    ext = f32(rows + 2 * MARGIN, wide)
    held_dens, mid = pl.pallas_call(
        coarse_kernel,
        in_specs=[whole()] * 4,
        out_specs=[whole()] * 2,
        scratch_shapes=[vmem(rows + 2 * MARGIN, wide)] * 2 + [bf16(4 * rows, wide), vmem(3 * rows, wide)],
        out_shape=[ext, ext],
        compiler_params=params(),
        cost_estimate=cost(rows * wide * 40, rows * wide * 12),
        name="coarse",
    )(coarse_dens, coarse_diff, coarse_pot, near_sum)

    packs = f32(boxes, PACK, LANES)
    _, mid, to_near, own, to_far = pl.pallas_call(
        functools.partial(rims_kernel, boxes=boxes),
        grid_spec=pltpu.PrefetchScalarGridSpec(
            num_scalar_prefetch=1,
            grid=(),
            in_specs=[whole()] * 6,
            out_specs=[whole()] * 5,
            scratch_shapes=[vmem(3, 24, wide), vmem(8, S * H)],
        ),
        out_shape=[ext, ext, packs, packs, packs],
        input_output_aliases={1: 0, 2: 1},
        compiler_params=params(),
        cost_estimate=cost(rows * wide * 8, rows * wide * 8),
        name="rims",
    )(parents, held_dens, mid, coarse_diff, coarse_pot, near_edge, far_edge)
    from_near, from_far = swap(to_near, to_far)

    fine_first, keep = pl.pallas_call(
        functools.partial(fine_first_kernel, boxes=boxes),
        in_specs=[whole()] * 4,
        out_specs=[whole()] * 2,
        scratch_shapes=[vmem(boxes, 48, wide)] * 4 + [bf16(4 * fine_rows, wide), vmem(3 * fine_rows, wide)],
        out_shape=[f32(fine_rows, wide)] * 2,
        compiler_params=params(),
        cost_estimate=cost(fine_rows * wide * 40, fine_rows * wide * 16),
        name="fine_first",
    )(fine_dens, fine_diff, fine_pot, near_sum)

    fine_out, averages = pl.pallas_call(
        functools.partial(fine_second_kernel, boxes=boxes, octants=octants),
        grid_spec=pltpu.PrefetchScalarGridSpec(
            num_scalar_prefetch=1,
            grid=(),
            in_specs=[whole()] * 10,
            out_specs=[anywhere, whole()],
            scratch_shapes=[vmem(boxes, 48, wide)] * 4
            + [
                vmem(boxes, 8, wide),
                bf16(4 * fine_rows, wide),
                vmem(2 * fine_rows, wide),
                vmem(2 * fine_rows, wide),
                bf16(2 * fine_rows, LANES),
                vmem(fine_rows, LANES),
                vmem(fine_rows, wide),
                vmem(2, fine_rows, LANES),
                dma((1,)),
            ],
        ),
        out_shape=[f32(fine_rows, wide), f32(boxes, H, H * H)],
        compiler_params=params(),
        cost_estimate=cost(fine_rows * wide * 60, fine_rows * wide * 16),
        name="fine_second",
    )(
        parents,
        fine_first,
        keep,
        fine_diff,
        fine_pot,
        near_sum,
        ghost_matrices(),
        average_matrix(),
        from_near,
        own,
        from_far,
    )

    pieces = [averages]
    for s in range(1, groups):
        pieces.append(lax.ppermute(averages, "group", [(i, (i + s) % groups) for i in range(groups)]))
    joined = pl.pallas_call(
        join_kernel,
        in_specs=[whole()] * groups,
        out_specs=whole(),
        out_shape=f32(groups * boxes, H, H * H),
        compiler_params=params(),
        name="join",
    )(*pieces)
    near_avg, far_avg = swap(joined, joined)

    def merge(kernel, count, out_specs, out_shape, scratch, name):
        return pl.pallas_call(
            kernel,
            grid_spec=pltpu.PrefetchScalarGridSpec(
                num_scalar_prefetch=1,
                grid=(),
                in_specs=[whole()] * (1 + count),
                out_specs=[whole()] + out_specs,
                scratch_shapes=scratch,
            ),
            out_shape=[ext] + out_shape,
            input_output_aliases={1: 0},
            compiler_params=params(),
            cost_estimate=cost(rows * wide * 4, rows * wide * 12),
            name=name,
        )

    far_list = jax.ShapeDtypeStruct((LIST,), jnp.int32)
    chip_kernel = functools.partial(merge_chip_kernel, boxes=boxes, octants=octants)
    lists = [pltpu.SMEM((octants + 1,), jnp.int32), pltpu.SMEM((LIST,), jnp.int32)]
    held, far_list = merge(chip_kernel, 2, [smem], [far_list], lists, "merge_chip")(parents, mid, joined, near_avg)
    _, coarse_out = merge(merge_far_kernel, 1, [anywhere], [f32(rows, wide)], [dma((rows // S,))], "merge_far")(
        far_list, held, far_avg
    )
    return coarse_out, fine_out


def solution(mesh):
    in_specs = (
        P("dev", None),
        P("dev", None),
        P("dev", None),
        P(("group", "dev"), None),
        P(("group", "dev"), None),
        P(("group", "dev"), None),
        P(),
    )
    out_specs = (P("dev", None), P(("group", "dev"), None))
    return jax.shard_map(on_device, mesh=mesh, in_specs=in_specs, out_specs=out_specs, check_vma=False)
```

```python
import functools

import jax
import jax.numpy as jnp
import numpy as np
from jax import lax
from jax.experimental import pallas as pl
from jax.experimental.pallas import tpu as pltpu
from jax.sharding import PartitionSpec as P

S = 32
H = 16
LANES = 128
GROUPS = 8
OCTANTS = 8
MARGIN = 16
PACK = 24
RATE = 0.06
VMEM_LIMIT = 32 * 1024 * 1024


def neighbour_matrix():
    source, target = np.arange(512)[:, None] - LANES, np.arange(256)[None, :]
    step = source - target
    same_y = source // S == target // S
    return jnp.asarray((np.abs(step) == S) | ((np.abs(step) == 1) & same_y), jnp.bfloat16)


def ghost_matrices():
    source, target = np.arange(LANES)[:, None], np.arange(S * S)[None, :]
    part, place = (source >> 4) & 3, source & (H - 1)
    y, z = target // S, target % S
    faces = (
        ((part == 0) & (z == S - 1) & (y // 2 == place))
        | ((part == 1) & (z == 0) & (y // 2 == place))
        | ((part == 2) & (y == S - 1) & (z // 2 == place))
        | ((part == 3) & (y == 0) & (z // 2 == place))
    )
    return jnp.asarray(np.stack([faces & (source // 64 == step) for step in range(2)]), jnp.bfloat16)


def average_matrix():
    source, target = np.arange(S * S)[:, None], np.arange(H * H)[None, :]
    return jnp.asarray((source // S // 2 == target // H) & (source % S // 2 == target % H), jnp.bfloat16)


def pieces_of(value):
    high = value.astype(jnp.bfloat16)
    return high, (value - high.astype(jnp.float32)).astype(jnp.bfloat16)


def windows():
    for n in range(4):
        low, high = max(256 * n - LANES, 0), min(256 * n + 256 + LANES, S * S)
        first = low - (256 * n - LANES)
        yield slice(low, high), slice(first, first + high - low), slice(256 * n, 256 * n + 256)


def product(left, right):
    return jnp.dot(left, right, preferred_element_type=jnp.float32)


def sides():
    dev, devices = lax.axis_index("dev"), lax.axis_size("dev")
    odd = dev & 1
    near = dev + 1 - 2 * odd
    far = lax.rem(dev + devices - 1 + 2 * odd, devices)
    return dev, near, far, odd


def edge_count():
    lane = lax.broadcasted_iota(jnp.int32, (1, S * S), 1)
    z, y = lane & (S - 1), lane >> 5
    return sum((at == end).astype(jnp.float32) for at in (z, y) for end in (0, S - 1))


def lane_ids():
    return lax.broadcasted_iota(jnp.int32, (8, LANES), 1)


def row_ids():
    return lax.broadcasted_iota(jnp.int32, (8, LANES), 0)


def gather_lanes(tile, index):
    return jnp.take_along_axis(tile, index, axis=1, mode="promise_in_bounds")


def lane_groups(ref, row):
    return [ref[row : row + 8, LANES * j : LANES * (j + 1)] for j in range(GROUPS)]


def sum_yz(tiles, lanes, edge):
    z = lanes & (S - 1)
    up = [pltpu.roll(t, S, 1) for t in tiles]
    down = [pltpu.roll(t, LANES - S, 1) for t in tiles]
    out = []
    for j, tile in enumerate(tiles):
        fill = tile if edge else jnp.zeros_like(tile)
        low = jnp.where(lanes >= S, up[j], up[j - 1] if j > 0 else fill)
        high = jnp.where(lanes < LANES - S, down[j], down[j + 1] if j + 1 < GROUPS else fill)
        left = jnp.where(z != 0, pltpu.roll(tile, 1, 1), fill)
        right = jnp.where(z != S - 1, pltpu.roll(tile, LANES - 1, 1), fill)
        out.append((low + high) + (left + right))
    return out


def octant_place(local_id):
    box = local_id >> 3
    return box * S + ((local_id >> 2) & 1) * H, (local_id >> 1) & 1, local_id & 1


def edges_kernel(u0, k0, v0, u1, k1, v1, near_ref, far_ref):
    _, _, _, odd = sides()
    first = (u0[0:2, :], k0[...].astype(jnp.float32)[0:2, :], v0[...].astype(jnp.float32)[0:2, :])
    last = (u1[6:8, :], k1[...].astype(jnp.float32)[14:16, :], v1[...].astype(jnp.float32)[14:16, :])
    is_odd = odd == 1
    for n, (low, high) in enumerate(zip(first, last)):
        near_ref[2 * n : 2 * n + 2, :] = jnp.where(is_odd, low, high)
        far_ref[2 * n : 2 * n + 2, :] = jnp.where(is_odd, high, low)
    for ref in (near_ref, far_ref):
        ref[6:8, :] = jnp.zeros((2, S * S), jnp.float32)


def pack_rims(old, mid, xs, pack_ref, slot, local_id, base):
    lanes, rows = lane_ids(), row_ids()
    start, oy, oz = octant_place(local_id)
    start = start + base
    half = pl.multiple_of(oy * (S * H), LANES)
    for n, (ref, shift, row) in enumerate(((old, -8, 7), (old, H, 0), (mid, -8, 7), (mid, H, 0))):
        tile = ref[pl.ds(pl.multiple_of(start + shift, 8), 8), pl.ds(half, S * H)]
        line = tile[row : row + 1, :]
        xs[n : n + 1, :] = line
        xs[n + 4 : n + 5, :] = line
    index_x = ((lanes >> 4) & 3) * S + oz * H + (lanes & (H - 1))
    picked = [gather_lanes(xs[:, LANES * s : LANES * (s + 1)], index_x) for s in range(4)]
    low = jnp.where(lanes < 64, picked[0], picked[1])
    high = jnp.where(lanes < 64, picked[2], picked[3])
    faces = jnp.where(rows < 4, low, high)
    mean = 0.5 * (faces + pltpu.roll(faces, 2, 0))
    pack_ref[slot, 0:8, :] = jnp.where((rows & 2) == 0, faces, mean)
    index_y = oy * (LANES - S) + oz * H + (lanes & (H - 1))
    index_z = (lanes & 3) * S + H - oz
    y_group = pl.multiple_of(S * H - LANES * oy, LANES)
    for t in range(2):
        at = pl.multiple_of(start + 8 * t, 8)
        values = []
        for ref in (old, mid):
            y_face = gather_lanes(ref[pl.ds(at, 8), pl.ds(y_group, LANES)], index_y)
            parts = [
                gather_lanes(ref[pl.ds(at, 8), pl.ds(pl.multiple_of(half + LANES * s, LANES), LANES)], index_z)
                for s in range(4)
            ]
            which = (lanes >> 2) & 3
            z_face = jnp.where(
                which < 2,
                jnp.where(which == 0, parts[0], parts[1]),
                jnp.where(which == 2, parts[2], parts[3]),
            )
            values.append(jnp.where((lanes & S) == 0, z_face, y_face))
        face = jnp.where(lanes < 64, values[0], 0.5 * (values[0] + values[1]))
        used = ((lanes >> 4) & 1) == jnp.where((lanes & S) == 0, oz, oy)
        pack_ref[slot, 8 + 8 * t : 16 + 8 * t, :] = jnp.where(used, face, 0.0)


def find_boxes(parents, covers, boxes, octants):
    dev, devices = lax.axis_index("dev"), lax.axis_size("dev")
    group, groups = lax.axis_index("group"), lax.axis_size("group")
    for n in range(octants + 1):
        covers[n] = jnp.int32(-1)
    for r in range(3):
        source = lax.rem(dev + devices + r - 1, devices)
        for s in range(groups):
            first = ((group ^ s) * devices + source) * boxes
            for k in range(boxes):
                local_id = parents[first + k] - dev * octants
                inside = jnp.logical_and(local_id >= 0, local_id < octants)
                covers[jnp.where(inside, local_id, octants)] = jnp.int32((r * groups + s) * boxes + k)


def step_tile(uc, pc, qc, ul, pll, ql, uh, ph, qh, lanes):
    sum_u = sum_yz(uc, lanes, False)
    sum_w = sum_yz([a * b for a, b in zip(pc, uc)], lanes, False)
    sum_q = sum_yz(qc, lanes, True)
    out = []
    for j in range(GROUPS):
        keep = (1.0 - 6.0 * pc[j]) - (sum_q[j] + (ql[j] + qh[j]))
        near_u = sum_u[j] + (ul[j] + uh[j])
        near_w = sum_w[j] + (pll[j] * ul[j] + ph[j] * uh[j])
        out.append(keep * uc[j] + (qc[j] * near_u + near_w))
    return out


def coarse_kernel(u_ref, k_ref, v_ref, near_sum, u, mid_out, p, q, split, sums):
    rows, wide = u_ref.shape
    base = MARGIN
    rate = 0.5 * RATE
    for ref in (u, p, q):
        for row in (base - 8, base + rows):
            ref[row : row + 8, :] = jnp.zeros((8, wide), jnp.float32)

    @pl.loop(0, rows // 16, unroll=True)
    def _(i):
        at = pl.multiple_of(i * 16, 16)
        to = pl.multiple_of(base + i * 16, 8)
        diff = rate * k_ref[pl.ds(at, 16), :].astype(jnp.float32)
        pot = rate * v_ref[pl.ds(at, 16), :].astype(jnp.float32)
        dens = u_ref[pl.ds(at, 16), :]
        u[pl.ds(to, 16), :] = dens
        p[pl.ds(to, 16), :] = diff + pot
        q[pl.ds(to, 16), :] = diff - pot
        store_split(split, rows, at, dens, (diff + pot) * dens)

    for window, part, out in windows():
        near = near_sum[part, :]
        sums[0:rows, out] = rate * (product(k_ref[:, window], near) - product(v_ref[:, window], near))
        sums[rows : 3 * rows, out] = product_of_split(split, near, window)

    ends = edge_count()

    @pl.loop(0, rows // 8, unroll=True)
    def _(i):
        at = pl.multiple_of(i * 8, 8)
        uv, pv, qv = (ref.at[pl.ds(pl.multiple_of(at + base - 8, 8), 24), :] for ref in (u, p, q))
        sum_q, sum_u, sum_w = (sums[pl.ds(pl.multiple_of(n * rows + at, 8), 8), :] for n in range(3))
        uc, pc, qc = (view[8:16, :] for view in (uv, pv, qv))
        ul, uh = uv[7:15, :], uv[9:17, :]
        keep = (1.0 - 6.0 * pc) - (sum_q + ends * qc + (qv[7:15, :] + qv[9:17, :]))
        near_u = sum_u + (ul + uh)
        near_w = sum_w + (pv[7:15, :] * ul + pv[9:17, :] * uh)
        mid_out[pl.ds(pl.multiple_of(at + base, 8), 8), :] = keep * uc + (qc * near_u + near_w)


def rims_kernel(parents, u_in, mid_in, k_ref, v_ref, near_edge, far_edge, u, m, to_near, to_own, to_far, e, xs, *, boxes):
    del u_in, mid_in
    base = MARGIN
    rows = u.shape[0] - 2 * base
    rate = 0.5 * RATE
    devices = lax.axis_size("dev")
    dev, near_dev, far_dev, odd = sides()
    group = lax.axis_index("group")
    octants = OCTANTS * (rows // S)
    lanes = lane_ids()
    before = jnp.where(odd == 1, near_edge[...], far_edge[...])
    after = jnp.where(odd == 1, far_edge[...], near_edge[...])
    u[base - 2 : base, :] = before[0:2, :]
    u[base + rows : base + rows + 2, :] = after[0:2, :]
    for n, (far, end, own, top) in enumerate(((before, 0, 0, base - 2), (after, rows - 16, 14, base + rows - 2))):
        e[0, 7:11, :] = u[top : top + 4, :]
        own_diff = rate * k_ref[end : end + 16, :].astype(jnp.float32)[own : own + 2, :]
        own_pot = rate * v_ref[end : end + 16, :].astype(jnp.float32)[own : own + 2, :]
        far_diff, far_pot = rate * far[2:4, :], rate * far[4:6, :]
        there, here = (7, 9) if n == 0 else (9, 7)
        e[1, there : there + 2, :] = far_diff + far_pot
        e[2, there : there + 2, :] = far_diff - far_pot
        e[1, here : here + 2, :] = own_diff + own_pot
        e[2, here : here + 2, :] = own_diff - own_pot
        tiles = [lane_groups(e.at[f], row) for row in (8, 7, 9) for f in range(3)]
        for j, new in enumerate(step_tile(*tiles, lanes)):
            m[top + 1 : top + 3, LANES * j : LANES * (j + 1)] = new[0:2, :]
    for ref, target in ((to_far, far_dev), (to_near, near_dev), (to_own, dev)):
        for k in range(boxes):
            local_id = parents[(group * devices + target) * boxes + k] - dev * octants
            local_id = jnp.minimum(jnp.maximum(local_id, 0), octants - 1)
            pack_rims(u, m, xs, ref, k, local_id, base)


def fine_rates(k_ref, v_ref, at):
    diff = RATE * k_ref[pl.ds(at, 16), :].astype(jnp.float32)
    pot = (0.5 * RATE) * v_ref[pl.ds(at, 16), :].astype(jnp.float32)
    return diff + pot, diff - pot


def store_split(split, rows, at, *values):
    pairs = [pieces_of(value) for value in values]
    for n, part in enumerate([high for high, _ in pairs] + [low for _, low in pairs]):
        split[pl.ds(pl.multiple_of(n * rows + at, 16), 16), :] = part


def product_of_split(split, matrix, window=slice(None)):
    half = split.shape[0] // 2
    both = product(split[:, window], matrix)
    return both[0:half] + both[half : 2 * half]


def fine_first_kernel(u_ref, k_ref, v_ref, near_sum, out_ref, keep_ref, u, w, p, q, split, sums, *, boxes):
    rows, wide = out_ref.shape
    base = 8
    @pl.loop(0, boxes, unroll=True)
    def _(k):
        for ref in (u, w):
            for ghost in (7, 40):
                ref[k, ghost : ghost + 1, :] = jnp.zeros((1, wide), jnp.float32)
        for i in range(2):
            at, to = pl.multiple_of(S * k + 16 * i, 16), base + 16 * i
            pc, qc = fine_rates(k_ref, v_ref, at)
            dens = u_ref[pl.ds(at, 16), :]
            p[k, to : to + 16, :] = pc
            q[k, to : to + 16, :] = qc
            u[k, to : to + 16, :] = dens
            w[k, to : to + 16, :] = pc * dens
            store_split(split, rows, at, dens, pc * dens)
        for ghost, cell in ((7, 8), (40, 39)):
            q[k, ghost : ghost + 1, :] = q[k, cell : cell + 1, :]

    for window, part, out in windows():
        near = near_sum[part, :]
        sums[0 : 2 * rows, out] = product_of_split(split, near, window)
        sums[2 * rows : 3 * rows, out] = RATE * product(k_ref[:, window], near) - (0.5 * RATE) * product(
            v_ref[:, window], near
        )
    ends = edge_count()

    @pl.loop(0, boxes, unroll=True)
    def _(k):
        for i in range(2):
            at, to = pl.multiple_of(S * k + 16 * i, 16), base + 16 * i
            here, low, high = (slice(to + m, to + m + 16) for m in (0, -1, 1))
            sum_u, sum_w, sum_q = (
                sums[pl.ds(pl.multiple_of(n * rows + at, 16), 16), :] + (ref[k, low, :] + ref[k, high, :])
                for n, ref in enumerate((u, w, q))
            )
            qc = q[k, here, :]
            stay = (1.0 - 6.0 * p[k, here, :]) - (sum_q + ends * qc)
            keep_ref[pl.ds(at, 16), :] = stay
            out_ref[pl.ds(at, 16), :] = stay * u[k, here, :] + (qc * sum_u + sum_w)


def fine_second_kernel(parents, first, keep, k_ref, v_ref, near_sum, ghost_sum, block_sum, from_near, from_own, from_far, out_any, avg_ref, u, w, p, q, lines, split, sums, ghosts, faces, dup, res, means, out_sems, *, boxes, octants):
    devices = lax.axis_size("dev")
    dev, near_dev, _, _ = sides()
    group = lax.axis_index("group")
    rows, wide = res.shape
    base = 8
    lanes = lane_ids()
    z = lanes & (S - 1)
    for k in range(boxes):
        parent = parents[(group * devices + dev) * boxes + k]
        own_id, near_id = parent - dev * octants, parent - near_dev * octants
        is_own = jnp.logical_and(own_id >= 0, own_id < octants)
        is_near = jnp.logical_and(near_id >= 0, near_id < octants)

        def chosen(n):
            there = slice(8 * n, 8 * n + 8)
            other = jnp.where(is_near, from_near[k, there, :], from_far[k, there, :])
            return jnp.where(is_own, from_own[k, there, :], other)

        for n in range(2):
            face = chosen(n + 1)
            dup[pl.ds(S * k + 16 * n, 8, 2), :] = face
            dup[pl.ds(S * k + 16 * n + 1, 8, 2), :] = face
        for n, part in enumerate(pieces_of(dup[S * k : S * k + S, :])):
            faces[n * rows + S * k : n * rows + S * k + S, :] = part
        x_faces = chosen(0)
        for n in range(4):
            spread = gather_lanes(x_faces, (2 * n + (lanes >> 6)) * H + (z >> 1))
            for half in range(2):
                j = 4 * half + n
                there = slice(LANES * j, LANES * (j + 1))
                lines[k, 0:2, there] = spread[4 * half : 4 * half + 2, :]
                u[k, 7:8, there] = spread[4 * half + 2 : 4 * half + 3, :]
                u[k, 40:41, there] = spread[4 * half + 3 : 4 * half + 4, :]
    for n in range(4):
        out = slice(256 * n, 256 * n + 256)
        for step in range(2):
            ghosts[step * rows : (step + 1) * rows, out] = product_of_split(faces, ghost_sum[step, :, out])
    row = lax.broadcasted_iota(jnp.int32, (16, wide), 0)

    @pl.loop(0, boxes, unroll=True)
    def _(k):
        for i in range(2):
            at, to = pl.multiple_of(S * k + 16 * i, 16), base + 16 * i
            pc, qc = fine_rates(k_ref, v_ref, at)
            beside = ghosts[pl.ds(at, 16), :] + jnp.where(row == 15 * i, lines[k, i : i + 1, :], 0.0)
            new = first[pl.ds(at, 16), :] + (pc + qc) * beside
            p[k, to : to + 16, :] = pc
            q[k, to : to + 16, :] = qc
            u[k, to : to + 16, :] = new
            w[k, to : to + 16, :] = pc * new
            store_split(split, rows, at, new, pc * new)
        for ghost, cell in ((7, 8), (40, 39)):
            w[k, ghost : ghost + 1, :] = p[k, cell : cell + 1, :] * u[k, ghost : ghost + 1, :]

    for window, part, out in windows():
        sums[:, out] = product_of_split(split, near_sum[part, :], window)

    @pl.loop(0, boxes, unroll=True)
    def _(k):
        for i in range(2):
            at, to = pl.multiple_of(S * k + 16 * i, 16), base + 16 * i
            here, low, high = (slice(to + m, to + m + 16) for m in (0, -1, 1))
            sum_u, sum_w = (
                sums[pl.ds(pl.multiple_of(n * rows + at, 16), 16), :] + (ref[k, low, :] + ref[k, high, :])
                for n, ref in enumerate((u, w))
            )
            pc, qc = p[k, here, :], q[k, here, :]
            beside = ghosts[pl.ds(pl.multiple_of(rows + at, 16), 16), :]
            new = (keep[pl.ds(at, 16), :] * u[k, here, :] + (qc * sum_u + sum_w)) + (pc + qc) * beside
            res[pl.ds(at, 16), :] = new
            store_split(split, rows, at, new)

    out_copy = pltpu.make_async_copy(res, out_any, out_sems.at[0])
    out_copy.start()
    total = product_of_split(split.at[0 : 2 * rows, :], block_sum[...])
    for half in range(2):
        means[half, :, :] = total[:, LANES * half : LANES * (half + 1)]
    for half in range(2):
        for k in range(boxes):
            for t in range(2):
                at = S * k + 16 * t
                pair = means[half, pl.ds(at, 8, 2), :] + means[half, pl.ds(at + 1, 8, 2), :]
                avg_ref[k, 8 * t : 8 * t + 8, LANES * half : LANES * (half + 1)] = 0.125 * pair
    out_copy.wait()


def join_kernel(*refs):
    *pieces, out_ref = refs
    count = pieces[0].shape[0]
    for n, piece in enumerate(pieces):
        out_ref[n * count : (n + 1) * count] = piece[...]


LIST = 64
COUNTS = 50
OCTANT_BITS = 7


def list_octants(covers, chip_list, far_list, count, octants):
    _, _, _, odd = sides()
    n_chip = n_far = jnp.int32(0)
    for octant in range(octants):
        if octant % OCTANTS == 0:
            far_list[COUNTS + octant // OCTANTS] = n_far
        place = covers[octant]
        is_next = (place >= 2 * count).astype(jnp.int32)
        is_own = jnp.logical_and(place >= count, is_next == 0).astype(jnp.int32)
        is_far = jnp.logical_and(jnp.logical_and(place >= 0, is_own == 0), is_next == odd).astype(jnp.int32)
        is_chip = jnp.logical_and(place >= 0, is_far == 0).astype(jnp.int32)
        slot = place - count * is_own - 2 * count * is_next
        chip_list[n_chip] = ((slot * 2 + is_own) << OCTANT_BITS) + octant
        far_list[n_far] = (slot << OCTANT_BITS) + octant
        n_chip, n_far = n_chip + is_chip, n_far + is_far
    far_list[COUNTS + octants // OCTANTS] = n_far
    return n_chip


def put_average(tile_of, octant, held):
    lanes = lane_ids()
    start, oy, oz = octant_place(octant)
    here = ((lanes >> 4) & 1) == oz
    for t in range(2):
        at = pl.ds(pl.multiple_of(MARGIN + start + 8 * t, 8), 8)
        for s in range(4):
            lane = pl.ds(pl.multiple_of(oy * (S * H) + LANES * s, LANES), LANES)
            half = s // 2
            tile = tile_of(slice(8 * t, 8 * t + 8), slice(LANES * half, LANES * (half + 1)))
            moved = gather_lanes(tile, (s % 2) * 64 + (lanes >> 5) * H + (lanes & (H - 1)))
            held[at, lane] = jnp.where(here, moved, held[at, lane])


def merge_chip_kernel(parents, mid, own, near, held, far_list, covers, chip_list, *, boxes, octants):
    del mid
    find_boxes(parents, covers, boxes, octants)
    count = list_octants(covers, chip_list, far_list, own.shape[0], octants)

    @pl.loop(0, count)
    def _(n):
        entry = chip_list[n]
        is_own = ((entry >> OCTANT_BITS) & 1) == 1
        slot = entry >> (OCTANT_BITS + 1)
        put_average(
            lambda rows, lanes: jnp.where(is_own, own[slot, rows, lanes], near[slot, rows, lanes]),
            entry & ((1 << OCTANT_BITS) - 1),
            held,
        )


def merge_far_kernel(far_list, held_in, far, held, out_any, out_sems):
    del held_in
    stores = []
    for box in range(out_any.shape[0] // S):

        @pl.loop(far_list[COUNTS + box], far_list[COUNTS + box + 1])
        def _(n):
            entry = far_list[n]
            slot = entry >> OCTANT_BITS
            put_average(lambda rows, lanes: far[slot, rows, lanes], entry & ((1 << OCTANT_BITS) - 1), held)

        there = held.at[MARGIN + box * S : MARGIN + (box + 1) * S, :]
        stores.append(pltpu.make_async_copy(there, out_any.at[box * S : (box + 1) * S, :], out_sems.at[box]))
        stores[-1].start()
    for copy in stores:
        copy.wait()


def params():
    return pltpu.CompilerParams(vmem_limit_bytes=VMEM_LIMIT)


def cost(flops, size):
    return pl.CostEstimate(flops=flops, bytes_accessed=size, transcendentals=0)


def f32(*shape):
    return jax.ShapeDtypeStruct(shape, jnp.float32)


def vmem(*shape):
    return pltpu.VMEM(shape, jnp.float32)


def bf16(*shape):
    return pltpu.VMEM(shape, jnp.bfloat16)


def whole():
    return pl.BlockSpec(memory_space=pltpu.VMEM)


def on_device(coarse_dens, coarse_diff, coarse_pot, fine_dens, fine_diff, fine_pot, parents):
    devices = lax.axis_size("dev")
    groups = lax.axis_size("group")
    rows = coarse_dens.shape[0]
    boxes = fine_dens.shape[0] // S
    fine_rows = boxes * S
    octants = OCTANTS * (rows // S)
    wide = S * S
    smem = pl.BlockSpec(memory_space=pltpu.SMEM)
    anywhere = pl.BlockSpec(memory_space=pl.ANY)
    dma = pltpu.SemaphoreType.DMA
    near_pairs = [(i, i ^ 1) for i in range(devices)]
    far_pairs = [(i, (i + devices - 1 + 2 * (i & 1)) % devices) for i in range(devices)]

    def swap(near, far):
        got_far = lax.ppermute(far, "dev", far_pairs)
        return lax.ppermute(near, "dev", near_pairs), got_far

    near_edge, far_edge = pl.pallas_call(
        edges_kernel,
        grid=(1,),
        in_specs=[
            pl.BlockSpec((8, wide), lambda i: (0, 0)),
            pl.BlockSpec((16, wide), lambda i: (0, 0)),
            pl.BlockSpec((16, wide), lambda i: (0, 0)),
            pl.BlockSpec((8, wide), lambda i: (rows // 8 - 1, 0)),
            pl.BlockSpec((16, wide), lambda i: (rows // 16 - 1, 0)),
            pl.BlockSpec((16, wide), lambda i: (rows // 16 - 1, 0)),
        ],
        out_specs=[pl.BlockSpec((8, wide), lambda i: (0, 0))] * 2,
        out_shape=[f32(8, wide)] * 2,
        name="edges",
    )(coarse_dens, coarse_diff, coarse_pot, coarse_dens, coarse_diff, coarse_pot)
    near_edge, far_edge = swap(near_edge, far_edge)

    near_sum = neighbour_matrix()
    ext = f32(rows + 2 * MARGIN, wide)
    held_dens, mid = pl.pallas_call(
        coarse_kernel,
        in_specs=[whole()] * 4,
        out_specs=[whole()] * 2,
        scratch_shapes=[vmem(rows + 2 * MARGIN, wide)] * 2 + [bf16(4 * rows, wide), vmem(3 * rows, wide)],
        out_shape=[ext, ext],
        compiler_params=params(),
        cost_estimate=cost(rows * wide * 40, rows * wide * 12),
        name="coarse",
    )(coarse_dens, coarse_diff, coarse_pot, near_sum)

    packs = f32(boxes, PACK, LANES)
    _, mid, to_near, own, to_far = pl.pallas_call(
        functools.partial(rims_kernel, boxes=boxes),
        grid_spec=pltpu.PrefetchScalarGridSpec(
            num_scalar_prefetch=1,
            grid=(),
            in_specs=[whole()] * 6,
            out_specs=[whole()] * 5,
            scratch_shapes=[vmem(3, 24, wide), vmem(8, S * H)],
        ),
        out_shape=[ext, ext, packs, packs, packs],
        input_output_aliases={1: 0, 2: 1},
        compiler_params=params(),
        cost_estimate=cost(rows * wide * 8, rows * wide * 8),
        name="rims",
    )(parents, held_dens, mid, coarse_diff, coarse_pot, near_edge, far_edge)
    from_near, from_far = swap(to_near, to_far)

    fine_first, keep = pl.pallas_call(
        functools.partial(fine_first_kernel, boxes=boxes),
        in_specs=[whole()] * 4,
        out_specs=[whole()] * 2,
        scratch_shapes=[vmem(boxes, 48, wide)] * 4 + [bf16(4 * fine_rows, wide), vmem(3 * fine_rows, wide)],
        out_shape=[f32(fine_rows, wide)] * 2,
        compiler_params=params(),
        cost_estimate=cost(fine_rows * wide * 40, fine_rows * wide * 16),
        name="fine_first",
    )(fine_dens, fine_diff, fine_pot, near_sum)

    fine_out, averages = pl.pallas_call(
        functools.partial(fine_second_kernel, boxes=boxes, octants=octants),
        grid_spec=pltpu.PrefetchScalarGridSpec(
            num_scalar_prefetch=1,
            grid=(),
            in_specs=[whole()] * 10,
            out_specs=[anywhere, whole()],
            scratch_shapes=[vmem(boxes, 48, wide)] * 4
            + [
                vmem(boxes, 8, wide),
                bf16(4 * fine_rows, wide),
                vmem(2 * fine_rows, wide),
                vmem(2 * fine_rows, wide),
                bf16(2 * fine_rows, LANES),
                vmem(fine_rows, LANES),
                vmem(fine_rows, wide),
                vmem(2, fine_rows, LANES),
                dma((1,)),
            ],
        ),
        out_shape=[f32(fine_rows, wide), f32(boxes, H, H * H)],
        compiler_params=params(),
        cost_estimate=cost(fine_rows * wide * 60, fine_rows * wide * 16),
        name="fine_second",
    )(
        parents,
        fine_first,
        keep,
        fine_diff,
        fine_pot,
        near_sum,
        ghost_matrices(),
        average_matrix(),
        from_near,
        own,
        from_far,
    )

    pieces = [averages]
    for s in range(1, groups):
        pieces.append(lax.ppermute(averages, "group", [(i, i ^ s) for i in range(groups)]))
    joined = pl.pallas_call(
        join_kernel,
        in_specs=[whole()] * groups,
        out_specs=whole(),
        out_shape=f32(groups * boxes, H, H * H),
        compiler_params=params(),
        name="join",
    )(*pieces)
    near_avg, far_avg = swap(joined, joined)

    def merge(kernel, count, out_specs, out_shape, scratch, name):
        return pl.pallas_call(
            kernel,
            grid_spec=pltpu.PrefetchScalarGridSpec(
                num_scalar_prefetch=1,
                grid=(),
                in_specs=[whole()] * (1 + count),
                out_specs=[whole()] + out_specs,
                scratch_shapes=scratch,
            ),
            out_shape=[ext] + out_shape,
            input_output_aliases={1: 0},
            compiler_params=params(),
            cost_estimate=cost(rows * wide * 4, rows * wide * 12),
            name=name,
        )

    far_list = jax.ShapeDtypeStruct((LIST,), jnp.int32)
    chip_kernel = functools.partial(merge_chip_kernel, boxes=boxes, octants=octants)
    lists = [pltpu.SMEM((octants + 1,), jnp.int32), pltpu.SMEM((LIST,), jnp.int32)]
    held, far_list = merge(chip_kernel, 2, [smem], [far_list], lists, "merge_chip")(parents, mid, joined, near_avg)
    _, coarse_out = merge(merge_far_kernel, 1, [anywhere], [f32(rows, wide)], [dma((rows // S,))], "merge_far")(
        far_list, held, far_avg
    )
    return coarse_out, fine_out


def solution(mesh):
    in_specs = (
        P("dev", None),
        P("dev", None),
        P("dev", None),
        P(("group", "dev"), None),
        P(("group", "dev"), None),
        P(("group", "dev"), None),
        P(),
    )
    out_specs = (P("dev", None), P(("group", "dev"), None))
    return jax.shard_map(on_device, mesh=mesh, in_specs=in_specs, out_specs=out_specs, check_vma=False)
```

```python
import functools

import jax
import jax.numpy as jnp
import numpy as np
from jax import lax
from jax.experimental import pallas as pl
from jax.experimental.pallas import tpu as pltpu
from jax.sharding import PartitionSpec as P

S = 32
H = 16
LANES = 128
GROUPS = 8
OCTANTS = 8
MARGIN = 16
PACK = 24
RATE = 0.06
VMEM_LIMIT = 32 * 1024 * 1024


def neighbour_matrix():
    source, target = np.arange(512)[:, None] - LANES, np.arange(256)[None, :]
    step = source - target
    same_y = source // S == target // S
    return jnp.asarray((np.abs(step) == S) | ((np.abs(step) == 1) & same_y), jnp.bfloat16)


def ghost_matrices():
    source, target = np.arange(LANES)[:, None], np.arange(S * S)[None, :]
    part, place = (source >> 4) & 3, source & (H - 1)
    y, z = target // S, target % S
    faces = (
        ((part == 0) & (z == S - 1) & (y // 2 == place))
        | ((part == 1) & (z == 0) & (y // 2 == place))
        | ((part == 2) & (y == S - 1) & (z // 2 == place))
        | ((part == 3) & (y == 0) & (z // 2 == place))
    )
    return jnp.asarray(np.stack([faces & (source // 64 == step) for step in range(2)]), jnp.bfloat16)


def average_matrix():
    source, target = np.arange(S * S)[:, None], np.arange(H * H)[None, :]
    return jnp.asarray((source // S // 2 == target // H) & (source % S // 2 == target % H), jnp.bfloat16)


def pieces_of(value):
    high = value.astype(jnp.bfloat16)
    return high, (value - high.astype(jnp.float32)).astype(jnp.bfloat16)


def windows():
    for n in range(4):
        low, high = max(256 * n - LANES, 0), min(256 * n + 256 + LANES, S * S)
        first = low - (256 * n - LANES)
        yield slice(low, high), slice(first, first + high - low), slice(256 * n, 256 * n + 256)


def product(left, right):
    return jnp.dot(left, right, preferred_element_type=jnp.float32)


def sides():
    dev, devices = lax.axis_index("dev"), lax.axis_size("dev")
    odd = dev & 1
    near = dev + 1 - 2 * odd
    far = lax.rem(dev + devices - 1 + 2 * odd, devices)
    return dev, near, far, odd


def edge_count():
    lane = lax.broadcasted_iota(jnp.int32, (1, S * S), 1)
    z, y = lane & (S - 1), lane >> 5
    return sum((at == end).astype(jnp.float32) for at in (z, y) for end in (0, S - 1))


def lane_ids():
    return lax.broadcasted_iota(jnp.int32, (8, LANES), 1)


def row_ids():
    return lax.broadcasted_iota(jnp.int32, (8, LANES), 0)


def gather_lanes(tile, index):
    return jnp.take_along_axis(tile, index, axis=1, mode="promise_in_bounds")


def lane_groups(ref, row):
    return [ref[row : row + 8, LANES * j : LANES * (j + 1)] for j in range(GROUPS)]


def sum_yz(tiles, lanes, edge):
    z = lanes & (S - 1)
    up = [pltpu.roll(t, S, 1) for t in tiles]
    down = [pltpu.roll(t, LANES - S, 1) for t in tiles]
    out = []
    for j, tile in enumerate(tiles):
        fill = tile if edge else jnp.zeros_like(tile)
        low = jnp.where(lanes >= S, up[j], up[j - 1] if j > 0 else fill)
        high = jnp.where(lanes < LANES - S, down[j], down[j + 1] if j + 1 < GROUPS else fill)
        left = jnp.where(z != 0, pltpu.roll(tile, 1, 1), fill)
        right = jnp.where(z != S - 1, pltpu.roll(tile, LANES - 1, 1), fill)
        out.append((low + high) + (left + right))
    return out


def octant_place(local_id):
    box = local_id >> 3
    return box * S + ((local_id >> 2) & 1) * H, (local_id >> 1) & 1, local_id & 1


def edges_kernel(u0, k0, v0, u1, k1, v1, near_ref, far_ref):
    _, _, _, odd = sides()
    first = (u0[0:2, :], k0[...].astype(jnp.float32)[0:2, :], v0[...].astype(jnp.float32)[0:2, :])
    last = (u1[6:8, :], k1[...].astype(jnp.float32)[14:16, :], v1[...].astype(jnp.float32)[14:16, :])
    is_odd = odd == 1
    for n, (low, high) in enumerate(zip(first, last)):
        near_ref[2 * n : 2 * n + 2, :] = jnp.where(is_odd, low, high)
        far_ref[2 * n : 2 * n + 2, :] = jnp.where(is_odd, high, low)
    for ref in (near_ref, far_ref):
        ref[6:8, :] = jnp.zeros((2, S * S), jnp.float32)


def pack_rims(old, mid, xs, pack_ref, slot, local_id, base):
    lanes, rows = lane_ids(), row_ids()
    start, oy, oz = octant_place(local_id)
    start = start + base
    half = pl.multiple_of(oy * (S * H), LANES)
    for n, (ref, shift, row) in enumerate(((old, -8, 7), (old, H, 0), (mid, -8, 7), (mid, H, 0))):
        tile = ref[pl.ds(pl.multiple_of(start + shift, 8), 8), pl.ds(half, S * H)]
        line = tile[row : row + 1, :]
        xs[n : n + 1, :] = line
        xs[n + 4 : n + 5, :] = line
    index_x = ((lanes >> 4) & 3) * S + oz * H + (lanes & (H - 1))
    picked = [gather_lanes(xs[:, LANES * s : LANES * (s + 1)], index_x) for s in range(4)]
    low = jnp.where(lanes < 64, picked[0], picked[1])
    high = jnp.where(lanes < 64, picked[2], picked[3])
    faces = jnp.where(rows < 4, low, high)
    mean = 0.5 * (faces + pltpu.roll(faces, 2, 0))
    pack_ref[slot, 0:8, :] = jnp.where((rows & 2) == 0, faces, mean)
    index_y = oy * (LANES - S) + oz * H + (lanes & (H - 1))
    index_z = (lanes & 3) * S + H - oz
    y_group = pl.multiple_of(S * H - LANES * oy, LANES)
    for t in range(2):
        at = pl.multiple_of(start + 8 * t, 8)
        values = []
        for ref in (old, mid):
            y_face = gather_lanes(ref[pl.ds(at, 8), pl.ds(y_group, LANES)], index_y)
            parts = [
                gather_lanes(ref[pl.ds(at, 8), pl.ds(pl.multiple_of(half + LANES * s, LANES), LANES)], index_z)
                for s in range(4)
            ]
            which = (lanes >> 2) & 3
            z_face = jnp.where(
                which < 2,
                jnp.where(which == 0, parts[0], parts[1]),
                jnp.where(which == 2, parts[2], parts[3]),
            )
            values.append(jnp.where((lanes & S) == 0, z_face, y_face))
        face = jnp.where(lanes < 64, values[0], 0.5 * (values[0] + values[1]))
        used = ((lanes >> 4) & 1) == jnp.where((lanes & S) == 0, oz, oy)
        pack_ref[slot, 8 + 8 * t : 16 + 8 * t, :] = jnp.where(used, face, 0.0)


def find_boxes(parents, covers, boxes, octants):
    dev, devices = lax.axis_index("dev"), lax.axis_size("dev")
    group, groups = lax.axis_index("group"), lax.axis_size("group")
    for n in range(octants + 1):
        covers[n] = jnp.int32(-1)
    for r in range(3):
        source = lax.rem(dev + devices + r - 1, devices)
        for s in range(groups):
            first = (lax.rem(group + groups - s, groups) * devices + source) * boxes
            for k in range(boxes):
                local_id = parents[first + k] - dev * octants
                inside = jnp.logical_and(local_id >= 0, local_id < octants)
                covers[jnp.where(inside, local_id, octants)] = jnp.int32((r * groups + s) * boxes + k)


def step_tile(uc, pc, qc, ul, pll, ql, uh, ph, qh, lanes):
    sum_u = sum_yz(uc, lanes, False)
    sum_w = sum_yz([a * b for a, b in zip(pc, uc)], lanes, False)
    sum_q = sum_yz(qc, lanes, True)
    out = []
    for j in range(GROUPS):
        keep = (1.0 - 6.0 * pc[j]) - (sum_q[j] + (ql[j] + qh[j]))
        near_u = sum_u[j] + (ul[j] + uh[j])
        near_w = sum_w[j] + (pll[j] * ul[j] + ph[j] * uh[j])
        out.append(keep * uc[j] + (qc[j] * near_u + near_w))
    return out


def coarse_kernel(u_ref, k_ref, v_ref, near_sum, u, mid_out, p, q, split, sums):
    rows, wide = u_ref.shape
    base = MARGIN
    rate = 0.5 * RATE
    for ref in (u, p, q):
        for row in (base - 8, base + rows):
            ref[row : row + 8, :] = jnp.zeros((8, wide), jnp.float32)

    @pl.loop(0, rows // 16, unroll=True)
    def _(i):
        at = pl.multiple_of(i * 16, 16)
        to = pl.multiple_of(base + i * 16, 8)
        diff = rate * k_ref[pl.ds(at, 16), :].astype(jnp.float32)
        pot = rate * v_ref[pl.ds(at, 16), :].astype(jnp.float32)
        dens = u_ref[pl.ds(at, 16), :]
        u[pl.ds(to, 16), :] = dens
        p[pl.ds(to, 16), :] = diff + pot
        q[pl.ds(to, 16), :] = diff - pot
        store_split(split, rows, at, dens, (diff + pot) * dens)

    for window, part, out in windows():
        near = near_sum[part, :]
        sums[0:rows, out] = rate * (product(k_ref[:, window], near) - product(v_ref[:, window], near))
        sums[rows : 3 * rows, out] = product_of_split(split, near, window)

    ends = edge_count()

    @pl.loop(0, rows // 8, unroll=True)
    def _(i):
        at = pl.multiple_of(i * 8, 8)
        uv, pv, qv = (ref.at[pl.ds(pl.multiple_of(at + base - 8, 8), 24), :] for ref in (u, p, q))
        sum_q, sum_u, sum_w = (sums[pl.ds(pl.multiple_of(n * rows + at, 8), 8), :] for n in range(3))
        uc, pc, qc = (view[8:16, :] for view in (uv, pv, qv))
        ul, uh = uv[7:15, :], uv[9:17, :]
        keep = (1.0 - 6.0 * pc) - (sum_q + ends * qc + (qv[7:15, :] + qv[9:17, :]))
        near_u = sum_u + (ul + uh)
        near_w = sum_w + (pv[7:15, :] * ul + pv[9:17, :] * uh)
        mid_out[pl.ds(pl.multiple_of(at + base, 8), 8), :] = keep * uc + (qc * near_u + near_w)


def rims_kernel(parents, u_in, mid_in, k_ref, v_ref, near_edge, far_edge, u, m, to_near, to_own, to_far, e, xs, *, boxes):
    del u_in, mid_in
    base = MARGIN
    rows = u.shape[0] - 2 * base
    rate = 0.5 * RATE
    devices = lax.axis_size("dev")
    dev, near_dev, far_dev, odd = sides()
    group = lax.axis_index("group")
    octants = OCTANTS * (rows // S)
    lanes = lane_ids()
    before = jnp.where(odd == 1, near_edge[...], far_edge[...])
    after = jnp.where(odd == 1, far_edge[...], near_edge[...])
    u[base - 2 : base, :] = before[0:2, :]
    u[base + rows : base + rows + 2, :] = after[0:2, :]
    for n, (far, end, own, top) in enumerate(((before, 0, 0, base - 2), (after, rows - 16, 14, base + rows - 2))):
        e[0, 7:11, :] = u[top : top + 4, :]
        own_diff = rate * k_ref[end : end + 16, :].astype(jnp.float32)[own : own + 2, :]
        own_pot = rate * v_ref[end : end + 16, :].astype(jnp.float32)[own : own + 2, :]
        far_diff, far_pot = rate * far[2:4, :], rate * far[4:6, :]
        there, here = (7, 9) if n == 0 else (9, 7)
        e[1, there : there + 2, :] = far_diff + far_pot
        e[2, there : there + 2, :] = far_diff - far_pot
        e[1, here : here + 2, :] = own_diff + own_pot
        e[2, here : here + 2, :] = own_diff - own_pot
        tiles = [lane_groups(e.at[f], row) for row in (8, 7, 9) for f in range(3)]
        for j, new in enumerate(step_tile(*tiles, lanes)):
            m[top + 1 : top + 3, LANES * j : LANES * (j + 1)] = new[0:2, :]
    for ref, target in ((to_far, far_dev), (to_near, near_dev), (to_own, dev)):
        for k in range(boxes):
            local_id = parents[(group * devices + target) * boxes + k] - dev * octants
            local_id = jnp.minimum(jnp.maximum(local_id, 0), octants - 1)
            pack_rims(u, m, xs, ref, k, local_id, base)


def fine_rates(k_ref, v_ref, at):
    diff = RATE * k_ref[pl.ds(at, 16), :].astype(jnp.float32)
    pot = (0.5 * RATE) * v_ref[pl.ds(at, 16), :].astype(jnp.float32)
    return diff + pot, diff - pot


def store_split(split, rows, at, *values):
    pairs = [pieces_of(value) for value in values]
    for n, part in enumerate([high for high, _ in pairs] + [low for _, low in pairs]):
        split[pl.ds(pl.multiple_of(n * rows + at, 16), 16), :] = part


def product_of_split(split, matrix, window=slice(None)):
    half = split.shape[0] // 2
    both = product(split[:, window], matrix)
    return both[0:half] + both[half : 2 * half]


def fine_first_kernel(u_ref, k_ref, v_ref, near_sum, out_ref, keep_ref, u, w, p, q, split, sums, *, boxes):
    rows, wide = out_ref.shape
    base = 8
    @pl.loop(0, boxes, unroll=True)
    def _(k):
        for ref in (u, w):
            for ghost in (7, 40):
                ref[k, ghost : ghost + 1, :] = jnp.zeros((1, wide), jnp.float32)
        for i in range(2):
            at, to = pl.multiple_of(S * k + 16 * i, 16), base + 16 * i
            pc, qc = fine_rates(k_ref, v_ref, at)
            dens = u_ref[pl.ds(at, 16), :]
            p[k, to : to + 16, :] = pc
            q[k, to : to + 16, :] = qc
            u[k, to : to + 16, :] = dens
            w[k, to : to + 16, :] = pc * dens
            store_split(split, rows, at, dens, pc * dens)
        for ghost, cell in ((7, 8), (40, 39)):
            q[k, ghost : ghost + 1, :] = q[k, cell : cell + 1, :]

    for window, part, out in windows():
        near = near_sum[part, :]
        sums[0 : 2 * rows, out] = product_of_split(split, near, window)
        sums[2 * rows : 3 * rows, out] = RATE * product(k_ref[:, window], near) - (0.5 * RATE) * product(
            v_ref[:, window], near
        )
    ends = edge_count()

    @pl.loop(0, boxes, unroll=True)
    def _(k):
        for i in range(2):
            at, to = pl.multiple_of(S * k + 16 * i, 16), base + 16 * i
            here, low, high = (slice(to + m, to + m + 16) for m in (0, -1, 1))
            sum_u, sum_w, sum_q = (
                sums[pl.ds(pl.multiple_of(n * rows + at, 16), 16), :] + (ref[k, low, :] + ref[k, high, :])
                for n, ref in enumerate((u, w, q))
            )
            qc = q[k, here, :]
            stay = (1.0 - 6.0 * p[k, here, :]) - (sum_q + ends * qc)
            keep_ref[pl.ds(at, 16), :] = stay
            out_ref[pl.ds(at, 16), :] = stay * u[k, here, :] + (qc * sum_u + sum_w)


def fine_second_kernel(parents, first, keep, k_ref, v_ref, near_sum, ghost_sum, block_sum, from_near, from_own, from_far, out_any, avg_ref, u, w, p, q, lines, split, sums, ghosts, faces, dup, res, means, out_sems, *, boxes, octants):
    devices = lax.axis_size("dev")
    dev, near_dev, _, _ = sides()
    group = lax.axis_index("group")
    rows, wide = res.shape
    base = 8
    lanes = lane_ids()
    z = lanes & (S - 1)
    for k in range(boxes):
        parent = parents[(group * devices + dev) * boxes + k]
        own_id, near_id = parent - dev * octants, parent - near_dev * octants
        is_own = jnp.logical_and(own_id >= 0, own_id < octants)
        is_near = jnp.logical_and(near_id >= 0, near_id < octants)

        def chosen(n):
            there = slice(8 * n, 8 * n + 8)
            other = jnp.where(is_near, from_near[k, there, :], from_far[k, there, :])
            return jnp.where(is_own, from_own[k, there, :], other)

        for n in range(2):
            face = chosen(n + 1)
            dup[pl.ds(S * k + 16 * n, 8, 2), :] = face
            dup[pl.ds(S * k + 16 * n + 1, 8, 2), :] = face
        for n, part in enumerate(pieces_of(dup[S * k : S * k + S, :])):
            faces[n * rows + S * k : n * rows + S * k + S, :] = part
        x_faces = chosen(0)
        for n in range(4):
            spread = gather_lanes(x_faces, (2 * n + (lanes >> 6)) * H + (z >> 1))
            for half in range(2):
                j = 4 * half + n
                there = slice(LANES * j, LANES * (j + 1))
                lines[k, 0:2, there] = spread[4 * half : 4 * half + 2, :]
                u[k, 7:8, there] = spread[4 * half + 2 : 4 * half + 3, :]
                u[k, 40:41, there] = spread[4 * half + 3 : 4 * half + 4, :]
    for n in range(4):
        out = slice(256 * n, 256 * n + 256)
        for step in range(2):
            ghosts[step * rows : (step + 1) * rows, out] = product_of_split(faces, ghost_sum[step, :, out])
    row = lax.broadcasted_iota(jnp.int32, (16, wide), 0)

    @pl.loop(0, boxes, unroll=True)
    def _(k):
        for i in range(2):
            at, to = pl.multiple_of(S * k + 16 * i, 16), base + 16 * i
            pc, qc = fine_rates(k_ref, v_ref, at)
            beside = ghosts[pl.ds(at, 16), :] + jnp.where(row == 15 * i, lines[k, i : i + 1, :], 0.0)
            new = first[pl.ds(at, 16), :] + (pc + qc) * beside
            p[k, to : to + 16, :] = pc
            q[k, to : to + 16, :] = qc
            u[k, to : to + 16, :] = new
            w[k, to : to + 16, :] = pc * new
            store_split(split, rows, at, new, pc * new)
        for ghost, cell in ((7, 8), (40, 39)):
            w[k, ghost : ghost + 1, :] = p[k, cell : cell + 1, :] * u[k, ghost : ghost + 1, :]

    for window, part, out in windows():
        sums[:, out] = product_of_split(split, near_sum[part, :], window)

    def out_copy(k):
        there = pl.ds(pl.multiple_of(S * k, S), S)
        return pltpu.make_async_copy(res.at[there, :], out_any.at[there, :], out_sems.at[k])

    @pl.loop(0, boxes, unroll=True)
    def _(k):
        for i in range(2):
            at, to = pl.multiple_of(S * k + 16 * i, 16), base + 16 * i
            here, low, high = (slice(to + m, to + m + 16) for m in (0, -1, 1))
            sum_u, sum_w = (
                sums[pl.ds(pl.multiple_of(n * rows + at, 16), 16), :] + (ref[k, low, :] + ref[k, high, :])
                for n, ref in enumerate((u, w))
            )
            pc, qc = p[k, here, :], q[k, here, :]
            beside = ghosts[pl.ds(pl.multiple_of(rows + at, 16), 16), :]
            new = (keep[pl.ds(at, 16), :] * u[k, here, :] + (qc * sum_u + sum_w)) + (pc + qc) * beside
            res[pl.ds(at, 16), :] = new
            store_split(split, rows, at, new)
        out_copy(k).start()

    total = product_of_split(split.at[0 : 2 * rows, :], block_sum[...])
    for half in range(2):
        means[half, :, :] = total[:, LANES * half : LANES * (half + 1)]
    for half in range(2):
        for k in range(boxes):
            for t in range(2):
                at = S * k + 16 * t
                pair = means[half, pl.ds(at, 8, 2), :] + means[half, pl.ds(at + 1, 8, 2), :]
                avg_ref[k, 8 * t : 8 * t + 8, LANES * half : LANES * (half + 1)] = 0.125 * pair
    for k in range(boxes):
        out_copy(k).wait()


def join_kernel(*refs):
    *pieces, out_ref = refs
    count = pieces[0].shape[0]
    for n, piece in enumerate(pieces):
        out_ref[n * count : (n + 1) * count] = piece[...]


LIST = 64
COUNTS = 50
OCTANT_BITS = 7


def list_octants(covers, chip_list, far_list, count, octants):
    _, _, _, odd = sides()
    n_chip = n_far = jnp.int32(0)
    for octant in range(octants):
        if octant % OCTANTS == 0:
            far_list[COUNTS + octant // OCTANTS] = n_far
        place = covers[octant]
        is_next = (place >= 2 * count).astype(jnp.int32)
        is_own = jnp.logical_and(place >= count, is_next == 0).astype(jnp.int32)
        is_far = jnp.logical_and(jnp.logical_and(place >= 0, is_own == 0), is_next == odd).astype(jnp.int32)
        is_chip = jnp.logical_and(place >= 0, is_far == 0).astype(jnp.int32)
        slot = place - count * is_own - 2 * count * is_next
        chip_list[n_chip] = ((slot * 2 + is_own) << OCTANT_BITS) + octant
        far_list[n_far] = (slot << OCTANT_BITS) + octant
        n_chip, n_far = n_chip + is_chip, n_far + is_far
    far_list[COUNTS + octants // OCTANTS] = n_far
    return n_chip


def put_average(tile_of, octant, held):
    lanes = lane_ids()
    start, oy, oz = octant_place(octant)
    here = ((lanes >> 4) & 1) == oz
    for t in range(2):
        at = pl.ds(pl.multiple_of(MARGIN + start + 8 * t, 8), 8)
        for s in range(4):
            lane = pl.ds(pl.multiple_of(oy * (S * H) + LANES * s, LANES), LANES)
            half = s // 2
            tile = tile_of(slice(8 * t, 8 * t + 8), slice(LANES * half, LANES * (half + 1)))
            moved = gather_lanes(tile, (s % 2) * 64 + (lanes >> 5) * H + (lanes & (H - 1)))
            held[at, lane] = jnp.where(here, moved, held[at, lane])


def merge_chip_kernel(parents, mid, own, near, held, far_list, covers, chip_list, *, boxes, octants):
    del mid
    find_boxes(parents, covers, boxes, octants)
    count = list_octants(covers, chip_list, far_list, own.shape[0], octants)

    @pl.loop(0, count)
    def _(n):
        entry = chip_list[n]
        is_own = ((entry >> OCTANT_BITS) & 1) == 1
        slot = entry >> (OCTANT_BITS + 1)
        put_average(
            lambda rows, lanes: jnp.where(is_own, own[slot, rows, lanes], near[slot, rows, lanes]),
            entry & ((1 << OCTANT_BITS) - 1),
            held,
        )


def merge_far_kernel(far_list, held_in, far, held, out_any, out_sems):
    del held_in
    stores = []
    for box in range(out_any.shape[0] // S):

        @pl.loop(far_list[COUNTS + box], far_list[COUNTS + box + 1])
        def _(n):
            entry = far_list[n]
            slot = entry >> OCTANT_BITS
            put_average(lambda rows, lanes: far[slot, rows, lanes], entry & ((1 << OCTANT_BITS) - 1), held)

        there = held.at[MARGIN + box * S : MARGIN + (box + 1) * S, :]
        stores.append(pltpu.make_async_copy(there, out_any.at[box * S : (box + 1) * S, :], out_sems.at[box]))
        stores[-1].start()
    for copy in stores:
        copy.wait()


def params():
    return pltpu.CompilerParams(vmem_limit_bytes=VMEM_LIMIT)


def cost(flops, size):
    return pl.CostEstimate(flops=flops, bytes_accessed=size, transcendentals=0)


def f32(*shape):
    return jax.ShapeDtypeStruct(shape, jnp.float32)


def vmem(*shape):
    return pltpu.VMEM(shape, jnp.float32)


def bf16(*shape):
    return pltpu.VMEM(shape, jnp.bfloat16)


def whole():
    return pl.BlockSpec(memory_space=pltpu.VMEM)


def on_device(coarse_dens, coarse_diff, coarse_pot, fine_dens, fine_diff, fine_pot, parents):
    devices = lax.axis_size("dev")
    groups = lax.axis_size("group")
    rows = coarse_dens.shape[0]
    boxes = fine_dens.shape[0] // S
    fine_rows = boxes * S
    octants = OCTANTS * (rows // S)
    wide = S * S
    smem = pl.BlockSpec(memory_space=pltpu.SMEM)
    anywhere = pl.BlockSpec(memory_space=pl.ANY)
    dma = pltpu.SemaphoreType.DMA
    near_pairs = [(i, i ^ 1) for i in range(devices)]
    far_pairs = [(i, (i + devices - 1 + 2 * (i & 1)) % devices) for i in range(devices)]

    def swap(near, far):
        got_far = lax.ppermute(far, "dev", far_pairs)
        return lax.ppermute(near, "dev", near_pairs), got_far

    near_edge, far_edge = pl.pallas_call(
        edges_kernel,
        grid=(1,),
        in_specs=[
            pl.BlockSpec((8, wide), lambda i: (0, 0)),
            pl.BlockSpec((16, wide), lambda i: (0, 0)),
            pl.BlockSpec((16, wide), lambda i: (0, 0)),
            pl.BlockSpec((8, wide), lambda i: (rows // 8 - 1, 0)),
            pl.BlockSpec((16, wide), lambda i: (rows // 16 - 1, 0)),
            pl.BlockSpec((16, wide), lambda i: (rows // 16 - 1, 0)),
        ],
        out_specs=[pl.BlockSpec((8, wide), lambda i: (0, 0))] * 2,
        out_shape=[f32(8, wide)] * 2,
        name="edges",
    )(coarse_dens, coarse_diff, coarse_pot, coarse_dens, coarse_diff, coarse_pot)
    near_edge, far_edge = swap(near_edge, far_edge)

    near_sum = neighbour_matrix()
    ext = f32(rows + 2 * MARGIN, wide)
    held_dens, mid = pl.pallas_call(
        coarse_kernel,
        in_specs=[whole()] * 4,
        out_specs=[whole()] * 2,
        scratch_shapes=[vmem(rows + 2 * MARGIN, wide)] * 2 + [bf16(4 * rows, wide), vmem(3 * rows, wide)],
        out_shape=[ext, ext],
        compiler_params=params(),
        cost_estimate=cost(rows * wide * 40, rows * wide * 12),
        name="coarse",
    )(coarse_dens, coarse_diff, coarse_pot, near_sum)

    packs = f32(boxes, PACK, LANES)
    _, mid, to_near, own, to_far = pl.pallas_call(
        functools.partial(rims_kernel, boxes=boxes),
        grid_spec=pltpu.PrefetchScalarGridSpec(
            num_scalar_prefetch=1,
            grid=(),
            in_specs=[whole()] * 6,
            out_specs=[whole()] * 5,
            scratch_shapes=[vmem(3, 24, wide), vmem(8, S * H)],
        ),
        out_shape=[ext, ext, packs, packs, packs],
        input_output_aliases={1: 0, 2: 1},
        compiler_params=params(),
        cost_estimate=cost(rows * wide * 8, rows * wide * 8),
        name="rims",
    )(parents, held_dens, mid, coarse_diff, coarse_pot, near_edge, far_edge)
    from_near, from_far = swap(to_near, to_far)

    fine_first, keep = pl.pallas_call(
        functools.partial(fine_first_kernel, boxes=boxes),
        in_specs=[whole()] * 4,
        out_specs=[whole()] * 2,
        scratch_shapes=[vmem(boxes, 48, wide)] * 4 + [bf16(4 * fine_rows, wide), vmem(3 * fine_rows, wide)],
        out_shape=[f32(fine_rows, wide)] * 2,
        compiler_params=params(),
        cost_estimate=cost(fine_rows * wide * 40, fine_rows * wide * 16),
        name="fine_first",
    )(fine_dens, fine_diff, fine_pot, near_sum)

    fine_out, averages = pl.pallas_call(
        functools.partial(fine_second_kernel, boxes=boxes, octants=octants),
        grid_spec=pltpu.PrefetchScalarGridSpec(
            num_scalar_prefetch=1,
            grid=(),
            in_specs=[whole()] * 10,
            out_specs=[anywhere, whole()],
            scratch_shapes=[vmem(boxes, 48, wide)] * 4
            + [
                vmem(boxes, 8, wide),
                bf16(4 * fine_rows, wide),
                vmem(2 * fine_rows, wide),
                vmem(2 * fine_rows, wide),
                bf16(2 * fine_rows, LANES),
                vmem(fine_rows, LANES),
                vmem(fine_rows, wide),
                vmem(2, fine_rows, LANES),
                dma((boxes,)),
            ],
        ),
        out_shape=[f32(fine_rows, wide), f32(boxes, H, H * H)],
        compiler_params=params(),
        cost_estimate=cost(fine_rows * wide * 60, fine_rows * wide * 16),
        name="fine_second",
    )(
        parents,
        fine_first,
        keep,
        fine_diff,
        fine_pot,
        near_sum,
        ghost_matrices(),
        average_matrix(),
        from_near,
        own,
        from_far,
    )

    pieces = [averages]
    for s in range(1, groups):
        pieces.append(lax.ppermute(averages, "group", [(i, (i + s) % groups) for i in range(groups)]))
    joined = pl.pallas_call(
        join_kernel,
        in_specs=[whole()] * groups,
        out_specs=whole(),
        out_shape=f32(groups * boxes, H, H * H),
        compiler_params=params(),
        name="join",
    )(*pieces)
    near_avg, far_avg = swap(joined, joined)

    def merge(kernel, count, out_specs, out_shape, scratch, name):
        return pl.pallas_call(
            kernel,
            grid_spec=pltpu.PrefetchScalarGridSpec(
                num_scalar_prefetch=1,
                grid=(),
                in_specs=[whole()] * (1 + count),
                out_specs=[whole()] + out_specs,
                scratch_shapes=scratch,
            ),
            out_shape=[ext] + out_shape,
            input_output_aliases={1: 0},
            compiler_params=params(),
            cost_estimate=cost(rows * wide * 4, rows * wide * 12),
            name=name,
        )

    far_list = jax.ShapeDtypeStruct((LIST,), jnp.int32)
    chip_kernel = functools.partial(merge_chip_kernel, boxes=boxes, octants=octants)
    lists = [pltpu.SMEM((octants + 1,), jnp.int32), pltpu.SMEM((LIST,), jnp.int32)]
    held, far_list = merge(chip_kernel, 2, [smem], [far_list], lists, "merge_chip")(parents, mid, joined, near_avg)
    _, coarse_out = merge(merge_far_kernel, 1, [anywhere], [f32(rows, wide)], [dma((rows // S,))], "merge_far")(
        far_list, held, far_avg
    )
    return coarse_out, fine_out


def solution(mesh):
    in_specs = (
        P("dev", None),
        P("dev", None),
        P("dev", None),
        P(("group", "dev"), None),
        P(("group", "dev"), None),
        P(("group", "dev"), None),
        P(),
    )
    out_specs = (P("dev", None), P(("group", "dev"), None))
    return jax.shard_map(on_device, mesh=mesh, in_specs=in_specs, out_specs=out_specs, check_vma=False)
```
